32 devices in a mesh: occ: 4 (over z), vir: 8 (over y, x, core).
Axes of the slice: x: 2, y: 2, z: 4, core: 2. Of those that a mesh axis runs over, the one named last changes fastest.
Arguments:
- amplitudes: float32 [4096, 3072], P(('occ', 'vir')), may hold values from -6 to 6
- amp_mask: int32 [128, 24], P(('occ', 'vir')), may hold values 0 or 1
- integrals: float32 [3072, 3072], P('vir', 'occ'), may hold values from -0.1875 to 0.1875
- int_mask: int32 [24, 24], P('vir', 'occ'), may hold values from 0 to 1, as said below
Outputs:
- residual: float32 [4096, 3072], P(('occ', 'vir'))
The draws below stay inside these ranges and needn't reach their ends.
Inputs may be any that keep to these rules, and one draw needn't show every extreme that they name: `int_mask`: 0/1 entries. `amp_mask`: 0/1 entries.
All inputs are finite; a program needn't handle non-finite values. No bound on the sum of `amp_mask` on one device may be relied on, other than what follows from the above.
Results may differ from the reference program's by a relative error of at most 0.000071.
Values sent between devices are 32-bit elements; how exact they have to be, the bound alone decides.
No kernel may reach another device: no remote copies, remote signals or barrier semaphores. Data moves between devices by JAX's collectives and lax.ppermute only.
A program may use at most 192 MiB of HBM per device.

```python
import jax
import jax.numpy as jnp
from jax import lax

TILE_O = 32
TILE_V = 128
NO_T = 128
ROWS = 4096
NQ = 24
COLS = 3072


def draw_int_mask(key, part):
    key = jax.random.fold_in(key, 7)
    first_key, second_key = jax.random.split(key)
    density = jax.random.randint(first_key, (NQ, 1), 2, 10)
    values = jax.random.randint(second_key, (NQ, NQ), 0, 10)
    return (values < density).astype(jnp.int32)


def plant(values, stream_key, smallest, top_value):
    spot = [jax.random.randint(jax.random.fold_in(stream_key, axis), (), 0, length) for axis, length in enumerate(values.shape)]
    longest = values.shape.index(max(values.shape))
    next_to = spot[:longest] + [(spot[longest] + 1) % values.shape[longest]] + spot[longest + 1:]
    return values.at[tuple(spot)].set(smallest).at[tuple(next_to)].set(top_value)


def shard_levels(key, extent, cuts, low, largest):
    gain, own = 1.0, jax.random.fold_in(key, 6)
    for position, shards_of in cuts:
        steps = jnp.exp(jax.random.uniform(jax.random.fold_in(own, position), (shards_of,), jnp.float32, low / len(cuts), largest / len(cuts)))
        gain = gain * jnp.repeat(steps, extent[position] // shards_of).reshape([-1 if axis == position else 1 for axis in range(len(extent))])
    return gain


def bell_draw(own_key, shape, width, bound, pieces=(), dtype=jnp.bfloat16):
    array = jax.random.normal(own_key, shape, jnp.float32) * width
    if len(pieces) > 0:
        array = shard_levels(own_key, shape, pieces, -0.22, 0.18) * array
    return jnp.clip(array, min=-bound, max=bound).astype(dtype)


def setup_inputs(seed: int = 0) -> dict:
    arg_keys = jax.random.split(jax.random.key(seed), 5)
    return {
        "amplitudes": bell_draw(arg_keys[0], (ROWS, COLS), 1.0, 6.0, ((0, 32),), jnp.float32),
        "amp_mask": plant((jax.random.randint(arg_keys[1], (NO_T, NQ), 0, 5) < 3).astype(jnp.int32), jax.random.fold_in(arg_keys[1], 1), 0, 1),
        "integrals": bell_draw(arg_keys[2], (COLS, COLS), (COLS // 3) ** -0.5, 0.1875, ((0, 8), (1, 4)), jnp.float32),
        "int_mask": draw_int_mask(jax.random.fold_in(arg_keys[4], 71), 0),
    }


def reference(amplitudes, amp_mask, integrals, int_mask):
    tile_count = amp_mask.shape[0]
    pair_tiles = amp_mask.shape[1]
    amp_scale = amp_mask.astype(jnp.float32)[:, None, :, None]
    kept = (amplitudes.reshape(tile_count, TILE_O, pair_tiles, TILE_V) * amp_scale).reshape(amplitudes.shape)
    int_scale = int_mask.astype(jnp.float32)[:, None, :, None]
    weighted = (integrals.reshape(pair_tiles, TILE_V, pair_tiles, TILE_V) * int_scale).reshape(integrals.shape)
    return jnp.dot(kept, weighted, precision=lax.Precision.HIGHEST, preferred_element_type=jnp.float32)
```

```python
import jax
import jax.numpy as jnp
from jax import lax
from jax.sharding import PartitionSpec as P

TILE_O = 32
TILE_V = 128
HIGH = lax.Precision.HIGH


def masked(values, mask, tile_rows):
    tile_r, tile_c = mask.shape
    scale = mask.astype(jnp.float32)[:, None, :, None]
    return (values.reshape(tile_r, tile_rows, tile_c, TILE_V) * scale).reshape(values.shape)


def line_blocks(own, nodes):
    here = lax.axis_index("occ")
    blocks = [own]
    origins = [list(range(nodes))]
    size = 1
    while size < nodes:
        fresh, fresh_origins = [], []
        place = here % (2 * size)
        dist = jnp.where(place < size, size - 1 - place, place - size)
        middles = [g * 2 * size + size for g in range(nodes // (2 * size))]
        for block, origin in zip(blocks, origins):
            pairs = [(m - 1, m) for m in middles] + [(m, m - 1) for m in middles]
            moving = lax.ppermute(block, "occ", pairs)
            got = moving
            for hop in range(1, size):
                pairs = [(m - hop, m - hop - 1) for m in middles] + [(m + hop - 1, m + hop) for m in middles]
                moving = lax.ppermute(moving, "occ", pairs)
                got = jnp.where(dist == hop, moving, got)
            fresh.append(got)
            table = [0] * nodes
            for m in middles:
                for k in range(size):
                    table[m - 1 - k] = origin[m]
                    table[m + k] = origin[m - 1]
            fresh_origins.append(table)
        blocks += fresh
        origins += fresh_origins
        size *= 2
    return blocks, origins


def per_device(sizes, amplitudes, amp_mask, integrals, int_mask):
    n_occ, n_vir = sizes
    rows = amplitudes.shape[0]
    half = rows // 2
    groups = n_vir // 2
    width = integrals.shape[1]
    depth = 2 * integrals.shape[0]

    def swap(x, bits):
        return lax.ppermute(x, "vir", [(i, i ^ bits) for i in range(n_vir)])

    me = lax.axis_index("vir")
    kept = masked(amplitudes, amp_mask, TILE_O)
    weighted = masked(integrals, int_mask, TILE_V)
    blocks, origins = line_blocks(weighted, n_occ)

    rel = []
    for r in range(groups):
        start = ((me // 2) ^ r) * depth
        part = lax.dynamic_slice_in_dim(kept, start, depth, axis=1)
        rel.append(part if r == 0 else swap(part, 2 * r))

    bits = []
    while (1 << len(bits)) < groups:
        bits.append(1 << len(bits))
    orders = [bits, bits[::-1]]
    cut = [slice(0, half), slice(half, rows)]
    away = [[r for r in range(groups) if r & o[0]] for o in orders]
    near = [[r for r in range(groups) if not r & o[0]] for o in orders]
    lhs_away = jnp.concatenate([rel[r][cut[h]] for h in range(2) for r in away[h]], axis=0)
    lhs_near = jnp.concatenate([rel[r][cut[h]] for h in range(2) for r in near[h]], axis=0)

    low = me % 2
    out = jnp.zeros((rows, n_occ * width), jnp.float32)
    for block, origin in zip(blocks, origins):
        other = swap(block, 1)
        first = jnp.where(low == 0, block, other)
        second = jnp.where(low == 0, other, block)
        rhs = jnp.concatenate([first, second], axis=0)
        sent = jnp.dot(lhs_away, rhs, precision=HIGH, preferred_element_type=jnp.float32)
        stay = jnp.dot(lhs_near, rhs, precision=HIGH, preferred_element_type=jnp.float32)
        count = groups // 2
        done = []
        for h in range(2):
            s = sent[h * count * half : (h + 1) * count * half]
            k = stay[h * count * half : (h + 1) * count * half]
            k = k + swap(s, 2 * orders[h][0])
            held = {r: k[i * half : (i + 1) * half] for i, r in enumerate(near[h])}
            for bit in orders[h][1:]:
                going = [r for r in held if r & bit]
                s = jnp.concatenate([held[r] for r in going], axis=0)
                got = swap(s, 2 * bit)
                for i, r in enumerate(going):
                    held[r ^ bit] = held[r ^ bit] + got[i * half : (i + 1) * half]
                    del held[r]
            done.append(held[0])
        col = jnp.array(origin, jnp.int32)[lax.axis_index("occ")] * width
        out = lax.dynamic_update_slice(out, jnp.concatenate(done, axis=0), (0, col))
    return out


def solution(mesh):
    sizes = (mesh.shape["occ"], mesh.shape["vir"])

    def run(*args):
        return per_device(sizes, *args)

    in_specs = (P(("occ", "vir"), None), P(("occ", "vir"), None), P("vir", "occ"), P("vir", "occ"))
    out_specs = P(("occ", "vir"), None)
    return jax.shard_map(run, mesh=mesh, in_specs=in_specs, out_specs=out_specs, check_vma=False)
```

```python
import jax
import jax.numpy as jnp
from jax import lax
from jax.sharding import PartitionSpec as P

TILE_O = 32
TILE_V = 128
HIGH = lax.Precision.HIGH


def masked(values, mask, tile_rows):
    tile_r, tile_c = mask.shape
    scale = mask.astype(jnp.float32)[:, None, :, None]
    return (values.reshape(tile_r, tile_rows, tile_c, TILE_V) * scale).reshape(values.shape)


def after(value, *earlier):
    return lax.optimization_barrier((value,) + earlier)[0]


def line_blocks(own, nodes, split_last):
    here = lax.axis_index("occ")
    blocks = [own]
    origins = [list(range(nodes))]
    size = 1
    while size < nodes:
        fresh, fresh_origins = [], []
        place = here % (2 * size)
        dist = jnp.where(place < size, size - 1 - place, place - size)
        middles = [g * 2 * size + size for g in range(nodes // (2 * size))]
        for n, (block, origin) in enumerate(zip(blocks, origins)):
            pairs = [(m - 1, m) for m in middles] + [(m, m - 1) for m in middles]
            got = lax.ppermute(block, "occ", pairs)
            parts = [got]
            if split_last and size * 2 == nodes and n == size - 1:
                mid = got.shape[1] // 2
                parts = [got[:, :mid], got[:, mid:]]
            whole = []
            for moving in parts:
                got = moving
                for hop in range(1, size):
                    pairs = [(m - hop, m - hop - 1) for m in middles] + [(m + hop - 1, m + hop) for m in middles]
                    moving = lax.ppermute(moving, "occ", pairs)
                    got = jnp.where(dist == hop, moving, got)
                whole.append(got)
            fresh.append(whole if len(whole) > 1 else whole[0])
            table = [0] * nodes
            for m in middles:
                for k in range(size):
                    table[m - 1 - k] = origin[m]
                    table[m + k] = origin[m - 1]
            fresh_origins.append(table)
        blocks += fresh
        origins += fresh_origins
        size *= 2
    return blocks, origins


def per_device(sizes, amplitudes, amp_mask, integrals, int_mask):
    n_occ, n_vir = sizes
    rows = amplitudes.shape[0]
    half = rows // 2
    groups = n_vir // 2
    width = integrals.shape[1]
    own_depth = integrals.shape[0]

    def swap(x, bits):
        return lax.ppermute(x, "vir", [(i, i ^ bits) for i in range(n_vir)])

    me = lax.axis_index("vir")
    low = me % 2
    blocks, origins = line_blocks(integrals, n_occ, True)

    mask_own = lax.all_gather(int_mask, "occ", axis=0)
    mask_pair = jnp.concatenate([mask_own, swap(mask_own, 1)], axis=1)

    kept = masked(amplitudes, amp_mask, TILE_O)
    rel = []
    for r in range(groups):
        start = ((me // 2) ^ r) * (2 * own_depth)
        mine = lax.dynamic_slice_in_dim(kept, start + low * own_depth, own_depth, axis=1)
        others = lax.dynamic_slice_in_dim(kept, start + (1 - low) * own_depth, own_depth, axis=1)
        part = jnp.concatenate([mine, others], axis=1)
        rel.append(part if r == 0 else swap(part, 2 * r))

    bits = []
    while (1 << len(bits)) < groups:
        bits.append(1 << len(bits))
    orders = [bits, bits[::-1]]
    cut = [slice(0, half), slice(half, rows)]
    away = [[r for r in range(groups) if r & o[0]] for o in orders]
    near = [[r for r in range(groups) if not r & o[0]] for o in orders]
    lhs_away = jnp.concatenate([rel[r][cut[h]] for h in range(2) for r in away[h]], axis=0)
    lhs_near = jnp.concatenate([rel[r][cut[h]] for h in range(2) for r in near[h]], axis=0)

    pieces = []
    for block, origin in zip(blocks, origins):
        place = jnp.array(origin, jnp.int32)[lax.axis_index("occ")]
        mask = lax.dynamic_index_in_dim(mask_pair, place, 0, keepdims=False)
        parts = block if isinstance(block, list) else [block]
        offset = 0
        for part in parts:
            tiles = part.shape[1] // TILE_V
            pieces.append((part, mask[:, offset // TILE_V : offset // TILE_V + tiles], place * width + offset))
            offset += part.shape[1]

    out = jnp.zeros((rows, n_occ * width), jnp.float32)
    previous = None
    for block, mask, col in pieces:
        if previous is not None:
            block = after(block, previous)
        other = swap(block, 1)
        rhs = masked(jnp.concatenate([block, other], axis=0), mask, TILE_V)
        sent = jnp.dot(lhs_away, rhs, precision=HIGH, preferred_element_type=jnp.float32)
        stay = jnp.dot(lhs_near, rhs, precision=HIGH, preferred_element_type=jnp.float32)
        previous = sent
        count = groups // 2
        done = []
        for h in range(2):
            s = sent[h * count * half : (h + 1) * count * half]
            k = stay[h * count * half : (h + 1) * count * half]
            k = k + swap(s, 2 * orders[h][0])
            held = {r: k[i * half : (i + 1) * half] for i, r in enumerate(near[h])}
            for bit in orders[h][1:]:
                going = [r for r in held if r & bit]
                s = jnp.concatenate([held[r] for r in going], axis=0)
                got = swap(s, 2 * bit)
                for i, r in enumerate(going):
                    held[r ^ bit] = held[r ^ bit] + got[i * half : (i + 1) * half]
                    del held[r]
            done.append(held[0])
        out = lax.dynamic_update_slice(out, jnp.concatenate(done, axis=0), (0, col))
    return out


def solution(mesh):
    sizes = (mesh.shape["occ"], mesh.shape["vir"])

    def run(*args):
        return per_device(sizes, *args)

    in_specs = (P(("occ", "vir"), None), P(("occ", "vir"), None), P("vir", "occ"), P("vir", "occ"))
    out_specs = P(("occ", "vir"), None)
    return jax.shard_map(run, mesh=mesh, in_specs=in_specs, out_specs=out_specs, check_vma=False)
```

```python
import jax
import jax.numpy as jnp
from jax import lax
from jax.sharding import PartitionSpec as P

TILE_O = 32
TILE_V = 128
HIGH = lax.Precision.HIGH


def masked(values, mask, tile_rows):
    tile_r, tile_c = mask.shape
    scale = mask.astype(jnp.float32)[:, None, :, None]
    return (values.reshape(tile_r, tile_rows, tile_c, TILE_V) * scale).reshape(values.shape)


def after(value, *earlier):
    return lax.optimization_barrier((value,) + earlier)[0]


def line_blocks(own, own_later, nodes, split_last):
    here = lax.axis_index("occ")
    blocks = [own]
    origins = [list(range(nodes))]
    size = 1
    while size < nodes:
        fresh, fresh_origins = [], []
        place = here % (2 * size)
        dist = jnp.where(place < size, size - 1 - place, place - size)
        middles = [g * 2 * size + size for g in range(nodes // (2 * size))]
        for n, (block, origin) in enumerate(zip(blocks, origins)):
            pairs = [(m - 1, m) for m in middles] + [(m, m - 1) for m in middles]
            got = lax.ppermute(own_later if size > 1 and n == 0 else block, "occ", pairs)
            parts = [got]
            if split_last and size * 2 == nodes and n == size - 1:
                mid = got.shape[1] // 2
                parts = [got[:, :mid], got[:, mid:]]
            whole = []
            for moving in parts:
                got = moving
                for hop in range(1, size):
                    pairs = [(m - hop, m - hop - 1) for m in middles] + [(m + hop - 1, m + hop) for m in middles]
                    moving = lax.ppermute(moving, "occ", pairs)
                    got = jnp.where(dist == hop, moving, got)
                whole.append(got)
            fresh.append(whole if len(whole) > 1 else whole[0])
            table = [0] * nodes
            for m in middles:
                for k in range(size):
                    table[m - 1 - k] = origin[m]
                    table[m + k] = origin[m - 1]
            fresh_origins.append(table)
        blocks += fresh
        origins += fresh_origins
        size *= 2
    return blocks, origins


def per_device(sizes, amplitudes, amp_mask, integrals, int_mask):
    n_occ, n_vir = sizes
    rows = amplitudes.shape[0]
    half = rows // 2
    groups = n_vir // 2
    width = integrals.shape[1]
    own_depth = integrals.shape[0]

    def swap(x, bits):
        return lax.ppermute(x, "vir", [(i, i ^ bits) for i in range(n_vir)])

    me = lax.axis_index("vir")
    low = me % 2
    weighted = masked(integrals, int_mask, TILE_V)
    kept = masked(amplitudes, after(amp_mask, weighted), TILE_O)

    parts = []
    for r in range(groups):
        start = ((me // 2) ^ r) * (2 * own_depth)
        mine = lax.dynamic_slice_in_dim(kept, start + low * own_depth, own_depth, axis=1)
        others = lax.dynamic_slice_in_dim(kept, start + (1 - low) * own_depth, own_depth, axis=1)
        parts.append(jnp.concatenate([mine, others], axis=1))
    rel = [parts[0]] + [None] * (groups - 1)
    for r in range(groups - 1, 0, -1):
        rel[r] = swap(parts[r], 2 * r)

    blocks, origins = line_blocks(weighted, after(weighted, *parts), n_occ, True)

    bits = []
    while (1 << len(bits)) < groups:
        bits.append(1 << len(bits))
    orders = [bits, bits[::-1]]
    cut = [slice(0, half), slice(half, rows)]
    away = [[r for r in range(groups) if r & o[0]] for o in orders]
    near = [[r for r in range(groups) if not r & o[0]] for o in orders]
    lhs_away = [jnp.concatenate([rel[r][cut[h]] for r in away[h]], axis=0) for h in range(2)]
    lhs_near = [jnp.concatenate([rel[r][cut[h]] for r in near[h]], axis=0) for h in range(2)]
    away_own = jnp.concatenate([x[:, :own_depth] for x in lhs_away], axis=0)
    near_own = jnp.concatenate([x[:, :own_depth] for x in lhs_near], axis=0)
    away_other = [x[:, own_depth:] for x in lhs_away]
    near_other = jnp.concatenate([x[:, own_depth:] for x in lhs_near], axis=0)
    count = groups // 2 * half

    pieces = []
    for n, (block, origin) in enumerate(zip(blocks, origins)):
        place = jnp.array(origin, jnp.int32)[lax.axis_index("occ")]
        offset = 0
        for part in block if isinstance(block, list) else [block]:
            pieces.append((after(part, *parts) if n == 0 else part, place * width + offset))
            offset += part.shape[1]

    out = jnp.zeros((rows, n_occ * width), jnp.float32)
    token = None
    waiting = None
    for block, col in pieces:
        other = swap(block, 1)
        if token is not None:
            block = after(block, *token)
        sent_own = dot(away_own, block)
        stay_own = dot(near_own, block)
        other = after(other, sent_own)
        sent = [dot(away_other[h], other) + sent_own[h * count : (h + 1) * count] for h in range(2)]
        first = [swap(sent[h], 2 * orders[h][0]) for h in range(2)]
        stay = dot(near_other, other) + stay_own
        if waiting is not None:
            out = finish(out, waiting, stay)
        held = []
        for h in range(2):
            held.append({
                r: stay[h * count + i * half : h * count + (i + 1) * half] + first[h][i * half : (i + 1) * half]
                for i, r in enumerate(near[h])
            })
        for level in range(1, len(bits)):
            going = [[r for r in held[h] if r & orders[h][level]] for h in range(2)]
            moved = [jnp.concatenate([held[h][r] for r in going[h]], axis=0) for h in range(2)]
            got = [swap(moved[h], 2 * orders[h][level]) for h in range(2)]
            if level == len(bits) - 1:
                token = moved
                waiting = ([held[h][0] for h in range(2)], got, col)
                break
            for h in range(2):
                for i, r in enumerate(going[h]):
                    held[h][r ^ orders[h][level]] += got[h][i * half : (i + 1) * half]
                    del held[h][r]
    return finish(out, waiting, None)


def dot(a, b):
    return jnp.dot(a, b, precision=HIGH, preferred_element_type=jnp.float32)


def finish(out, waiting, dep):
    held, got, col = waiting
    if dep is not None:
        got = lax.optimization_barrier((*got, dep))[:2]
    done = jnp.concatenate([held[h] + got[h] for h in range(2)], axis=0)
    return lax.dynamic_update_slice(out, done, (0, col))


def solution(mesh):
    sizes = (mesh.shape["occ"], mesh.shape["vir"])

    def run(*args):
        return per_device(sizes, *args)

    in_specs = (P(("occ", "vir"), None), P(("occ", "vir"), None), P("vir", "occ"), P("vir", "occ"))
    out_specs = P(("occ", "vir"), None)
    return jax.shard_map(run, mesh=mesh, in_specs=in_specs, out_specs=out_specs, check_vma=False)
```

```python
import functools

import jax
import jax.numpy as jnp
from jax import lax
from jax.experimental import pallas as pl
from jax.experimental.pallas import tpu as pltpu
from jax.sharding import PartitionSpec as P

TILE_O = 32
TILE_V = 128
VMEM_LIMIT = 40 * 1024 * 1024


def masked(values, mask, tile_rows):
    tile_r, tile_c = mask.shape
    scale = mask.astype(jnp.float32)[:, None, :, None]
    return (values.reshape(tile_r, tile_rows, tile_c, TILE_V) * scale).reshape(values.shape)


def after(value, *earlier):
    return lax.optimization_barrier((value,) + earlier)[0]


def in_vmem(count):
    return [pl.BlockSpec(memory_space=pltpu.VMEM)] * count


def cut_kernel(groups, own_tiles, place_ref, mask_ref, amp_ref, *out_refs):
    group, low = place_ref[0], place_ref[1]
    for r in range(groups):
        start = (group ^ r) * (2 * own_tiles)
        for t in range(2 * own_tiles):
            half = low if t < own_tiles else 1 - low
            q = start + half * own_tiles + t % own_tiles
            columns = pl.ds(pl.multiple_of(q * TILE_V, TILE_V), TILE_V)
            for o in range(amp_ref.shape[0] // TILE_O):
                rows = pl.ds(o * TILE_O, TILE_O)
                scale = mask_ref[o, q].astype(jnp.float32)
                out_refs[r][rows, pl.ds(t * TILE_V, TILE_V)] = amp_ref[rows, columns] * scale


def cut_amplitudes(place, mask, amplitudes, groups, own_tiles):
    rows = amplitudes.shape[0]
    depth = 2 * own_tiles * TILE_V
    smem = pl.BlockSpec(memory_space=pltpu.SMEM)
    return pl.pallas_call(
        functools.partial(cut_kernel, groups, own_tiles),
        out_shape=[jax.ShapeDtypeStruct((rows, depth), jnp.float32)] * groups,
        in_specs=[smem, smem] + in_vmem(1),
        out_specs=in_vmem(groups),
        compiler_params=pltpu.CompilerParams(vmem_limit_bytes=VMEM_LIMIT),
        cost_estimate=pl.CostEstimate(flops=1, bytes_accessed=1, transcendentals=0),
        name="cut",
    )(place, mask, amplitudes)


def split(x):
    high = x.astype(jnp.bfloat16)
    return high, (x - high.astype(jnp.float32)).astype(jnp.bfloat16)


def dot_kernel(lists, names, *refs):
    n = len(names)
    rel = dict(zip(names, refs[:n]))
    own_ref, other_ref = refs[n : n + 2]
    outs = refs[n + 2 :]
    depth = own_ref.shape[0]
    rows = refs[0].shape[0]
    parts = {r: split(rel[r][...]) for r in names}
    width = own_ref.shape[1] // 2
    for h in range(2):
        columns = pl.ds(h * width, width)
        right = [split(ref[:, columns]) for ref in (own_ref, other_ref)]
        for i, r in enumerate(lists[h]):
            total = None
            for k in range(2):
                b_high, b_low = right[k]
                a_high, a_low = (x[:, k * depth : (k + 1) * depth] for x in parts[r])
                for a, b in ((a_high, b_low), (a_low, b_high), (a_high, b_high)):
                    term = jnp.dot(a, b, preferred_element_type=jnp.float32)
                    total = term if total is None else total + term
            outs[h][i * rows : (i + 1) * rows, :] = total


def products(lists, rel, own, other):
    names = sorted(set(lists[0]) | set(lists[1]))
    rows, depth = rel[0].shape
    width = own.shape[1] // 2
    count = len(lists[0])
    return pl.pallas_call(
        functools.partial(dot_kernel, lists, names),
        out_shape=[jax.ShapeDtypeStruct((rows * count, width), jnp.float32)] * 2,
        in_specs=in_vmem(len(names) + 2),
        out_specs=in_vmem(2),
        compiler_params=pltpu.CompilerParams(vmem_limit_bytes=VMEM_LIMIT),
        cost_estimate=pl.CostEstimate(flops=1, bytes_accessed=1, transcendentals=0),
        name="products",
    )(*[rel[r] for r in names], own, other)


def pick(values, here):
    result = jnp.int32(values[0])
    for i in range(1, len(values)):
        result = jnp.where(here == i, jnp.int32(values[i]), result)
    return result


def line_blocks(own, nodes):
    here = lax.axis_index("occ")
    blocks = [own]
    places = [here]
    origins = [list(range(nodes))]
    size = 1
    while size < nodes:
        fresh, fresh_origins = [], []
        place = here % (2 * size)
        dist = jnp.where(place < size, size - 1 - place, place - size)
        middles = [g * 2 * size + size for g in range(nodes // (2 * size))]
        for block, origin in zip(blocks, origins):
            pairs = [(m - 1, m) for m in middles] + [(m, m - 1) for m in middles]
            moving = lax.ppermute(block, "occ", pairs)
            got = moving
            for hop in range(1, size):
                pairs = [(m - hop, m - hop - 1) for m in middles] + [(m + hop - 1, m + hop) for m in middles]
                moving = lax.ppermute(moving, "occ", pairs)
                got = jnp.where(dist == hop, moving, got)
            fresh.append(got)
            table = [0] * nodes
            for m in middles:
                for k in range(size):
                    table[m - 1 - k] = origin[m]
                    table[m + k] = origin[m - 1]
            fresh_origins.append(table)
        blocks += fresh
        origins += fresh_origins
        size *= 2
    return blocks, [pick(origin, here) for origin in origins]


def per_device(sizes, amplitudes, amp_mask, integrals, int_mask):
    n_occ, n_vir = sizes
    rows = amplitudes.shape[0]
    groups = n_vir // 2
    own_depth, width = integrals.shape
    half = width // 2

    def swap(x, bits):
        return lax.ppermute(x, "vir", [(i, i ^ bits) for i in range(n_vir)])

    me = lax.axis_index("vir")
    weighted = masked(integrals, int_mask, TILE_V)
    blocks, places = line_blocks(weighted, n_occ)

    position = jnp.stack([me // 2, me % 2]).astype(jnp.int32)
    parts = cut_amplitudes(after(position, weighted), amp_mask, amplitudes, groups, own_depth // TILE_V)
    rel = [parts[0]] + [None] * (groups - 1)
    for r in range(groups - 1, 0, -1):
        rel[r] = swap(parts[r], 2 * r)

    bits = []
    while (1 << len(bits)) < groups:
        bits.append(1 << len(bits))
    orders = [bits, bits[::-1]]
    away = [[r for r in range(groups) if r & o[0]] for o in orders]
    near = [[r for r in range(groups) if not r & o[0]] for o in orders]

    out = jnp.zeros((rows, n_occ * width), jnp.float32)
    token = parts
    for block, place in zip(blocks, places):
        block = after(block, *token)
        other = swap(block, 1)
        sent = products(away, rel, block, other)
        moving = [swap(sent[h], 2 * orders[h][0]) for h in range(2)]
        stay = products(near, rel, block, after(other, *sent))
        held = [{r: stay[h][i * rows : (i + 1) * rows] for i, r in enumerate(near[h])} for h in range(2)]
        for level in range(len(bits)):
            for h in range(2):
                for i, r in enumerate(sorted(held[h])):
                    held[h][r] = held[h][r] + moving[h][i * rows : (i + 1) * rows]
            if level + 1 == len(bits):
                break
            for h in range(2):
                bit = orders[h][level + 1]
                going = [r for r in sorted(held[h]) if r & bit]
                moving[h] = swap(jnp.concatenate([held[h][r] for r in going], axis=0), 2 * bit)
                for r in going:
                    del held[h][r]
        done = jnp.concatenate([held[h][0] for h in range(2)], axis=1)
        out = lax.dynamic_update_slice(out, done, (0, place * width))
        token = moving
    return out


def solution(mesh):
    sizes = (mesh.shape["occ"], mesh.shape["vir"])

    def run(*args):
        return per_device(sizes, *args)

    in_specs = (P(("occ", "vir"), None), P(("occ", "vir"), None), P("vir", "occ"), P("vir", "occ"))
    out_specs = P(("occ", "vir"), None)
    return jax.shard_map(run, mesh=mesh, in_specs=in_specs, out_specs=out_specs, check_vma=False)
```

```python
import functools

import jax
import jax.numpy as jnp
from jax import lax
from jax.experimental import pallas as pl
from jax.experimental.pallas import tpu as pltpu
from jax.sharding import PartitionSpec as P

TILE_O = 32
TILE_V = 128
VMEM_LIMIT = 12 * 1024 * 1024


def masked(values, mask, tile_rows):
    tile_r, tile_c = mask.shape
    scale = mask.astype(jnp.float32)[:, None, :, None]
    return (values.reshape(tile_r, tile_rows, tile_c, TILE_V) * scale).reshape(values.shape)


def after(value, *earlier):
    return lax.optimization_barrier((value,) + earlier)[0]


def in_vmem(count):
    return [pl.BlockSpec(memory_space=pltpu.VMEM)] * count


def cut_kernel(groups, own_tiles, place_ref, mask_ref, amp_ref, *out_refs):
    group, low = place_ref[0], place_ref[1]
    for r in range(groups):
        start = (group ^ r) * (2 * own_tiles)
        for t in range(2 * own_tiles):
            half = low if t < own_tiles else 1 - low
            q = start + half * own_tiles + t % own_tiles
            columns = pl.ds(pl.multiple_of(q * TILE_V, TILE_V), TILE_V)
            for o in range(amp_ref.shape[0] // TILE_O):
                rows = pl.ds(o * TILE_O, TILE_O)
                scale = mask_ref[o, q].astype(jnp.float32)
                out_refs[r][rows, pl.ds(t * TILE_V, TILE_V)] = amp_ref[rows, columns] * scale


def cut_amplitudes(place, mask, amplitudes, groups, own_tiles):
    rows = amplitudes.shape[0]
    depth = 2 * own_tiles * TILE_V
    smem = pl.BlockSpec(memory_space=pltpu.SMEM)
    return pl.pallas_call(
        functools.partial(cut_kernel, groups, own_tiles),
        out_shape=[jax.ShapeDtypeStruct((rows, depth), jnp.float32)] * groups,
        in_specs=[smem, smem] + in_vmem(1),
        out_specs=in_vmem(groups),
        compiler_params=pltpu.CompilerParams(vmem_limit_bytes=VMEM_LIMIT),
        cost_estimate=pl.CostEstimate(flops=1, bytes_accessed=1, transcendentals=0),
        name="cut",
    )(place, mask, amplitudes)


def split(x):
    high = x.astype(jnp.bfloat16)
    return high, (x - high.astype(jnp.float32)).astype(jnp.bfloat16)


def dot_kernel(lists, names, choices, *refs):
    n = len(names)
    which_ref, refs = refs[0], refs[1:]
    rel = dict(zip(names, refs[:n]))
    outs = refs[n + 2 * choices :]

    def body(own_ref, other_ref):
        depth = own_ref.shape[0]
        rows = refs[0].shape[0]
        parts = {r: split(rel[r][...]) for r in names}
        width = own_ref.shape[1] // 2
        for h in range(2):
            columns = pl.ds(h * width, width)
            right = [split(ref[:, columns]) for ref in (own_ref, other_ref)]
            for i, r in enumerate(lists[h]):
                total = None
                for k in range(2):
                    b_high, b_low = right[k]
                    a_high, a_low = (x[:, k * depth : (k + 1) * depth] for x in parts[r])
                    for a, b in ((a_high, b_low), (a_low, b_high), (a_high, b_high)):
                        term = jnp.dot(a, b, preferred_element_type=jnp.float32)
                        total = term if total is None else total + term
                outs[h][i * rows : (i + 1) * rows, :] = total

    for c in range(choices):
        if choices == 1:
            body(refs[n], refs[n + 1])
        else:
            pl.when(which_ref[0] == c)(functools.partial(body, refs[n + 2 * c], refs[n + 2 * c + 1]))


def products(lists, rel, which, rights):
    names = sorted(set(lists[0]) | set(lists[1]))
    rows = rel[0].shape[0]
    width = rights[0][0].shape[1] // 2
    count = len(lists[0])
    return pl.pallas_call(
        functools.partial(dot_kernel, lists, names, len(rights)),
        out_shape=[jax.ShapeDtypeStruct((rows * count, width), jnp.float32)] * 2,
        in_specs=[pl.BlockSpec(memory_space=pltpu.SMEM)] + in_vmem(len(names) + 2 * len(rights)),
        out_specs=in_vmem(2),
        compiler_params=pltpu.CompilerParams(vmem_limit_bytes=VMEM_LIMIT),
        cost_estimate=pl.CostEstimate(flops=1, bytes_accessed=1, transcendentals=0),
        name="products",
    )(which, *[rel[r] for r in names], *[x for pair in rights for x in pair])


def pick(values, here):
    result = jnp.int32(values[0])
    for i in range(1, len(values)):
        result = jnp.where(here == i, jnp.int32(values[i]), result)
    return result


def line_blocks(own, nodes):
    blocks = [[own]]
    origins = [list(range(nodes))]
    dists = [[0] * nodes]
    here = lax.axis_index("occ")
    size = 1
    while size < nodes:
        fresh, fresh_origins = [], []
        dist = [size - 1 - p if p < size else p - size for p in [i % (2 * size) for i in range(nodes)]]
        middles = [g * 2 * size + size for g in range(nodes // (2 * size))]
        for block, origin, far in zip(blocks, origins, dists):
            whole = block[0]
            for k in range(1, len(block)):
                whole = jnp.where(pick(far, here) == k, block[k], whole)
            pairs = [(m - 1, m) for m in middles] + [(m, m - 1) for m in middles]
            got = [lax.ppermute(whole, "occ", pairs)]
            for hop in range(1, size):
                pairs = [(m - hop, m - hop - 1) for m in middles] + [(m + hop - 1, m + hop) for m in middles]
                got.append(lax.ppermute(got[-1], "occ", pairs))
            fresh.append(got)
            table = [0] * nodes
            for m in middles:
                for k in range(size):
                    table[m - 1 - k] = origin[m]
                    table[m + k] = origin[m - 1]
            fresh_origins.append(table)
        dists += [dist] * len(fresh)
        blocks += fresh
        origins += fresh_origins
        size *= 2
    return blocks, dists, origins


def per_device(sizes, amplitudes, amp_mask, integrals, int_mask):
    n_occ, n_vir = sizes
    rows = amplitudes.shape[0]
    groups = n_vir // 2
    own_depth, width = integrals.shape
    half = width // 2

    def swap(x, bits):
        return lax.ppermute(x, "vir", [(i, i ^ bits) for i in range(n_vir)])

    def swap_cores(x, planes):
        pairs = [(o * n_vir + i, o * n_vir + (i ^ 1)) for o in planes for i in range(n_vir)]
        return lax.ppermute(x, ("occ", "vir"), pairs)

    me = lax.axis_index("vir")
    here = lax.axis_index("occ")
    weighted = masked(integrals, int_mask, TILE_V)
    blocks, dists, origins = line_blocks(weighted, n_occ)

    position = jnp.stack([me // 2, me % 2]).astype(jnp.int32)
    parts = cut_amplitudes(after(position, weighted), amp_mask, amplitudes, groups, own_depth // TILE_V)
    other = swap(weighted, 1)
    parts = lax.optimization_barrier((*parts, other))[:groups]
    rel = [parts[0]] + [None] * (groups - 1)
    for r in range(groups - 1, 0, -1):
        rel[r] = swap(parts[r], 2 * r)

    bits = []
    while (1 << len(bits)) < groups:
        bits.append(1 << len(bits))
    orders = [bits, bits[::-1]]
    away = [[r for r in range(groups) if r & o[0]] for o in orders]
    near = [[r for r in range(groups) if not r & o[0]] for o in orders]

    out = jnp.zeros((rows, n_occ * width), jnp.float32)
    last = len(blocks) - 1
    token = None
    for n, (block, far, origin) in enumerate(zip(blocks, dists, origins)):
        which = pick(far, here)
        if n > 1:
            block = list(lax.optimization_barrier((*block, *sent)))[: len(block)]
        if n == 0:
            rights = [(after(weighted, *[b[0] for b in blocks[1:3]]), other)]
        elif n == last:
            rights = [(b, swap_cores(b, [o for o in range(n_occ) if far[o] == k])) for k, b in enumerate(block)]
        else:
            whole = block[0]
            for k in range(1, len(block)):
                whole = jnp.where(which == k, block[k], whole)
            rights = [(whole, swap(whole, 1))]
        if token is not None:
            flat = lax.optimization_barrier((*[x for pair in rights for x in pair], *token))
            rights = [(flat[2 * k], flat[2 * k + 1]) for k in range(len(rights))]
        which = which.reshape(1)
        sent = products(away, rel, which, rights)
        moving = [swap(sent[h], 2 * orders[h][0]) for h in range(2)]
        stay = products(near, rel, after(which, *sent), rights)
        held = [{r: stay[h][i * rows : (i + 1) * rows] for i, r in enumerate(near[h])} for h in range(2)]
        moved = [None, None]
        for level in range(len(bits)):
            if n == 1 and level == 0 and last > 2:
                moving = list(lax.optimization_barrier((*moving, blocks[2][-1], blocks[3][0]))[:2])
            for h in range(2):
                for i, r in enumerate(sorted(held[h])):
                    held[h][r] = held[h][r] + moving[h][i * rows : (i + 1) * rows]
            if level + 1 == len(bits):
                break
            for h in range(2):
                bit = orders[h][level + 1]
                going = [r for r in sorted(held[h]) if r & bit]
                moved[h] = jnp.concatenate([held[h][r] for r in going], axis=0)
                moving[h] = swap(moved[h], 2 * bit)
                for r in going:
                    del held[h][r]
        done = jnp.concatenate([held[h][0] for h in range(2)], axis=1)
        out = lax.dynamic_update_slice(out, done, (0, pick(origin, here) * width))
        token = moving if n == 0 else moved
    return out


def solution(mesh):
    sizes = (mesh.shape["occ"], mesh.shape["vir"])

    def run(*args):
        return per_device(sizes, *args)

    in_specs = (P(("occ", "vir"), None), P(("occ", "vir"), None), P("vir", "occ"), P("vir", "occ"))
    out_specs = P(("occ", "vir"), None)
    return jax.shard_map(run, mesh=mesh, in_specs=in_specs, out_specs=out_specs, check_vma=False)
```

```python
import functools

import jax
import jax.numpy as jnp
from jax import lax
from jax.experimental import pallas as pl
from jax.experimental.pallas import tpu as pltpu
from jax.sharding import PartitionSpec as P

TILE_O = 32
TILE_V = 128
VMEM_LIMIT = 12 * 1024 * 1024


def masked(values, mask, tile_rows):
    tile_r, tile_c = mask.shape
    scale = mask.astype(jnp.float32)[:, None, :, None]
    return (values.reshape(tile_r, tile_rows, tile_c, TILE_V) * scale).reshape(values.shape)


def after(value, *earlier):
    return lax.optimization_barrier((value,) + earlier)[0]


def in_vmem(count):
    return [pl.BlockSpec(memory_space=pltpu.VMEM)] * count


def cut_kernel(groups, own_tiles, place_ref, mask_ref, amp_ref, *out_refs):
    group, low = place_ref[0], place_ref[1]
    for r in range(groups):
        start = (group ^ r) * (2 * own_tiles)
        for t in range(2 * own_tiles):
            half = low if t < own_tiles else 1 - low
            q = start + half * own_tiles + t % own_tiles
            columns = pl.ds(pl.multiple_of(q * TILE_V, TILE_V), TILE_V)
            for o in range(amp_ref.shape[0] // TILE_O):
                rows = pl.ds(o * TILE_O, TILE_O)
                scale = mask_ref[o, q].astype(jnp.float32)
                out_refs[r][rows, pl.ds(t * TILE_V, TILE_V)] = amp_ref[rows, columns] * scale


def cut_amplitudes(place, mask, amplitudes, groups, own_tiles):
    rows = amplitudes.shape[0]
    depth = 2 * own_tiles * TILE_V
    smem = pl.BlockSpec(memory_space=pltpu.SMEM)
    return pl.pallas_call(
        functools.partial(cut_kernel, groups, own_tiles),
        out_shape=[jax.ShapeDtypeStruct((rows, depth), jnp.float32)] * groups,
        in_specs=[smem, smem] + in_vmem(1),
        out_specs=in_vmem(groups),
        compiler_params=pltpu.CompilerParams(vmem_limit_bytes=VMEM_LIMIT),
        cost_estimate=pl.CostEstimate(flops=1, bytes_accessed=1, transcendentals=0),
        name="cut",
    )(place, mask, amplitudes)


def split(x):
    high = x.astype(jnp.bfloat16)
    return high, (x - high.astype(jnp.float32)).astype(jnp.bfloat16)


def dot_kernel(lists, names, *refs):
    n = len(names)
    rel = dict(zip(names, refs[:n]))
    own_ref, other_ref = refs[n : n + 2]
    outs = refs[n + 2 :]
    depth = own_ref.shape[0]
    rows = refs[0].shape[0]
    parts = {r: split(rel[r][...]) for r in names}
    width = own_ref.shape[1] // 2
    for h in range(2):
        columns = pl.ds(h * width, width)
        right = [split(ref[:, columns]) for ref in (own_ref, other_ref)]
        for i, r in enumerate(lists[h]):
            total = None
            for k in range(2):
                b_high, b_low = right[k]
                a_high, a_low = (x[:, k * depth : (k + 1) * depth] for x in parts[r])
                for a, b in ((a_high, b_low), (a_low, b_high), (a_high, b_high)):
                    term = jnp.dot(a, b, preferred_element_type=jnp.float32)
                    total = term if total is None else total + term
            outs[h][i * rows : (i + 1) * rows, :] = total


def products(lists, rel, own, other):
    names = sorted(set(lists[0]) | set(lists[1]))
    rows = rel[0].shape[0]
    width = own.shape[1] // 2
    count = len(lists[0])
    return pl.pallas_call(
        functools.partial(dot_kernel, lists, names),
        out_shape=[jax.ShapeDtypeStruct((rows * count, width), jnp.float32)] * 2,
        in_specs=in_vmem(len(names) + 2),
        out_specs=in_vmem(2),
        compiler_params=pltpu.CompilerParams(vmem_limit_bytes=VMEM_LIMIT),
        cost_estimate=pl.CostEstimate(flops=1, bytes_accessed=1, transcendentals=0),
        name="products",
    )(*[rel[r] for r in names], own, other)


def line_blocks(own, nodes):
    here = lax.axis_index("occ")

    def direct(x, d):
        return lax.ppermute(x, "occ", [(i, i ^ d) for i in range(nodes)])

    if nodes != 4:
        return [(d, own if d == 0 else direct(own, d)) for d in range(nodes)]
    near = direct(own, 1)
    centre = lax.ppermute(own, "occ", [(1, 2), (2, 1)])
    far = lax.ppermute(own, "occ", [(0, 3), (3, 0)])
    middle = (here == 1) | (here == 2)
    last = lax.ppermute(jnp.where(middle, centre, own), "occ", [(1, 0), (2, 3), (0, 2), (3, 1)])
    return [(0, own), (1, near), (3, (middle, centre, far)), (2, last)]


def per_device(sizes, amplitudes, amp_mask, integrals, int_mask):
    n_occ, n_vir = sizes
    rows = amplitudes.shape[0]
    groups = n_vir // 2
    own_depth, width = integrals.shape

    def swap(x, bits):
        return lax.ppermute(x, "vir", [(i, i ^ bits) for i in range(n_vir)])

    me = lax.axis_index("vir")
    weighted = masked(integrals, int_mask, TILE_V)
    blocks = line_blocks(weighted, n_occ)

    position = jnp.stack([me // 2, me % 2]).astype(jnp.int32)
    parts = cut_amplitudes(after(position, weighted), amp_mask, amplitudes, groups, own_depth // TILE_V)
    rel = [parts[0]] + [None] * (groups - 1)
    for r in range(groups - 1, 0, -1):
        rel[r] = swap(parts[r], 2 * r)

    bits = []
    while (1 << len(bits)) < groups:
        bits.append(1 << len(bits))
    orders = [bits, bits[::-1]]
    away = [[r for r in range(groups) if r & o[0]] for o in orders]
    near = [[r for r in range(groups) if not r & o[0]] for o in orders]

    out = jnp.zeros((rows, n_occ * width), jnp.float32)
    token = [rel[1]]
    for n, (d, block) in enumerate(blocks):
        if isinstance(block, tuple):
            middle, centre, far = block
            centre, far = lax.optimization_barrier((centre, far, *sent))[:2]
            block = jnp.where(middle, centre, far)
        elif n > 1:
            block = after(block, *sent)
        if n == 0:
            first_blocks = [blocks[1][1]] + ([blocks[2][1][1]] if isinstance(blocks[2][1], tuple) else [])
            other = swap(after(block, rel[1]), 1)
            block = after(block, *first_blocks)
        else:
            other = swap(block, 1)
            block, other = lax.optimization_barrier((block, other, *token))[:2]
        sent = products(away, rel, block, other)
        moving = [swap(sent[h], 2 * orders[h][0]) for h in range(2)]
        stay = products(near, rel, after(block, *sent), other)
        held = [{r: stay[h][i * rows : (i + 1) * rows] for i, r in enumerate(near[h])} for h in range(2)]
        moved = [None, None]
        for level in range(len(bits)):
            if n in (1, 2) and level == 0:
                soon = blocks[n + 1][1]
                moving = list(lax.optimization_barrier((*moving, soon[2] if isinstance(soon, tuple) else soon))[:2])
            for h in range(2):
                for i, r in enumerate(sorted(held[h])):
                    held[h][r] = held[h][r] + moving[h][i * rows : (i + 1) * rows]
            if level + 1 == len(bits):
                break
            for h in range(2):
                bit = orders[h][level + 1]
                going = [r for r in sorted(held[h]) if r & bit]
                moved[h] = jnp.concatenate([held[h][r] for r in going], axis=0)
                moving[h] = swap(moved[h], 2 * bit)
                for r in going:
                    del held[h][r]
        done = jnp.concatenate([held[h][0] for h in range(2)], axis=1)
        place = lax.axis_index("occ") ^ d
        out = lax.dynamic_update_slice(out, done, (0, place * width))
        token = moved if n > 1 else moving
    return out


def solution(mesh):
    sizes = (mesh.shape["occ"], mesh.shape["vir"])

    def run(*args):
        return per_device(sizes, *args)

    in_specs = (P(("occ", "vir"), None), P(("occ", "vir"), None), P("vir", "occ"), P("vir", "occ"))
    out_specs = P(("occ", "vir"), None)
    return jax.shard_map(run, mesh=mesh, in_specs=in_specs, out_specs=out_specs, check_vma=False)
```

```python
import functools

import jax
import jax.numpy as jnp
from jax import lax
from jax.experimental import pallas as pl
from jax.experimental.pallas import tpu as pltpu
from jax.sharding import PartitionSpec as P

TILE_O = 32
TILE_V = 128
VMEM_LIMIT = 12 * 1024 * 1024


def masked(values, mask, tile_rows):
    tile_r, tile_c = mask.shape
    scale = mask.astype(jnp.float32)[:, None, :, None]
    return (values.reshape(tile_r, tile_rows, tile_c, TILE_V) * scale).reshape(values.shape)


def after(value, *earlier):
    return lax.optimization_barrier((value,) + earlier)[0]


def in_vmem(count):
    return [pl.BlockSpec(memory_space=pltpu.VMEM)] * count


def kernel_call(body, outs, operands, smem, name):
    smem_spec = pl.BlockSpec(memory_space=pltpu.SMEM)
    return pl.pallas_call(
        body,
        out_shape=[jax.ShapeDtypeStruct(shape, jnp.float32) for shape in outs],
        in_specs=[smem_spec] * smem + in_vmem(len(operands) - smem),
        out_specs=in_vmem(len(outs)),
        compiler_params=pltpu.CompilerParams(vmem_limit_bytes=VMEM_LIMIT),
        cost_estimate=pl.CostEstimate(flops=1, bytes_accessed=1, transcendentals=0),
        name=name,
    )(*operands)


def tiles(start, count):
    return pl.ds(pl.multiple_of(start * TILE_V, TILE_V), count * TILE_V)


def cut_kernel(groups, depth_tiles, place_ref, mask_ref, amp_ref, *out_refs):
    for r in range(groups):
        start = (place_ref[0] ^ r) * depth_tiles
        for t in range(depth_tiles):
            for o in range(amp_ref.shape[0] // TILE_O):
                rows = pl.ds(o * TILE_O, TILE_O)
                scale = mask_ref[o, start + t].astype(jnp.float32)
                out_refs[r][rows, tiles(t, 1)] = amp_ref[rows, tiles(start + t, 1)] * scale


def halves_kernel(place_ref, mask_ref, int_ref, mine_ref, theirs_ref):
    low = place_ref[1]
    count = mine_ref.shape[1] // TILE_V
    for half, out_ref in ((low, mine_ref), (1 - low, theirs_ref)):
        for t in range(count):
            q = half * count + t
            for k in range(int_ref.shape[0] // TILE_V):
                scale = mask_ref[k, q].astype(jnp.float32)
                out_ref[tiles(k, 1), tiles(t, 1)] = int_ref[tiles(k, 1), tiles(q, 1)] * scale


def join_kernel(place_ref, mine_ref, other_ref, out_ref):
    low = place_ref[1]
    depth = mine_ref.shape[0]
    out_ref[pl.ds(pl.multiple_of(low * depth, depth), depth), :] = mine_ref[...]
    out_ref[pl.ds(pl.multiple_of((1 - low) * depth, depth), depth), :] = other_ref[...]


def split(x):
    high = x.astype(jnp.bfloat16)
    return high, (x - high.astype(jnp.float32)).astype(jnp.bfloat16)


def dot_kernel(count, *refs):
    left, block_ref, outs = refs[: 2 * count], refs[2 * count], refs[2 * count + 1 :]
    rows = left[0].shape[0]
    b_high, b_low = split(block_ref[...])
    for h in range(2):
        for i in range(count):
            a_high, a_low = split(left[h * count + i][...])
            total = None
            for a, b in ((a_high, b_low), (a_low, b_high), (a_high, b_high)):
                term = jnp.dot(a, b, preferred_element_type=jnp.float32)
                total = term if total is None else total + term
            outs[h][i * rows : (i + 1) * rows, :] = total


def products(left, block):
    count = len(left[0])
    shape = (count * left[0][0].shape[0], block.shape[1])
    return kernel_call(functools.partial(dot_kernel, count), [shape] * 2, [*left[0], *left[1], block], 0, "products")


def line_blocks(own, nodes):
    here = lax.axis_index("occ")

    def direct(x, d):
        return lax.ppermute(x, "occ", [(i, i ^ d) for i in range(nodes)])

    if nodes != 4:
        return [(d, own if d == 0 else direct(own, d)) for d in range(nodes)]
    near = direct(own, 1)
    centre = lax.ppermute(own, "occ", [(1, 2), (2, 1)])
    far = lax.ppermute(own, "occ", [(0, 3), (3, 0)])
    middle = (here == 1) | (here == 2)
    last = lax.ppermute(jnp.where(middle, centre, own), "occ", [(1, 0), (2, 3), (0, 2), (3, 1)])
    return [(0, own), (1, near), (3, (middle, centre, far)), (2, last)]


def per_device(sizes, amplitudes, amp_mask, integrals, int_mask):
    n_occ, n_vir = sizes
    rows = amplitudes.shape[0]
    groups = n_vir // 2
    own_depth, width = integrals.shape
    depth, half = 2 * own_depth, width // 2

    def swap(x, bits):
        return lax.ppermute(x, "vir", [(i, i ^ bits) for i in range(n_vir)])

    me, here = lax.axis_index("vir"), lax.axis_index("occ")
    position = jnp.stack([me // 2, me % 2]).astype(jnp.int32)
    mine, theirs = kernel_call(halves_kernel, [(own_depth, half)] * 2, [position, int_mask, integrals], 2, "halves")
    other = swap(theirs, 1)
    parts = kernel_call(
        functools.partial(cut_kernel, groups, depth // TILE_V), [(rows, depth)] * groups, [after(position, mine), amp_mask, amplitudes], 2, "cut"
    )
    (whole,) = kernel_call(join_kernel, [(depth, half)], [position, mine, after(other, *parts)], 1, "join")
    blocks = line_blocks(whole, n_occ)

    rel = [[parts[0]] + [None] * (groups - 1), [None] * groups]
    for r in range(groups - 1, 0, -1):
        rel[0][r] = swap(parts[r], 2 * r)
    for r in range(groups - 1, -1, -1):
        rel[1][r] = swap(rel[0][r] if r else after(parts[0], rel[0][groups - 1]), 1)

    bits = []
    while (1 << len(bits)) < groups:
        bits.append(1 << len(bits))
    orders = [bits, bits[::-1]]
    away = [[r for r in range(groups) if r & o[0]] for o in orders]
    near = [[r for r in range(groups) if not r & o[0]] for o in orders]

    out = jnp.zeros((rows, n_occ * width), jnp.float32)
    token = None
    for n, (d, block) in enumerate(blocks):
        if isinstance(block, tuple):
            middle, centre, far = block
            centre, far = lax.optimization_barrier((centre, far, *sent))[:2]
            block = jnp.where(middle, centre, far)
        if n == 0:
            block = after(block, blocks[1][1], *(blocks[2][1][1:2] if isinstance(blocks[2][1], tuple) else ()))
        else:
            block = after(block, *token)
        sent = products([[rel[h][r] for r in away[h]] for h in range(2)], block)
        moving = [swap(sent[h], 2 * orders[h][0]) for h in range(2)]
        stay = products([[rel[h][r] for r in near[h]] for h in range(2)], after(block, *sent))
        held = [{r: stay[h][i * rows : (i + 1) * rows] for i, r in enumerate(near[h])} for h in range(2)]
        moved = [None, None]
        for level in range(len(bits)):
            if n in (1, 2) and level == 0:
                soon = blocks[n + 1][1]
                moving = list(lax.optimization_barrier((*moving, soon[2] if isinstance(soon, tuple) else soon))[:2])
            for h in range(2):
                for i, r in enumerate(sorted(held[h])):
                    held[h][r] = held[h][r] + moving[h][i * rows : (i + 1) * rows]
            if level + 1 == len(bits):
                break
            for h in range(2):
                bit = orders[h][level + 1]
                going = [r for r in sorted(held[h]) if r & bit]
                moved[h] = jnp.concatenate([held[h][r] for r in going], axis=0)
                moving[h] = swap(moved[h], 2 * bit)
                for r in going:
                    del held[h][r]
        column = (here ^ d) * width
        out = lax.dynamic_update_slice(out, held[0][0], (0, column + (me % 2) * half))
        out = lax.dynamic_update_slice(out, swap(held[1][0], 1), (0, column + (1 - me % 2) * half))
        token = moved if n > 1 else moving
    return out


def solution(mesh):
    sizes = (mesh.shape["occ"], mesh.shape["vir"])

    def run(*args):
        return per_device(sizes, *args)

    in_specs = (P(("occ", "vir"), None), P(("occ", "vir"), None), P("vir", "occ"), P("vir", "occ"))
    out_specs = P(("occ", "vir"), None)
    return jax.shard_map(run, mesh=mesh, in_specs=in_specs, out_specs=out_specs, check_vma=False)
```

```python
import functools

import jax
import jax.numpy as jnp
from jax import lax
from jax.experimental import pallas as pl
from jax.experimental.pallas import tpu as pltpu
from jax.sharding import PartitionSpec as P

TILE_O = 32
TILE_V = 128
VMEM_LIMIT = 12 * 1024 * 1024


def after(value, *earlier):
    return lax.optimization_barrier((value,) + earlier)[0]


def in_vmem(count):
    return [pl.BlockSpec(memory_space=pltpu.VMEM)] * count


def in_hbm(count):
    return [pl.BlockSpec(memory_space=pltpu.HBM)] * count


def kernel_call(body, outs, operands, name, from_hbm=False, scratch=()):
    if from_hbm:
        operands = [pltpu.with_memory_space_constraint(x, pltpu.HBM) for x in operands]
    return pl.pallas_call(
        body,
        out_shape=[pltpu.VMEM(shape, jnp.float32) for shape in outs],
        in_specs=in_hbm(len(operands)) if from_hbm else in_vmem(len(operands)),
        out_specs=in_vmem(len(outs)),
        scratch_shapes=list(scratch),
        compiler_params=pltpu.CompilerParams(vmem_limit_bytes=VMEM_LIMIT),
        cost_estimate=pl.CostEstimate(flops=1, bytes_accessed=1, transcendentals=0),
        name=name,
    )(*operands)


def tiles(start, count):
    return pl.ds(pl.multiple_of(start * TILE_V, TILE_V), count * TILE_V)


def cut_kernel(groups, depth_tiles, mask_hbm, amp_hbm, *refs):
    out_refs, (mask_ref, amp_ref, mask_sem, amp_sems) = refs[:groups], refs[groups:]
    group = lax.axis_index("vir") // 2
    mask_copy = pltpu.make_async_copy(mask_hbm, mask_ref, mask_sem)
    mask_copy.start()
    starts = [(group ^ r) * depth_tiles for r in range(groups)]
    order = range(groups - 1, -1, -1)
    copies = {
        r: pltpu.make_async_copy(amp_hbm.at[:, tiles(starts[r], depth_tiles)], amp_ref.at[r], amp_sems.at[r]) for r in order
    }
    for r in order:
        copies[r].start()
    mask_copy.wait()
    for r in order:
        copies[r].wait()
        for t in range(depth_tiles):
            for o in range(amp_hbm.shape[0] // TILE_O):
                rows = pl.ds(o * TILE_O, TILE_O)
                scale = mask_ref[o, starts[r] + t].astype(jnp.float32)
                out_refs[r][rows, tiles(t, 1)] = amp_ref[r, rows, tiles(t, 1)] * scale


def cut(mask, amplitudes, groups, depth):
    rows = amplitudes.shape[0]
    scratch = [
        pltpu.SMEM(mask.shape, jnp.int32),
        pltpu.VMEM((groups, rows, depth), jnp.float32),
        pltpu.SemaphoreType.DMA,
        pltpu.SemaphoreType.DMA((groups,)),
    ]
    body = functools.partial(cut_kernel, groups, depth // TILE_V)
    return kernel_call(body, [(rows, depth)] * groups, [mask, amplitudes], "cut", True, scratch)


def halves_kernel(mask_hbm, int_hbm, mine_ref, theirs_ref, mask_ref, int_ref, mask_sem, int_sems):
    low = lax.axis_index("vir") % 2
    count = mine_ref.shape[1] // TILE_V
    mask_copy = pltpu.make_async_copy(mask_hbm, mask_ref, mask_sem)
    mask_copy.start()
    work = ((1 - low, theirs_ref), (low, mine_ref))
    copies = [
        pltpu.make_async_copy(int_hbm.at[:, tiles(half * count, count)], int_ref.at[i], int_sems.at[i])
        for i, (half, _) in enumerate(work)
    ]
    for copy in copies:
        copy.start()
    mask_copy.wait()
    for i, (half, out_ref) in enumerate(work):
        copies[i].wait()
        for t in range(count):
            for k in range(int_hbm.shape[0] // TILE_V):
                scale = mask_ref[k, half * count + t].astype(jnp.float32)
                out_ref[tiles(k, 1), tiles(t, 1)] = int_ref[i, tiles(k, 1), tiles(t, 1)] * scale


def halves(mask, integrals):
    depth, width = integrals.shape
    scratch = [
        pltpu.SMEM(mask.shape, jnp.int32),
        pltpu.VMEM((2, depth, width // 2), jnp.float32),
        pltpu.SemaphoreType.DMA,
        pltpu.SemaphoreType.DMA((2,)),
    ]
    return kernel_call(halves_kernel, [(depth, width // 2)] * 2, [mask, integrals], "halves", True, scratch)


def join_kernel(mine_ref, other_ref, out_ref):
    low = lax.axis_index("vir") % 2
    depth = mine_ref.shape[0]
    out_ref[pl.ds(pl.multiple_of(low * depth, depth), depth), :] = mine_ref[...]
    out_ref[pl.ds(pl.multiple_of((1 - low) * depth, depth), depth), :] = other_ref[...]


def fold_kernel(rows, stays, goes, held_ref, got_ref, *out_refs):
    for out_ref, places in zip(out_refs, (stays, goes)):
        for i, k in enumerate(places):
            take = pl.ds(k * rows, rows)
            out_ref[i * rows : (i + 1) * rows, :] = held_ref[take, :] + got_ref[take, :]


def fold(rows, stays, goes, held, got):
    outs = [(len(places) * rows, held.shape[1]) for places in (stays, goes) if places]
    return kernel_call(functools.partial(fold_kernel, rows, stays, goes), outs, [held, got], "fold")


def write_kernel(d, half, offset, held_ref, got_ref, other_ref, *refs):
    out_ref, piece_ref, sems = refs[-3:]
    low = lax.axis_index("vir") % 2
    place = lax.axis_index("occ") ^ d
    width = held_ref.shape[1] // TILE_V
    starts = [(2 * place + h) * (half // TILE_V) + offset // TILE_V for h in (low, 1 - low)]
    piece_ref[...] = held_ref[...] + got_ref[...]
    copies = [
        pltpu.make_async_copy(source, out_ref.at[:, tiles(start, width)], sems.at[i])
        for i, (source, start) in enumerate(zip((piece_ref, other_ref), starts))
    ]
    for copy in copies:
        copy.start()
    for copy in copies:
        copy.wait()


def write(out, shape, d, half, offset, held, got, other):
    given = [] if out is None else [out]
    return pl.pallas_call(
        functools.partial(write_kernel, d, half, offset),
        out_shape=jax.ShapeDtypeStruct(shape, jnp.float32),
        in_specs=in_vmem(3) + in_hbm(len(given)),
        out_specs=pl.BlockSpec(memory_space=pltpu.HBM),
        scratch_shapes=[pltpu.VMEM(held.shape, jnp.float32), pltpu.SemaphoreType.DMA((2,))],
        input_output_aliases={3: 0} if given else {},
        compiler_params=pltpu.CompilerParams(vmem_limit_bytes=VMEM_LIMIT),
        cost_estimate=pl.CostEstimate(flops=1, bytes_accessed=1, transcendentals=0),
        name="write",
    )(held, got, other, *given)


def split(x):
    high = x.astype(jnp.bfloat16)
    return high, (x - high.astype(jnp.float32)).astype(jnp.bfloat16)


def dot_kernel(count, *refs):
    left, block_ref, outs = refs[: 2 * count], refs[2 * count], refs[2 * count + 1 :]
    rows = left[0].shape[0]
    b_high, b_low = split(block_ref[...])
    for h in range(2):
        for i in range(count):
            a_high, a_low = split(left[h * count + i][...])
            total = None
            for a, b in ((a_high, b_low), (a_low, b_high), (a_high, b_high)):
                term = jnp.dot(a, b, preferred_element_type=jnp.float32)
                total = term if total is None else total + term
            outs[h][i * rows : (i + 1) * rows, :] = total


def products(left, block):
    count = len(left[0])
    shape = (count * left[0][0].shape[0], block.shape[1])
    return kernel_call(functools.partial(dot_kernel, count), [shape] * 2, [*left[0], *left[1], block], "products")


def line_blocks(own, nodes):
    here = lax.axis_index("occ")

    def direct(x, d):
        return lax.ppermute(x, "occ", [(i, i ^ d) for i in range(nodes)])

    if nodes != 4:
        return [(d, own if d == 0 else direct(own, d), 0) for d in range(nodes)]
    near = direct(own, 1)
    centre = lax.ppermute(own, "occ", [(1, 2), (2, 1)])
    far = lax.ppermute(own, "occ", [(0, 3), (3, 0)])
    middle = (here == 1) | (here == 2)
    count = own.shape[1] // TILE_V
    cuts = [0, (2 * count + 2) // 3 * TILE_V, own.shape[1]]
    last = []
    for lo, hi in zip(cuts, cuts[1:]):
        moving = jnp.where(middle, centre[:, lo:hi], own[:, lo:hi])
        last.append((2, lax.ppermute(moving, "occ", [(1, 0), (2, 3), (0, 2), (3, 1)]), lo))
    return [(0, own, 0), (1, near, 0), (3, (middle, centre, far), 0), *last]


def per_device(sizes, amplitudes, amp_mask, integrals, int_mask):
    n_occ, n_vir = sizes
    rows = amplitudes.shape[0]
    groups = n_vir // 2
    own_depth, width = integrals.shape
    depth, half = 2 * own_depth, width // 2

    def swap(x, bits):
        return lax.ppermute(x, "vir", [(i, i ^ bits) for i in range(n_vir)])

    mine, theirs = halves(int_mask, integrals)
    other = swap(theirs, 1)
    parts = cut(after(amp_mask, mine), amplitudes, groups, depth)
    (whole,) = kernel_call(join_kernel, [(depth, half)], [mine, after(other, *parts)], "join")
    blocks = line_blocks(whole, n_occ)
    arrived = [block[2] if isinstance(block, tuple) else block for _, block, _ in blocks]

    rel = [[parts[0]] + [None] * (groups - 1), [None] * groups]
    for r in range(groups - 1, 0, -1):
        rel[0][r] = swap(parts[r], 2 * r)
    for r in range(groups - 1, -1, -1):
        rel[1][r] = swap(rel[0][r] if r else after(parts[0], rel[0][groups - 1]), 1)

    bits = []
    while (1 << len(bits)) < groups:
        bits.append(1 << len(bits))
    orders = [bits, bits[::-1]]
    away = [[r for r in range(groups) if r & o[0]] for o in orders]
    near = [[r for r in range(groups) if not r & o[0]] for o in orders]

    out = None
    token = None
    for n, (d, block, offset) in enumerate(blocks):
        if isinstance(block, tuple):
            middle, centre, far = block
            centre, far = lax.optimization_barrier((centre, far, *sent))[:2]
            block = jnp.where(middle, centre, far)
        if n == 0:
            block = after(block, blocks[1][1], *(blocks[2][1][1:2] if isinstance(blocks[2][1], tuple) else ()))
        else:
            block = after(block, *token)
        sent = products([[rel[h][r] for r in away[h]] for h in range(2)], block)
        moving = [swap(sent[h], 2 * orders[h][0]) for h in range(2)]
        soon = arrived[n + 1 : n + 2] if n > 0 else []
        held = list(products([[rel[h][r] for r in near[h]] for h in range(2)], after(block, *sent, *soon)))
        names = [near[0], near[1]]
        for level in range(1, len(bits)):
            for h in (1, 0):
                bit = orders[h][level]
                stays = [i for i, r in enumerate(names[h]) if not r & bit]
                goes = [i for i, r in enumerate(names[h]) if r & bit]
                held[h], moved = fold(rows, stays, goes, held[h], moving[h])
                moving[h] = swap(moved, 2 * bit)
                names[h] = [names[h][i] for i in stays]
        token = held if out is None else [*held, out]
        (theirs,) = fold(rows, [0], [], held[1], moving[1])
        out = write(out, (rows, n_occ * width), d, half, offset, held[0], moving[0], swap(theirs, 1))
    return out


def solution(mesh):
    sizes = (mesh.shape["occ"], mesh.shape["vir"])

    def run(*args):
        return per_device(sizes, *args)

    in_specs = (P(("occ", "vir"), None), P(("occ", "vir"), None), P("vir", "occ"), P("vir", "occ"))
    out_specs = P(("occ", "vir"), None)
    return jax.shard_map(run, mesh=mesh, in_specs=in_specs, out_specs=out_specs, check_vma=False)
```

```python
import functools

import jax
import jax.numpy as jnp
from jax import lax
from jax.experimental import pallas as pl
from jax.experimental.pallas import tpu as pltpu
from jax.sharding import PartitionSpec as P

TILE_O = 32
TILE_V = 128
VMEM_LIMIT = 12 * 1024 * 1024


def after(value, *earlier):
    return lax.optimization_barrier((value,) + earlier)[0]


def in_vmem(count):
    return [pl.BlockSpec(memory_space=pltpu.VMEM)] * count


def in_hbm(count):
    return [pl.BlockSpec(memory_space=pltpu.HBM)] * count


def kernel_call(body, outs, operands, name, from_hbm=False, scratch=()):
    space = pltpu.HBM if from_hbm else pltpu.VMEM
    operands = [pltpu.with_memory_space_constraint(x, space) for x in operands]
    return pl.pallas_call(
        body,
        out_shape=[pltpu.VMEM(shape, jnp.float32) for shape in outs],
        in_specs=in_hbm(len(operands)) if from_hbm else in_vmem(len(operands)),
        out_specs=in_vmem(len(outs)),
        scratch_shapes=list(scratch),
        compiler_params=pltpu.CompilerParams(vmem_limit_bytes=VMEM_LIMIT),
        cost_estimate=pl.CostEstimate(flops=1, bytes_accessed=1, transcendentals=0),
        name=name,
    )(*operands)


def tiles(start, count):
    return pl.ds(pl.multiple_of(start * TILE_V, TILE_V), count * TILE_V)


def cut_kernel(groups, depth_tiles, mask_hbm, amp_hbm, *refs):
    out_refs, (mask_ref, amp_ref, mask_sem, amp_sems) = refs[:groups], refs[groups:]
    group = lax.axis_index("vir") // 2
    mask_copy = pltpu.make_async_copy(mask_hbm, mask_ref, mask_sem)
    mask_copy.start()
    starts = [(group ^ r) * depth_tiles for r in range(groups)]
    order = range(groups - 1, -1, -1)
    copies = {
        r: pltpu.make_async_copy(amp_hbm.at[:, tiles(starts[r], depth_tiles)], amp_ref.at[r], amp_sems.at[r]) for r in order
    }
    for r in order:
        copies[r].start()
    mask_copy.wait()
    for r in order:
        copies[r].wait()
        for t in range(depth_tiles):
            for o in range(amp_hbm.shape[0] // TILE_O):
                rows = pl.ds(o * TILE_O, TILE_O)
                scale = mask_ref[o, starts[r] + t].astype(jnp.float32)
                out_refs[r][rows, tiles(t, 1)] = amp_ref[r, rows, tiles(t, 1)] * scale


def cut(mask, amplitudes, groups, depth):
    rows = amplitudes.shape[0]
    scratch = [
        pltpu.SMEM(mask.shape, jnp.int32),
        pltpu.VMEM((groups, rows, depth), jnp.float32),
        pltpu.SemaphoreType.DMA,
        pltpu.SemaphoreType.DMA((groups,)),
    ]
    body = functools.partial(cut_kernel, groups, depth // TILE_V)
    return kernel_call(body, [(rows, depth)] * groups, [mask, amplitudes], "cut", True, scratch)


def halves_kernel(mask_hbm, int_hbm, mine_ref, theirs_ref, mask_ref, int_ref, mask_sem, int_sems):
    low = lax.axis_index("vir") % 2
    count = mine_ref.shape[1] // TILE_V
    mask_copy = pltpu.make_async_copy(mask_hbm, mask_ref, mask_sem)
    mask_copy.start()
    work = ((1 - low, theirs_ref), (low, mine_ref))
    copies = [
        pltpu.make_async_copy(int_hbm.at[:, tiles(half * count, count)], int_ref.at[i], int_sems.at[i])
        for i, (half, _) in enumerate(work)
    ]
    for copy in copies:
        copy.start()
    mask_copy.wait()
    for i, (half, out_ref) in enumerate(work):
        copies[i].wait()
        for t in range(count):
            for k in range(int_hbm.shape[0] // TILE_V):
                scale = mask_ref[k, half * count + t].astype(jnp.float32)
                out_ref[tiles(k, 1), tiles(t, 1)] = int_ref[i, tiles(k, 1), tiles(t, 1)] * scale


def halves(mask, integrals):
    depth, width = integrals.shape
    scratch = [
        pltpu.SMEM(mask.shape, jnp.int32),
        pltpu.VMEM((2, depth, width // 2), jnp.float32),
        pltpu.SemaphoreType.DMA,
        pltpu.SemaphoreType.DMA((2,)),
    ]
    return kernel_call(halves_kernel, [(depth, width // 2)] * 2, [mask, integrals], "halves", True, scratch)


def join_kernel(mine_ref, other_ref, out_ref):
    low = lax.axis_index("vir") % 2
    depth = mine_ref.shape[0]
    out_ref[pl.ds(pl.multiple_of(low * depth, depth), depth), :] = mine_ref[...]
    out_ref[pl.ds(pl.multiple_of((1 - low) * depth, depth), depth), :] = other_ref[...]


def fold_kernel(rows, stays, goes, held_ref, got_ref, *out_refs):
    for out_ref, places in zip(out_refs, (stays, goes)):
        for i, k in enumerate(places):
            take = pl.ds(k * rows, rows)
            out_ref[i * rows : (i + 1) * rows, :] = held_ref[take, :] + got_ref[take, :]


def fold(rows, stays, goes, held, got):
    outs = [(len(places) * rows, held.shape[1]) for places in (stays, goes) if places]
    return kernel_call(functools.partial(fold_kernel, rows, stays, goes), outs, [held, got], "fold")


def write_kernel(d, half, offset, held_ref, got_ref, other_ref, *refs):
    out_ref, piece_ref, sems = refs[-3:]
    low = lax.axis_index("vir") % 2
    place = lax.axis_index("occ") ^ d
    width = held_ref.shape[1] // TILE_V
    starts = [(2 * place + h) * (half // TILE_V) + offset // TILE_V for h in (low, 1 - low)]
    piece_ref[...] = held_ref[...] + got_ref[...]
    copies = [
        pltpu.make_async_copy(source, out_ref.at[:, tiles(start, width)], sems.at[i])
        for i, (source, start) in enumerate(zip((piece_ref, other_ref), starts))
    ]
    for copy in copies:
        copy.start()
    for copy in copies:
        copy.wait()


def write(out, shape, d, half, offset, held, got, other):
    given = [] if out is None else [out]
    return pl.pallas_call(
        functools.partial(write_kernel, d, half, offset),
        out_shape=jax.ShapeDtypeStruct(shape, jnp.float32),
        in_specs=in_vmem(3) + in_hbm(len(given)),
        out_specs=pl.BlockSpec(memory_space=pltpu.HBM),
        scratch_shapes=[pltpu.VMEM(held.shape, jnp.float32), pltpu.SemaphoreType.DMA((2,))],
        input_output_aliases={3: 0} if given else {},
        compiler_params=pltpu.CompilerParams(vmem_limit_bytes=VMEM_LIMIT),
        cost_estimate=pl.CostEstimate(flops=1, bytes_accessed=1, transcendentals=0),
        name="write",
    )(held, got, other, *given)


def split(x):
    high = x.astype(jnp.bfloat16)
    return high, (x - high.astype(jnp.float32)).astype(jnp.bfloat16)


def dot_kernel(count, *refs):
    left, block_ref, outs = refs[: 2 * count], refs[2 * count], refs[2 * count + 1 :]
    rows = left[0].shape[0]
    b_high, b_low = split(block_ref[...])
    for h in range(2):
        for i in range(count):
            a_high, a_low = split(left[h * count + i][...])
            total = None
            for a, b in ((a_high, b_low), (a_low, b_high), (a_high, b_high)):
                term = jnp.dot(a, b, preferred_element_type=jnp.float32)
                total = term if total is None else total + term
            outs[h][i * rows : (i + 1) * rows, :] = total


def products(left, block):
    count = len(left[0])
    shape = (count * left[0][0].shape[0], block.shape[1])
    return kernel_call(functools.partial(dot_kernel, count), [shape] * 2, [*left[0], *left[1], block], "products")


def line_blocks(own, nodes):
    here = lax.axis_index("occ")

    def direct(x, d):
        return lax.ppermute(x, "occ", [(i, i ^ d) for i in range(nodes)])

    if nodes != 4:
        return [(d, own if d == 0 else direct(own, d), 0) for d in range(nodes)]
    centre = lax.ppermute(own, "occ", [(1, 2), (2, 1)])
    near = direct(own, 1)
    far = lax.ppermute(after(own, centre, near), "occ", [(0, 3), (3, 0)])
    middle = (here == 1) | (here == 2)
    last = lax.ppermute(jnp.where(middle, centre, own), "occ", [(1, 0), (2, 3), (0, 2), (3, 1)])
    return [(0, own, 0), (1, near, 0), (3, (middle, centre, far), 0), (2, last, 0)]


def per_device(sizes, amplitudes, amp_mask, integrals, int_mask):
    n_occ, n_vir = sizes
    rows = amplitudes.shape[0]
    groups = n_vir // 2
    own_depth, width = integrals.shape
    depth, half = 2 * own_depth, width // 2

    def swap(x, bits):
        return lax.ppermute(x, "vir", [(i, i ^ bits) for i in range(n_vir)])

    mine, theirs = halves(int_mask, integrals)
    other = swap(theirs, 1)
    parts = cut(after(amp_mask, mine), amplitudes, groups, depth)
    (whole,) = kernel_call(join_kernel, [(depth, half)], [mine, after(other, *parts)], "join")
    blocks = line_blocks(whole, n_occ)
    arrived = [block[2] if isinstance(block, tuple) else block for _, block, _ in blocks]

    rel = [[parts[0]] + [None] * (groups - 1), [None] * groups]
    for r in range(groups - 1, 0, -1):
        rel[0][r] = swap(parts[r], 2 * r)
    for r in range(groups - 1, -1, -1):
        rel[1][r] = swap(rel[0][r] if r else after(parts[0], rel[0][groups - 1]), 1)

    bits = []
    while (1 << len(bits)) < groups:
        bits.append(1 << len(bits))
    orders = [bits, bits[::-1]]
    away = [[r for r in range(groups) if r & o[0]] for o in orders]
    near = [[r for r in range(groups) if not r & o[0]] for o in orders]

    out = None
    token = None
    for n, (d, block, offset) in enumerate(blocks):
        if isinstance(block, tuple):
            middle, centre, far = block
            centre, far = lax.optimization_barrier((centre, far, *sent))[:2]
            block = jnp.where(middle, centre, far)
        if n == 0:
            block = after(block, blocks[1][1], *(blocks[2][1][1:2] if isinstance(blocks[2][1], tuple) else ()))
        else:
            block = after(block, *token)
        sent = products([[rel[h][r] for r in away[h]] for h in range(2)], block)
        moving = [swap(sent[h], 2 * orders[h][0]) for h in range(2)]
        soon = arrived[2:3] if n == 1 else []
        if n == 2:
            moving = list(lax.optimization_barrier((*moving, *arrived[3:4]))[:2])
        held = list(products([[rel[h][r] for r in near[h]] for h in range(2)], after(block, *sent, *soon)))
        names = [near[0], near[1]]
        for level in range(1, len(bits)):
            for h in (1, 0):
                bit = orders[h][level]
                stays = [i for i, r in enumerate(names[h]) if not r & bit]
                goes = [i for i, r in enumerate(names[h]) if r & bit]
                held[h], moved = fold(rows, stays, goes, held[h], moving[h])
                moving[h] = swap(moved, 2 * bit)
                names[h] = [names[h][i] for i in stays]
        token = held if out is None else [*held, out]
        (theirs,) = fold(rows, [0], [], held[1], moving[1])
        out = write(out, (rows, n_occ * width), d, half, offset, held[0], moving[0], swap(theirs, 1))
    return out


def solution(mesh):
    sizes = (mesh.shape["occ"], mesh.shape["vir"])

    def run(*args):
        return per_device(sizes, *args)

    in_specs = (P(("occ", "vir"), None), P(("occ", "vir"), None), P("vir", "occ"), P("vir", "occ"))
    out_specs = P(("occ", "vir"), None)
    return jax.shard_map(run, mesh=mesh, in_specs=in_specs, out_specs=out_specs, check_vma=False)
```

```python
import functools

import jax
import jax.numpy as jnp
from jax import lax
from jax.experimental import pallas as pl
from jax.experimental.pallas import tpu as pltpu
from jax.sharding import PartitionSpec as P

TILE_O = 32
TILE_V = 128
VMEM_LIMIT = 12 * 1024 * 1024


def after(value, *earlier):
    return lax.optimization_barrier((value,) + earlier)[0]


def in_vmem(count):
    return [pl.BlockSpec(memory_space=pltpu.VMEM)] * count


def in_hbm(count):
    return [pl.BlockSpec(memory_space=pltpu.HBM)] * count


def kernel_call(body, outs, operands, name, from_hbm=False, scratch=()):
    space = pltpu.HBM if from_hbm else pltpu.VMEM
    operands = [pltpu.with_memory_space_constraint(x, space) for x in operands]
    return pl.pallas_call(
        body,
        out_shape=[pltpu.VMEM(shape, jnp.float32) for shape in outs],
        in_specs=in_hbm(len(operands)) if from_hbm else in_vmem(len(operands)),
        out_specs=in_vmem(len(outs)),
        scratch_shapes=list(scratch),
        compiler_params=pltpu.CompilerParams(vmem_limit_bytes=VMEM_LIMIT),
        cost_estimate=pl.CostEstimate(flops=1, bytes_accessed=1, transcendentals=0),
        name=name,
    )(*operands)


def tiles(start, count):
    return pl.ds(pl.multiple_of(start * TILE_V, TILE_V), count * TILE_V)


def cut_kernel(groups, depth_tiles, mask_hbm, amp_hbm, *refs):
    out_refs, (mask_ref, amp_ref, mask_sem, amp_sems) = refs[:groups], refs[groups:]
    group = lax.axis_index("vir") // 2
    mask_copy = pltpu.make_async_copy(mask_hbm, mask_ref, mask_sem)
    mask_copy.start()
    starts = [(group ^ r) * depth_tiles for r in range(groups)]
    order = range(groups - 1, -1, -1)
    copies = {
        r: pltpu.make_async_copy(amp_hbm.at[:, tiles(starts[r], depth_tiles)], amp_ref.at[r], amp_sems.at[r]) for r in order
    }
    for r in order:
        copies[r].start()
    mask_copy.wait()
    for r in order:
        copies[r].wait()
        for t in range(depth_tiles):
            for o in range(amp_hbm.shape[0] // TILE_O):
                rows = pl.ds(o * TILE_O, TILE_O)
                scale = mask_ref[o, starts[r] + t].astype(jnp.float32)
                out_refs[r][rows, tiles(t, 1)] = amp_ref[r, rows, tiles(t, 1)] * scale


def cut(mask, amplitudes, groups, depth):
    rows = amplitudes.shape[0]
    scratch = [
        pltpu.SMEM(mask.shape, jnp.int32),
        pltpu.VMEM((groups, rows, depth), jnp.float32),
        pltpu.SemaphoreType.DMA,
        pltpu.SemaphoreType.DMA((groups,)),
    ]
    body = functools.partial(cut_kernel, groups, depth // TILE_V)
    return kernel_call(body, [(rows, depth)] * groups, [mask, amplitudes], "cut", True, scratch)


def halves_kernel(mask_hbm, int_hbm, mine_ref, theirs_ref, mask_ref, int_ref, mask_sem, int_sems):
    low = lax.axis_index("vir") % 2
    count = mine_ref.shape[1] // TILE_V
    mask_copy = pltpu.make_async_copy(mask_hbm, mask_ref, mask_sem)
    mask_copy.start()
    work = ((1 - low, theirs_ref), (low, mine_ref))
    copies = [
        pltpu.make_async_copy(int_hbm.at[:, tiles(half * count, count)], int_ref.at[i], int_sems.at[i])
        for i, (half, _) in enumerate(work)
    ]
    for copy in copies:
        copy.start()
    mask_copy.wait()
    for i, (half, out_ref) in enumerate(work):
        copies[i].wait()
        for t in range(count):
            for k in range(int_hbm.shape[0] // TILE_V):
                scale = mask_ref[k, half * count + t].astype(jnp.float32)
                out_ref[tiles(k, 1), tiles(t, 1)] = int_ref[i, tiles(k, 1), tiles(t, 1)] * scale


def halves(mask, integrals):
    depth, width = integrals.shape
    scratch = [
        pltpu.SMEM(mask.shape, jnp.int32),
        pltpu.VMEM((2, depth, width // 2), jnp.float32),
        pltpu.SemaphoreType.DMA,
        pltpu.SemaphoreType.DMA((2,)),
    ]
    return kernel_call(halves_kernel, [(depth, width // 2)] * 2, [mask, integrals], "halves", True, scratch)


def join_kernel(mine_ref, other_ref, out_ref):
    low = lax.axis_index("vir") % 2
    depth = mine_ref.shape[0]
    out_ref[pl.ds(pl.multiple_of(low * depth, depth), depth), :] = mine_ref[...]
    out_ref[pl.ds(pl.multiple_of((1 - low) * depth, depth), depth), :] = other_ref[...]


def fold_kernel(rows, stays, goes, held_ref, got_ref, *out_refs):
    for out_ref, places in zip(out_refs, (stays, goes)):
        for i, k in enumerate(places):
            take = pl.ds(k * rows, rows)
            out_ref[i * rows : (i + 1) * rows, :] = held_ref[take, :] + got_ref[take, :]


def fold(rows, stays, goes, held, got):
    outs = [(len(places) * rows, held.shape[1]) for places in (stays, goes) if places]
    return kernel_call(functools.partial(fold_kernel, rows, stays, goes), outs, [held, got], "fold")


def write_kernel(d, half, offset, held_ref, got_ref, other_ref, *refs):
    out_ref, piece_ref, sems = refs[-3:]
    low = lax.axis_index("vir") % 2
    place = lax.axis_index("occ") ^ d
    width = held_ref.shape[1] // TILE_V
    starts = [(2 * place + h) * (half // TILE_V) + offset // TILE_V for h in (low, 1 - low)]
    piece_ref[...] = held_ref[...] + got_ref[...]
    copies = [
        pltpu.make_async_copy(source, out_ref.at[:, tiles(start, width)], sems.at[i])
        for i, (source, start) in enumerate(zip((piece_ref, other_ref), starts))
    ]
    for copy in copies:
        copy.start()
    for copy in copies:
        copy.wait()


def write(out, shape, d, half, offset, held, got, other):
    given = [] if out is None else [out]
    return pl.pallas_call(
        functools.partial(write_kernel, d, half, offset),
        out_shape=jax.ShapeDtypeStruct(shape, jnp.float32),
        in_specs=in_vmem(3) + in_hbm(len(given)),
        out_specs=pl.BlockSpec(memory_space=pltpu.HBM),
        scratch_shapes=[pltpu.VMEM(held.shape, jnp.float32), pltpu.SemaphoreType.DMA((2,))],
        input_output_aliases={3: 0} if given else {},
        compiler_params=pltpu.CompilerParams(vmem_limit_bytes=VMEM_LIMIT),
        cost_estimate=pl.CostEstimate(flops=1, bytes_accessed=1, transcendentals=0),
        name="write",
    )(held, got, other, *given)


def split(x):
    high = x.astype(jnp.bfloat16)
    return high, (x - high.astype(jnp.float32)).astype(jnp.bfloat16)


def dot_kernel(count, *refs):
    left, block_ref, outs = refs[: 2 * count], refs[2 * count], refs[2 * count + 1 :]
    rows = left[0].shape[0]
    b_high, b_low = split(block_ref[...])
    for h in range(2):
        for i in range(count):
            a_high, a_low = split(left[h * count + i][...])
            total = None
            for a, b in ((a_high, b_low), (a_low, b_high), (a_high, b_high)):
                term = jnp.dot(a, b, preferred_element_type=jnp.float32)
                total = term if total is None else total + term
            outs[h][i * rows : (i + 1) * rows, :] = total


def products(left, block):
    count = len(left[0])
    shape = (count * left[0][0].shape[0], block.shape[1])
    return kernel_call(functools.partial(dot_kernel, count), [shape] * 2, [*left[0], *left[1], block], "products")


def line_blocks(own, nodes):
    here = lax.axis_index("occ")

    def direct(x, d):
        return lax.ppermute(x, "occ", [(i, i ^ d) for i in range(nodes)])

    if nodes != 4:
        return [(d, own if d == 0 else direct(own, d), 0) for d in range(nodes)]
    centre = lax.ppermute(own, "occ", [(1, 2), (2, 1)])
    near = direct(own, 1)
    far = lax.ppermute(after(own, centre, near), "occ", [(0, 3), (3, 0)])
    middle = (here == 1) | (here == 2)
    last = lax.ppermute(jnp.where(middle, centre, own), "occ", [(1, 0), (2, 3), (0, 2), (3, 1)])
    return [(0, own, 0), (1, near, 0), (3, (middle, centre, far), 0), (2, last, 0)]


def per_device(sizes, amplitudes, amp_mask, integrals, int_mask):
    n_occ, n_vir = sizes
    rows = amplitudes.shape[0]
    groups = n_vir // 2
    own_depth, width = integrals.shape
    depth, half = 2 * own_depth, width // 2

    def swap(x, bits):
        return lax.ppermute(x, "vir", [(i, i ^ bits) for i in range(n_vir)])

    mine, theirs = halves(int_mask, integrals)
    other = swap(theirs, 1)
    parts = cut(after(amp_mask, mine), amplitudes, groups, depth)
    (whole,) = kernel_call(join_kernel, [(depth, half)], [mine, after(other, *parts)], "join")
    blocks = line_blocks(whole, n_occ)

    rel = [[parts[0]] + [None] * (groups - 1), [None] * groups]
    for r in range(groups - 1, 0, -1):
        rel[0][r] = swap(parts[r], 2 * r)
    for r in range(groups - 1, -1, -1):
        rel[1][r] = swap(rel[0][r] if r else after(parts[0], rel[0][groups - 1]), 1)

    bits = []
    while (1 << len(bits)) < groups:
        bits.append(1 << len(bits))
    orders = [bits, bits[::-1]]
    away = [[r for r in range(groups) if r & o[0]] for o in orders]
    near = [[r for r in range(groups) if not r & o[0]] for o in orders]

    out = None
    token = None
    settled = []
    for n, (d, block, offset) in enumerate(blocks):
        if isinstance(block, tuple):
            middle, centre, far = block
            centre, far = lax.optimization_barrier((centre, far, *sent))[:2]
            block = jnp.where(middle, centre, far)
        if n > 0:
            block = after(block, *token)
        sent = products([[rel[h][r] for r in away[h]] for h in range(2)], block)
        moving = [swap(sent[h], 2 * orders[h][0]) for h in range(2)]
        held = list(products([[rel[h][r] for r in near[h]] for h in range(2)], after(block, *sent, *settled)))
        names = [near[0], near[1]]
        for level in range(1, len(bits)):
            for h in (1, 0):
                bit = orders[h][level]
                stays = [i for i, r in enumerate(names[h]) if not r & bit]
                goes = [i for i, r in enumerate(names[h]) if r & bit]
                held[h], moved = fold(rows, stays, goes, held[h], moving[h])
                moving[h] = swap(moved, 2 * bit)
                names[h] = [names[h][i] for i in stays]
        token = held if out is None else [*held, out]
        settled = moving
        (theirs,) = fold(rows, [0], [], held[1], moving[1])
        out = write(out, (rows, n_occ * width), d, half, offset, held[0], moving[0], swap(theirs, 1))
    return out


def solution(mesh):
    sizes = (mesh.shape["occ"], mesh.shape["vir"])

    def run(*args):
        return per_device(sizes, *args)

    in_specs = (P(("occ", "vir"), None), P(("occ", "vir"), None), P("vir", "occ"), P("vir", "occ"))
    out_specs = P(("occ", "vir"), None)
    return jax.shard_map(run, mesh=mesh, in_specs=in_specs, out_specs=out_specs, check_vma=False)
```

```python
import functools

import jax
import jax.numpy as jnp
from jax import lax
from jax.experimental import pallas as pl
from jax.experimental.pallas import tpu as pltpu
from jax.sharding import PartitionSpec as P

TILE_O = 32
TILE_V = 128
VMEM_LIMIT = 6 * 1024 * 1024


def after(value, *earlier):
    return lax.optimization_barrier((value,) + earlier)[0]


def in_vmem(count):
    return [pl.BlockSpec(memory_space=pltpu.VMEM)] * count


def in_hbm(count):
    return [pl.BlockSpec(memory_space=pltpu.HBM)] * count


def kernel_call(body, outs, operands, name, from_hbm=False, scratch=()):
    space = pltpu.HBM if from_hbm else pltpu.VMEM
    operands = [pltpu.with_memory_space_constraint(x, space) for x in operands]
    return pl.pallas_call(
        body,
        out_shape=[pltpu.VMEM(shape, jnp.float32) for shape in outs],
        in_specs=in_hbm(len(operands)) if from_hbm else in_vmem(len(operands)),
        out_specs=in_vmem(len(outs)),
        scratch_shapes=list(scratch),
        compiler_params=pltpu.CompilerParams(vmem_limit_bytes=VMEM_LIMIT),
        cost_estimate=pl.CostEstimate(flops=1, bytes_accessed=1, transcendentals=0),
        name=name,
    )(*operands)


def tiles(start, count):
    return pl.ds(pl.multiple_of(start * TILE_V, TILE_V), count * TILE_V)


def cut_kernel(groups, depth_tiles, mask_hbm, amp_hbm, *refs):
    out_refs, (mask_ref, amp_ref, mask_sem, amp_sems) = refs[:groups], refs[groups:]
    group = lax.axis_index("vir") // 2
    mask_copy = pltpu.make_async_copy(mask_hbm, mask_ref, mask_sem)
    mask_copy.start()
    starts = [(group ^ r) * depth_tiles for r in range(groups)]
    order = range(groups - 1, -1, -1)
    copies = {
        r: pltpu.make_async_copy(amp_hbm.at[:, tiles(starts[r], depth_tiles)], amp_ref.at[r], amp_sems.at[r]) for r in order
    }
    for r in order:
        copies[r].start()
    mask_copy.wait()
    for r in order:
        copies[r].wait()
        for t in range(depth_tiles):
            for o in range(amp_hbm.shape[0] // TILE_O):
                rows = pl.ds(o * TILE_O, TILE_O)
                scale = mask_ref[o, starts[r] + t].astype(jnp.float32)
                out_refs[r][rows, tiles(t, 1)] = amp_ref[r, rows, tiles(t, 1)] * scale


def cut(mask, amplitudes, groups, depth):
    rows = amplitudes.shape[0]
    scratch = [
        pltpu.SMEM(mask.shape, jnp.int32),
        pltpu.VMEM((groups, rows, depth), jnp.float32),
        pltpu.SemaphoreType.DMA,
        pltpu.SemaphoreType.DMA((groups,)),
    ]
    body = functools.partial(cut_kernel, groups, depth // TILE_V)
    return kernel_call(body, [(rows, depth)] * groups, [mask, amplitudes], "cut", True, scratch)


def halves_kernel(mask_hbm, int_hbm, mine_ref, theirs_ref, mask_ref, int_ref, mask_sem, int_sems):
    low = lax.axis_index("vir") % 2
    count = mine_ref.shape[1] // TILE_V
    mask_copy = pltpu.make_async_copy(mask_hbm, mask_ref, mask_sem)
    mask_copy.start()
    work = ((1 - low, theirs_ref), (low, mine_ref))
    copies = [
        pltpu.make_async_copy(int_hbm.at[:, tiles(half * count, count)], int_ref.at[i], int_sems.at[i])
        for i, (half, _) in enumerate(work)
    ]
    for copy in copies:
        copy.start()
    mask_copy.wait()
    for i, (half, out_ref) in enumerate(work):
        copies[i].wait()
        for t in range(count):
            for k in range(int_hbm.shape[0] // TILE_V):
                scale = mask_ref[k, half * count + t].astype(jnp.float32)
                out_ref[tiles(k, 1), tiles(t, 1)] = int_ref[i, tiles(k, 1), tiles(t, 1)] * scale


def halves(mask, integrals):
    depth, width = integrals.shape
    scratch = [
        pltpu.SMEM(mask.shape, jnp.int32),
        pltpu.VMEM((2, depth, width // 2), jnp.float32),
        pltpu.SemaphoreType.DMA,
        pltpu.SemaphoreType.DMA((2,)),
    ]
    return kernel_call(halves_kernel, [(depth, width // 2)] * 2, [mask, integrals], "halves", True, scratch)


def join_kernel(mine_ref, other_ref, out_ref):
    low = lax.axis_index("vir") % 2
    depth = mine_ref.shape[0]
    out_ref[pl.ds(pl.multiple_of(low * depth, depth), depth), :] = mine_ref[...]
    out_ref[pl.ds(pl.multiple_of((1 - low) * depth, depth), depth), :] = other_ref[...]


def fold_kernel(rows, stays, goes, held_ref, got_ref, *out_refs):
    for out_ref, places in zip(out_refs, (stays, goes)):
        for i, k in enumerate(places):
            take = pl.ds(k * rows, rows)
            out_ref[i * rows : (i + 1) * rows, :] = held_ref[take, :] + got_ref[take, :]


def fold(rows, stays, goes, held, got):
    outs = [(len(places) * rows, held.shape[1]) for places in (stays, goes) if places]
    return kernel_call(functools.partial(fold_kernel, rows, stays, goes), outs, [held, got], "fold")


def write_kernel(d, half, offset, held_ref, got_ref, other_ref, *refs):
    out_ref, piece_ref, sems = refs[-3:]
    low = lax.axis_index("vir") % 2
    place = lax.axis_index("occ") ^ d
    width = held_ref.shape[1] // TILE_V
    starts = [(2 * place + h) * (half // TILE_V) + offset // TILE_V for h in (low, 1 - low)]
    piece_ref[...] = held_ref[...] + got_ref[...]
    copies = [
        pltpu.make_async_copy(source, out_ref.at[:, tiles(start, width)], sems.at[i])
        for i, (source, start) in enumerate(zip((piece_ref, other_ref), starts))
    ]
    for copy in copies:
        copy.start()
    for copy in copies:
        copy.wait()


def write(out, shape, d, half, offset, held, got, other):
    given = [] if out is None else [out]
    return pl.pallas_call(
        functools.partial(write_kernel, d, half, offset),
        out_shape=jax.ShapeDtypeStruct(shape, jnp.float32),
        in_specs=in_vmem(3) + in_hbm(len(given)),
        out_specs=pl.BlockSpec(memory_space=pltpu.HBM),
        scratch_shapes=[pltpu.VMEM(held.shape, jnp.float32), pltpu.SemaphoreType.DMA((2,))],
        input_output_aliases={3: 0} if given else {},
        compiler_params=pltpu.CompilerParams(vmem_limit_bytes=VMEM_LIMIT),
        cost_estimate=pl.CostEstimate(flops=1, bytes_accessed=1, transcendentals=0),
        name="write",
    )(held, got, other, *given)


def split(x):
    high = x.astype(jnp.bfloat16)
    return high, (x - high.astype(jnp.float32)).astype(jnp.bfloat16)


def dot_kernel(count, *refs):
    left, block_ref, outs = refs[: 2 * count], refs[2 * count], refs[2 * count + 1 :]
    rows = left[0].shape[0]
    b_high, b_low = split(block_ref[...])
    for h in range(2):
        for i in range(count):
            a_high, a_low = split(left[h * count + i][...])
            total = None
            for a, b in ((a_high, b_low), (a_low, b_high), (a_high, b_high)):
                term = jnp.dot(a, b, preferred_element_type=jnp.float32)
                total = term if total is None else total + term
            outs[h][i * rows : (i + 1) * rows, :] = total


def products(left, block):
    count = len(left[0])
    shape = (count * left[0][0].shape[0], block.shape[1])
    return kernel_call(functools.partial(dot_kernel, count), [shape] * 2, [*left[0], *left[1], block], "products")


def line_blocks(own, nodes):
    def direct(x, d):
        return lax.ppermute(x, "occ", [(i, i ^ d) for i in range(nodes)])

    if nodes != 4:
        return [(d, own if d == 0 else direct(own, d)) for d in range(nodes)]
    centre = lax.ppermute(own, "occ", [(1, 2), (2, 1)])
    near = direct(own, 1)
    return [(0, own), (1, near), (3, centre), (2, None)]


def far_blocks(own, near, centre):
    far = lax.ppermute(after(own, centre, near), "occ", [(0, 3), (3, 0)])
    here = lax.axis_index("occ")
    middle = (here == 1) | (here == 2)
    last = lax.ppermute(jnp.where(middle, centre, own), "occ", [(1, 0), (2, 3), (0, 2), (3, 1)])
    return (middle, centre, far), last


def per_device(sizes, amplitudes, amp_mask, integrals, int_mask):
    n_occ, n_vir = sizes
    rows = amplitudes.shape[0]
    groups = n_vir // 2
    own_depth, width = integrals.shape
    depth, half = 2 * own_depth, width // 2

    def swap(x, bits):
        return lax.ppermute(x, "vir", [(i, i ^ bits) for i in range(n_vir)])

    mine, theirs = halves(int_mask, integrals)
    other = swap(theirs, 1)
    parts = cut(after(amp_mask, mine), amplitudes, groups, depth)
    (whole,) = kernel_call(join_kernel, [(depth, half)], [mine, after(other, *parts)], "join")
    blocks = line_blocks(whole, n_occ)

    rel = [[parts[0]] + [None] * (groups - 1), [None] * groups]
    for r in range(groups - 1, 0, -1):
        rel[0][r] = swap(parts[r], 2 * r)
    for r in range(groups - 1, -1, -1):
        rel[1][r] = swap(rel[0][r] if r else after(parts[0], rel[0][groups - 1]), 1)

    bits = []
    while (1 << len(bits)) < groups:
        bits.append(1 << len(bits))
    orders = [bits, bits[::-1]]
    away = [[r for r in range(groups) if r & o[0]] for o in orders]
    near = [[r for r in range(groups) if not r & o[0]] for o in orders]

    out = None
    token = settled = []
    for n in range(n_occ):
        d, block = blocks[n]
        if isinstance(block, tuple):
            middle, centre, far = block
            centre, far = lax.optimization_barrier((centre, far, *token))[:2]
            block = jnp.where(middle, centre, far)
        elif n > 0:
            block = after(block, *token)
        sent = products([[rel[h][r] for r in away[h]] for h in range(2)], block)
        moving = [swap(sent[h], 2 * orders[h][0]) for h in range(2)]
        if n == 0 and blocks[-1][1] is None:
            first, second = lax.optimization_barrier((blocks[1][1], blocks[2][1], *sent))[:2]
            passed = far_blocks(block, first, second)
            blocks[1:] = [(1, first), (3, passed[0]), (2, passed[1])]
        held = list(products([[rel[h][r] for r in near[h]] for h in range(2)], after(block, *sent, *settled)))
        names = [near[0], near[1]]
        for level in range(1, len(bits)):
            for h in (1, 0):
                bit = orders[h][level]
                stays = [i for i, r in enumerate(names[h]) if not r & bit]
                goes = [i for i, r in enumerate(names[h]) if r & bit]
                held[h], moved = fold(rows, stays, goes, held[h], moving[h])
                moving[h] = swap(moved, 2 * bit)
                names[h] = [names[h][i] for i in stays]
        token = held if n == 0 else [*moving, out]
        settled = moving if n == 0 else []
        (theirs,) = fold(rows, [0], [], held[1], moving[1])
        out = write(out, (rows, n_occ * width), d, half, 0, held[0], moving[0], swap(theirs, 1))
    return out


def solution(mesh):
    sizes = (mesh.shape["occ"], mesh.shape["vir"])

    def run(*args):
        return per_device(sizes, *args)

    in_specs = (P(("occ", "vir"), None), P(("occ", "vir"), None), P("vir", "occ"), P("vir", "occ"))
    out_specs = P(("occ", "vir"), None)
    return jax.shard_map(run, mesh=mesh, in_specs=in_specs, out_specs=out_specs, check_vma=False)
```

```python
import functools

import jax
import jax.numpy as jnp
from jax import lax
from jax.experimental import pallas as pl
from jax.experimental.pallas import tpu as pltpu
from jax.sharding import PartitionSpec as P

TILE_O = 32
TILE_V = 128
VMEM_LIMIT = 6 * 1024 * 1024


def after(value, *earlier):
    return lax.optimization_barrier((value,) + earlier)[0]


def in_vmem(count):
    return [pl.BlockSpec(memory_space=pltpu.VMEM)] * count


def in_hbm(count):
    return [pl.BlockSpec(memory_space=pltpu.HBM)] * count


def kernel_call(body, outs, operands, name, from_hbm=False, scratch=()):
    space = pltpu.HBM if from_hbm else pltpu.VMEM
    operands = [pltpu.with_memory_space_constraint(x, space) for x in operands]
    return pl.pallas_call(
        body,
        out_shape=[pltpu.VMEM(shape, jnp.float32) for shape in outs],
        in_specs=in_hbm(len(operands)) if from_hbm else in_vmem(len(operands)),
        out_specs=in_vmem(len(outs)),
        scratch_shapes=list(scratch),
        compiler_params=pltpu.CompilerParams(vmem_limit_bytes=VMEM_LIMIT),
        cost_estimate=pl.CostEstimate(flops=1, bytes_accessed=1, transcendentals=0),
        name=name,
    )(*operands)


def tiles(start, count):
    return pl.ds(pl.multiple_of(start * TILE_V, TILE_V), count * TILE_V)


def cut_kernel(groups, depth_tiles, mask_hbm, amp_hbm, *refs):
    out_refs, (mask_ref, amp_ref, mask_sem, amp_sems) = refs[:groups], refs[groups:]
    group = lax.axis_index("vir") // 2
    mask_copy = pltpu.make_async_copy(mask_hbm, mask_ref, mask_sem)
    mask_copy.start()
    starts = [(group ^ r) * depth_tiles for r in range(groups)]
    order = range(groups - 1, -1, -1)
    copies = {
        r: pltpu.make_async_copy(amp_hbm.at[:, tiles(starts[r], depth_tiles)], amp_ref.at[r], amp_sems.at[r]) for r in order
    }
    for r in order:
        copies[r].start()
    mask_copy.wait()
    for r in order:
        copies[r].wait()
        for t in range(depth_tiles):
            for o in range(amp_hbm.shape[0] // TILE_O):
                rows = pl.ds(o * TILE_O, TILE_O)
                scale = mask_ref[o, starts[r] + t].astype(jnp.float32)
                out_refs[r][rows, tiles(t, 1)] = amp_ref[r, rows, tiles(t, 1)] * scale


def cut(mask, amplitudes, groups, depth):
    rows = amplitudes.shape[0]
    scratch = [
        pltpu.SMEM(mask.shape, jnp.int32),
        pltpu.VMEM((groups, rows, depth), jnp.float32),
        pltpu.SemaphoreType.DMA,
        pltpu.SemaphoreType.DMA((groups,)),
    ]
    body = functools.partial(cut_kernel, groups, depth // TILE_V)
    return kernel_call(body, [(rows, depth)] * groups, [mask, amplitudes], "cut", True, scratch)


def halves_kernel(mask_hbm, int_hbm, mine_ref, theirs_ref, mask_ref, int_ref, mask_sem, int_sems):
    low = lax.axis_index("vir") % 2
    count = mine_ref.shape[1] // TILE_V
    mask_copy = pltpu.make_async_copy(mask_hbm, mask_ref, mask_sem)
    mask_copy.start()
    work = ((1 - low, theirs_ref), (low, mine_ref))
    copies = [
        pltpu.make_async_copy(int_hbm.at[:, tiles(half * count, count)], int_ref.at[i], int_sems.at[i])
        for i, (half, _) in enumerate(work)
    ]
    for copy in copies:
        copy.start()
    mask_copy.wait()
    for i, (half, out_ref) in enumerate(work):
        copies[i].wait()
        for t in range(count):
            for k in range(int_hbm.shape[0] // TILE_V):
                scale = mask_ref[k, half * count + t].astype(jnp.float32)
                out_ref[tiles(k, 1), tiles(t, 1)] = int_ref[i, tiles(k, 1), tiles(t, 1)] * scale


def halves(mask, integrals):
    depth, width = integrals.shape
    scratch = [
        pltpu.SMEM(mask.shape, jnp.int32),
        pltpu.VMEM((2, depth, width // 2), jnp.float32),
        pltpu.SemaphoreType.DMA,
        pltpu.SemaphoreType.DMA((2,)),
    ]
    return kernel_call(halves_kernel, [(depth, width // 2)] * 2, [mask, integrals], "halves", True, scratch)


def join_kernel(mine_ref, other_ref, out_ref):
    low = lax.axis_index("vir") % 2
    depth = mine_ref.shape[0]
    out_ref[pl.ds(pl.multiple_of(low * depth, depth), depth), :] = mine_ref[...]
    out_ref[pl.ds(pl.multiple_of((1 - low) * depth, depth), depth), :] = other_ref[...]


def fold_kernel(rows, stays, goes, held_ref, got_ref, *out_refs):
    for out_ref, places in zip(out_refs, (stays, goes)):
        for i, k in enumerate(places):
            take = pl.ds(k * rows, rows)
            out_ref[i * rows : (i + 1) * rows, :] = held_ref[take, :] + got_ref[take, :]


def fold(rows, stays, goes, held, got):
    outs = [(len(places) * rows, held.shape[1]) for places in (stays, goes) if places]
    return kernel_call(functools.partial(fold_kernel, rows, stays, goes), outs, [held, got], "fold")


def write_kernel(ds, half, mine_a, mine_b, other_a, other_b, *refs):
    out_ref, piece_ref, sems = refs[-3:]
    low = lax.axis_index("vir") % 2
    here = lax.axis_index("occ")
    piece_ref[0] = mine_a[...] + mine_b[...]
    piece_ref[1] = other_a[...] + other_b[...]
    copies = []
    for k, d in enumerate(ds):
        for i, h in enumerate((low, 1 - low)):
            start = (2 * (here ^ d) + h) * (half // TILE_V)
            source = piece_ref.at[i, :, pl.ds(k * half, half)]
            copies.append(pltpu.make_async_copy(source, out_ref.at[:, tiles(start, half // TILE_V)], sems.at[2 * k + i]))
    for copy in copies:
        copy.start()
    for copy in copies:
        copy.wait()


def write(out, shape, ds, half, pieces):
    given = [] if out is None else [out]
    pieces = [pltpu.with_memory_space_constraint(x, pltpu.VMEM) for x in pieces]
    return pl.pallas_call(
        functools.partial(write_kernel, ds, half),
        out_shape=jax.ShapeDtypeStruct(shape, jnp.float32),
        in_specs=in_vmem(4) + in_hbm(len(given)),
        out_specs=pl.BlockSpec(memory_space=pltpu.HBM),
        scratch_shapes=[pltpu.VMEM((2, *pieces[0].shape), jnp.float32), pltpu.SemaphoreType.DMA((2 * len(ds),))],
        input_output_aliases={4: 0} if given else {},
        compiler_params=pltpu.CompilerParams(vmem_limit_bytes=VMEM_LIMIT),
        cost_estimate=pl.CostEstimate(flops=1, bytes_accessed=1, transcendentals=0),
        name="write",
    )(*pieces, *given)


def split(x):
    high = x.astype(jnp.bfloat16)
    return high, (x - high.astype(jnp.float32)).astype(jnp.bfloat16)


def dot_kernel(count, blocks, *refs):
    left, right, outs = refs[: 2 * count], refs[2 * count : 2 * count + blocks], refs[2 * count + blocks :]
    rows, width = left[0].shape[0], right[0].shape[1]
    for k in range(blocks):
        b_high, b_low = split(right[k][...])
        for h in range(2):
            for i in range(count):
                a_high, a_low = split(left[h * count + i][...])
                total = None
                for a, b in ((a_high, b_low), (a_low, b_high), (a_high, b_high)):
                    term = jnp.dot(a, b, preferred_element_type=jnp.float32)
                    total = term if total is None else total + term
                outs[h][i * rows : (i + 1) * rows, k * width : (k + 1) * width] = total


def products(left, right):
    count = len(left[0])
    shape = (count * left[0][0].shape[0], len(right) * right[0].shape[1])
    return kernel_call(functools.partial(dot_kernel, count, len(right)), [shape] * 2, [*left[0], *left[1], *right], "products")


def line_stages(own, nodes):
    def direct(x, d):
        return lax.ppermute(x, "occ", [(i, i ^ d) for i in range(nodes)])

    if nodes != 4:
        return [[(d, own if d == 0 else direct(own, d))] for d in range(nodes)]
    centre = lax.ppermute(own, "occ", [(1, 2), (2, 1)])
    near = direct(own, 1)
    far = lax.ppermute(after(own, centre, near), "occ", [(0, 3), (3, 0)])
    here = lax.axis_index("occ")
    middle = (here == 1) | (here == 2)

    def last(*earlier):
        moving = jnp.where(middle, after(centre, *earlier), own)
        return [(2, lax.ppermute(moving, "occ", [(1, 0), (2, 3), (0, 2), (3, 1)]))]

    return [[(0, own), (1, near)], [(3, (middle, centre, far))], last]


def per_device(sizes, amplitudes, amp_mask, integrals, int_mask):
    n_occ, n_vir = sizes
    rows = amplitudes.shape[0]
    groups = n_vir // 2
    own_depth, width = integrals.shape
    depth, half = 2 * own_depth, width // 2

    def swap(x, bits):
        return lax.ppermute(x, "vir", [(i, i ^ bits) for i in range(n_vir)])

    mine, theirs = halves(int_mask, integrals)
    other = swap(theirs, 1)
    parts = cut(after(amp_mask, mine), amplitudes, groups, depth)
    (whole,) = kernel_call(join_kernel, [(depth, half)], [mine, after(other, *parts)], "join")
    stages = line_stages(whole, n_occ)

    rel = [[parts[0]] + [None] * (groups - 1), [None] * groups]
    for r in range(groups - 1, 0, -1):
        rel[0][r] = swap(parts[r], 2 * r)
    for r in range(groups - 1, -1, -1):
        rel[1][r] = swap(rel[0][r] if r else after(parts[0], rel[0][groups - 1]), 1)

    bits = []
    while (1 << len(bits)) < groups:
        bits.append(1 << len(bits))
    orders = [bits, bits[::-1]]
    away = [[r for r in range(groups) if r & o[0]] for o in orders]
    near = [[r for r in range(groups) if not r & o[0]] for o in orders]

    out = None
    token = []
    for n in range(len(stages)):
        ds, right = [d for d, _ in stages[n]], [block for _, block in stages[n]]
        if isinstance(right[0], tuple):
            middle, centre, far = right[0]
            centre, far = lax.optimization_barrier((centre, far, *sent))[:2]
            right = [jnp.where(middle, centre, far)]
        right = list(lax.optimization_barrier((*right, *token))[: len(right)])
        sent = products([[rel[h][r] for r in away[h]] for h in range(2)], right)
        moving = [swap(sent[h], 2 * orders[h][0]) for h in range(2)]
        if callable(stages[-1]):
            stages[-1] = stages[-1](*moving)
        right[0] = after(right[0], *sent)
        held = list(products([[rel[h][r] for r in near[h]] for h in range(2)], right))
        names = [near[0], near[1]]
        for level in range(1, len(bits)):
            for h in (1, 0):
                bit = orders[h][level]
                stays = [i for i, r in enumerate(names[h]) if not r & bit]
                goes = [i for i, r in enumerate(names[h]) if r & bit]
                held[h], moved = fold(rows, stays, goes, held[h], moving[h])
                moving[h] = swap(moved, 2 * bit + (h if level == len(bits) - 1 else 0))
                names[h] = [names[h][i] for i in stays]
        pieces = [held[0], moving[0], swap(held[1], 1), moving[1]]
        token = [*pieces[1:]] if out is None else [*pieces[1:], out]
        out = write(out, (rows, n_occ * width), ds, half, pieces)
    return out


def solution(mesh):
    sizes = (mesh.shape["occ"], mesh.shape["vir"])

    def run(*args):
        return per_device(sizes, *args)

    in_specs = (P(("occ", "vir"), None), P(("occ", "vir"), None), P("vir", "occ"), P("vir", "occ"))
    out_specs = P(("occ", "vir"), None)
    return jax.shard_map(run, mesh=mesh, in_specs=in_specs, out_specs=out_specs, check_vma=False)
```

```python
import functools

import jax
import jax.numpy as jnp
from jax import lax
from jax.experimental import pallas as pl
from jax.experimental.pallas import tpu as pltpu
from jax.sharding import PartitionSpec as P

TILE_O = 32
TILE_V = 128
VMEM_LIMIT = 6 * 1024 * 1024


def after(value, *earlier):
    return lax.optimization_barrier((value,) + earlier)[0]


def in_vmem(count):
    return [pl.BlockSpec(memory_space=pltpu.VMEM)] * count


def in_hbm(count):
    return [pl.BlockSpec(memory_space=pltpu.HBM)] * count


def kernel_call(body, outs, operands, name, from_hbm=False, scratch=()):
    space = pltpu.HBM if from_hbm else pltpu.VMEM
    operands = [pltpu.with_memory_space_constraint(x, space) for x in operands]
    return pl.pallas_call(
        body,
        out_shape=[pltpu.VMEM(shape, jnp.float32) for shape in outs],
        in_specs=in_hbm(len(operands)) if from_hbm else in_vmem(len(operands)),
        out_specs=in_vmem(len(outs)),
        scratch_shapes=list(scratch),
        compiler_params=pltpu.CompilerParams(vmem_limit_bytes=VMEM_LIMIT),
        cost_estimate=pl.CostEstimate(flops=1, bytes_accessed=1, transcendentals=0),
        name=name,
    )(*operands)


def tiles(start, count):
    return pl.ds(pl.multiple_of(start * TILE_V, TILE_V), count * TILE_V)


def cut_kernel(groups, depth_tiles, mask_hbm, amp_hbm, *refs):
    out_refs, (mask_ref, amp_ref, mask_sem, amp_sems) = refs[:groups], refs[groups:]
    group = lax.axis_index("vir") // 2
    mask_copy = pltpu.make_async_copy(mask_hbm, mask_ref, mask_sem)
    mask_copy.start()
    starts = [(group ^ r) * depth_tiles for r in range(groups)]
    order = range(groups - 1, -1, -1)
    copies = {
        r: pltpu.make_async_copy(amp_hbm.at[:, tiles(starts[r], depth_tiles)], amp_ref.at[r], amp_sems.at[r]) for r in order
    }
    for r in order:
        copies[r].start()
    mask_copy.wait()
    for r in order:
        copies[r].wait()
        for t in range(depth_tiles):
            for o in range(amp_hbm.shape[0] // TILE_O):
                rows = pl.ds(o * TILE_O, TILE_O)
                scale = mask_ref[o, starts[r] + t].astype(jnp.float32)
                out_refs[r][rows, tiles(t, 1)] = amp_ref[r, rows, tiles(t, 1)] * scale


def cut(mask, amplitudes, groups, depth):
    rows = amplitudes.shape[0]
    scratch = [
        pltpu.SMEM(mask.shape, jnp.int32),
        pltpu.VMEM((groups, rows, depth), jnp.float32),
        pltpu.SemaphoreType.DMA,
        pltpu.SemaphoreType.DMA((groups,)),
    ]
    body = functools.partial(cut_kernel, groups, depth // TILE_V)
    return kernel_call(body, [(rows, depth)] * groups, [mask, amplitudes], "cut", True, scratch)


def halves_kernel(mask_hbm, int_hbm, mine_ref, theirs_ref, mask_ref, int_ref, mask_sem, int_sems):
    low = lax.axis_index("vir") % 2
    count = mine_ref.shape[1] // TILE_V
    mask_copy = pltpu.make_async_copy(mask_hbm, mask_ref, mask_sem)
    mask_copy.start()
    work = ((1 - low, theirs_ref), (low, mine_ref))
    copies = [
        pltpu.make_async_copy(int_hbm.at[:, tiles(half * count, count)], int_ref.at[i], int_sems.at[i])
        for i, (half, _) in enumerate(work)
    ]
    for copy in copies:
        copy.start()
    mask_copy.wait()
    for i, (half, out_ref) in enumerate(work):
        copies[i].wait()
        for t in range(count):
            for k in range(int_hbm.shape[0] // TILE_V):
                scale = mask_ref[k, half * count + t].astype(jnp.float32)
                out_ref[tiles(k, 1), tiles(t, 1)] = int_ref[i, tiles(k, 1), tiles(t, 1)] * scale


def halves(mask, integrals):
    depth, width = integrals.shape
    scratch = [
        pltpu.SMEM(mask.shape, jnp.int32),
        pltpu.VMEM((2, depth, width // 2), jnp.float32),
        pltpu.SemaphoreType.DMA,
        pltpu.SemaphoreType.DMA((2,)),
    ]
    return kernel_call(halves_kernel, [(depth, width // 2)] * 2, [mask, integrals], "halves", True, scratch)


def join_kernel(mine_ref, other_ref, out_ref):
    low = lax.axis_index("vir") % 2
    depth = mine_ref.shape[0]
    out_ref[pl.ds(pl.multiple_of(low * depth, depth), depth), :] = mine_ref[...]
    out_ref[pl.ds(pl.multiple_of((1 - low) * depth, depth), depth), :] = other_ref[...]


def fold_kernel(rows, stays, goes, held_ref, got_ref, *out_refs):
    for out_ref, places in zip(out_refs, (stays, goes)):
        for i, k in enumerate(places):
            take = pl.ds(k * rows, rows)
            out_ref[i * rows : (i + 1) * rows, :] = held_ref[take, :] + got_ref[take, :]


def fold(rows, stays, goes, held, got):
    outs = [(len(places) * rows, held.shape[1]) for places in (stays, goes) if places]
    return kernel_call(functools.partial(fold_kernel, rows, stays, goes), outs, [held, got], "fold")


def write_kernel(ds, half, mine_a, mine_b, other_a, other_b, *refs):
    out_ref, piece_ref, sems = refs[-3:]
    low = lax.axis_index("vir") % 2
    here = lax.axis_index("occ")
    piece_ref[0] = mine_a[...] + mine_b[...]
    piece_ref[1] = other_a[...] + other_b[...]
    copies = []
    for k, d in enumerate(ds):
        for i, h in enumerate((low, 1 - low)):
            start = (2 * (here ^ d) + h) * (half // TILE_V)
            source = piece_ref.at[i, :, pl.ds(k * half, half)]
            copies.append(pltpu.make_async_copy(source, out_ref.at[:, tiles(start, half // TILE_V)], sems.at[2 * k + i]))
    for copy in copies:
        copy.start()
    for copy in copies:
        copy.wait()


def write(out, shape, ds, half, pieces):
    given = [] if out is None else [out]
    pieces = [pltpu.with_memory_space_constraint(x, pltpu.VMEM) for x in pieces]
    return pl.pallas_call(
        functools.partial(write_kernel, ds, half),
        out_shape=jax.ShapeDtypeStruct(shape, jnp.float32),
        in_specs=in_vmem(4) + in_hbm(len(given)),
        out_specs=pl.BlockSpec(memory_space=pltpu.HBM),
        scratch_shapes=[pltpu.VMEM((2, *pieces[0].shape), jnp.float32), pltpu.SemaphoreType.DMA((2 * len(ds),))],
        input_output_aliases={4: 0} if given else {},
        compiler_params=pltpu.CompilerParams(vmem_limit_bytes=VMEM_LIMIT),
        cost_estimate=pl.CostEstimate(flops=1, bytes_accessed=1, transcendentals=0),
        name="write",
    )(*pieces, *given)


def split(x):
    high = x.astype(jnp.bfloat16)
    return high, (x - high.astype(jnp.float32)).astype(jnp.bfloat16)


def dot_kernel(count, blocks, *refs):
    left, right, outs = refs[: 2 * count], refs[2 * count : 2 * count + blocks], refs[2 * count + blocks :]
    rows, width = left[0].shape[0], right[0].shape[1]
    for k in range(blocks):
        b_high, b_low = split(right[k][...])
        for h in range(2):
            for i in range(count):
                a_high, a_low = split(left[h * count + i][...])
                total = None
                for a, b in ((a_high, b_low), (a_low, b_high), (a_high, b_high)):
                    term = jnp.dot(a, b, preferred_element_type=jnp.float32)
                    total = term if total is None else total + term
                outs[h][i * rows : (i + 1) * rows, k * width : (k + 1) * width] = total


def products(left, right):
    count = len(left[0])
    shape = (count * left[0][0].shape[0], len(right) * right[0].shape[1])
    return kernel_call(functools.partial(dot_kernel, count, len(right)), [shape] * 2, [*left[0], *left[1], *right], "products")


def line_stages(own, nodes):
    def direct(x, d):
        return lax.ppermute(x, "occ", [(i, i ^ d) for i in range(nodes)])

    if nodes != 4:
        return [[(d, own if d == 0 else direct(own, d))] for d in range(nodes)]
    centre = lax.ppermute(own, "occ", [(1, 2), (2, 1)])
    near = direct(own, 1)
    far = lax.ppermute(after(own, centre, near), "occ", [(0, 3), (3, 0)])
    here = lax.axis_index("occ")
    middle = (here == 1) | (here == 2)

    def last(*earlier):
        moving = jnp.where(middle, after(centre, *earlier), own)
        return [(2, lax.ppermute(moving, "occ", [(1, 0), (2, 3), (0, 2), (3, 1)]))]

    return [[(0, own)], [(1, near)], [(3, (middle, centre, far))], last]


def per_device(sizes, amplitudes, amp_mask, integrals, int_mask):
    n_occ, n_vir = sizes
    rows = amplitudes.shape[0]
    groups = n_vir // 2
    own_depth, width = integrals.shape
    depth, half = 2 * own_depth, width // 2

    def swap(x, bits):
        return lax.ppermute(x, "vir", [(i, i ^ bits) for i in range(n_vir)])

    mine, theirs = halves(int_mask, integrals)
    other = swap(theirs, 1)
    parts = cut(after(amp_mask, mine), amplitudes, groups, depth)
    (whole,) = kernel_call(join_kernel, [(depth, half)], [mine, after(other, *parts)], "join")
    stages = line_stages(whole, n_occ)

    rel = [[parts[0]] + [None] * (groups - 1), [None] * groups]
    for r in range(groups - 1, 0, -1):
        rel[0][r] = swap(parts[r], 2 * r)
    for r in range(groups - 1, -1, -1):
        rel[1][r] = swap(rel[0][r] if r else after(parts[0], rel[0][groups - 1]), 1)

    bits = []
    while (1 << len(bits)) < groups:
        bits.append(1 << len(bits))
    orders = [bits, bits[::-1]]
    away = [[r for r in range(groups) if r & o[0]] for o in orders]
    near = [[r for r in range(groups) if not r & o[0]] for o in orders]

    out = None
    token = []
    for n in range(len(stages)):
        ds, right = [d for d, _ in stages[n]], [block for _, block in stages[n]]
        if isinstance(right[0], tuple):
            middle, centre, far = right[0]
            centre, far = lax.optimization_barrier((centre, far, *sent))[:2]
            right = [jnp.where(middle, centre, far)]
        right = list(lax.optimization_barrier((*right, *token))[: len(right)])
        sent = products([[rel[h][r] for r in away[h]] for h in range(2)], right)
        moving = [swap(sent[h], 2 * orders[h][0]) for h in range(2)]
        right[0] = after(right[0], *sent)
        held = list(products([[rel[h][r] for r in near[h]] for h in range(2)], right))
        if n == 1 and callable(stages[-1]):
            stages[-1] = stages[-1](*held)
        names = [near[0], near[1]]
        for level in range(1, len(bits)):
            for h in (1, 0):
                bit = orders[h][level]
                stays = [i for i, r in enumerate(names[h]) if not r & bit]
                goes = [i for i, r in enumerate(names[h]) if r & bit]
                held[h], moved = fold(rows, stays, goes, held[h], moving[h])
                moving[h] = swap(moved, 2 * bit + (h if level == len(bits) - 1 else 0))
                names[h] = [names[h][i] for i in stays]
        pieces = [held[0], moving[0], swap(held[1], 1), moving[1]]
        token = pieces if n + 2 == len(stages) else held
        if out is not None:
            token = [*token, out]
        out = write(out, (rows, n_occ * width), ds, half, pieces)
    return out


def solution(mesh):
    sizes = (mesh.shape["occ"], mesh.shape["vir"])

    def run(*args):
        return per_device(sizes, *args)

    in_specs = (P(("occ", "vir"), None), P(("occ", "vir"), None), P("vir", "occ"), P("vir", "occ"))
    out_specs = P(("occ", "vir"), None)
    return jax.shard_map(run, mesh=mesh, in_specs=in_specs, out_specs=out_specs, check_vma=False)
```

```python
import functools

import jax
import jax.numpy as jnp
from jax import lax
from jax.experimental import pallas as pl
from jax.experimental.pallas import tpu as pltpu
from jax.sharding import PartitionSpec as P

TILE_O = 32
TILE_V = 128
VMEM_LIMIT = 6 * 1024 * 1024


def after(value, *earlier):
    return lax.optimization_barrier((value,) + earlier)[0]


def in_vmem(count):
    return [pl.BlockSpec(memory_space=pltpu.VMEM)] * count


def in_hbm(count):
    return [pl.BlockSpec(memory_space=pltpu.HBM)] * count


def kernel_call(body, outs, operands, name, from_hbm=False, scratch=()):
    space = pltpu.HBM if from_hbm else pltpu.VMEM
    operands = [pltpu.with_memory_space_constraint(x, space) for x in operands]
    return pl.pallas_call(
        body,
        out_shape=[pltpu.VMEM(shape, jnp.float32) for shape in outs],
        in_specs=in_hbm(len(operands)) if from_hbm else in_vmem(len(operands)),
        out_specs=in_vmem(len(outs)),
        scratch_shapes=list(scratch),
        compiler_params=pltpu.CompilerParams(vmem_limit_bytes=VMEM_LIMIT),
        cost_estimate=pl.CostEstimate(flops=1, bytes_accessed=1, transcendentals=0),
        name=name,
    )(*operands)


def tiles(start, count):
    return pl.ds(pl.multiple_of(start * TILE_V, TILE_V), count * TILE_V)


def cut_kernel(groups, depth_tiles, mask_hbm, amp_hbm, *refs):
    out_refs, (mask_ref, amp_ref, mask_sem, amp_sems) = refs[:groups], refs[groups:]
    group = lax.axis_index("vir") // 2
    mask_copy = pltpu.make_async_copy(mask_hbm, mask_ref, mask_sem)
    mask_copy.start()
    starts = [(group ^ r) * depth_tiles for r in range(groups)]
    order = range(groups - 1, -1, -1)
    copies = {
        r: pltpu.make_async_copy(amp_hbm.at[:, tiles(starts[r], depth_tiles)], amp_ref.at[r], amp_sems.at[r]) for r in order
    }
    for r in order:
        copies[r].start()
    mask_copy.wait()
    for r in order:
        copies[r].wait()
        for t in range(depth_tiles):
            for o in range(amp_hbm.shape[0] // TILE_O):
                rows = pl.ds(o * TILE_O, TILE_O)
                scale = mask_ref[o, starts[r] + t].astype(jnp.float32)
                out_refs[r][rows, tiles(t, 1)] = amp_ref[r, rows, tiles(t, 1)] * scale


def cut(mask, amplitudes, groups, depth):
    rows = amplitudes.shape[0]
    scratch = [
        pltpu.SMEM(mask.shape, jnp.int32),
        pltpu.VMEM((groups, rows, depth), jnp.float32),
        pltpu.SemaphoreType.DMA,
        pltpu.SemaphoreType.DMA((groups,)),
    ]
    body = functools.partial(cut_kernel, groups, depth // TILE_V)
    return kernel_call(body, [(rows, depth)] * groups, [mask, amplitudes], "cut", True, scratch)


def halves_kernel(mask_hbm, int_hbm, mine_ref, theirs_ref, mask_ref, int_ref, mask_sem, int_sems):
    low = lax.axis_index("vir") % 2
    count = mine_ref.shape[1] // TILE_V
    mask_copy = pltpu.make_async_copy(mask_hbm, mask_ref, mask_sem)
    mask_copy.start()
    work = ((1 - low, theirs_ref), (low, mine_ref))
    copies = [
        pltpu.make_async_copy(int_hbm.at[:, tiles(half * count, count)], int_ref.at[i], int_sems.at[i])
        for i, (half, _) in enumerate(work)
    ]
    for copy in copies:
        copy.start()
    mask_copy.wait()
    for i, (half, out_ref) in enumerate(work):
        copies[i].wait()
        for t in range(count):
            for k in range(int_hbm.shape[0] // TILE_V):
                scale = mask_ref[k, half * count + t].astype(jnp.float32)
                out_ref[tiles(k, 1), tiles(t, 1)] = int_ref[i, tiles(k, 1), tiles(t, 1)] * scale


def halves(mask, integrals):
    depth, width = integrals.shape
    scratch = [
        pltpu.SMEM(mask.shape, jnp.int32),
        pltpu.VMEM((2, depth, width // 2), jnp.float32),
        pltpu.SemaphoreType.DMA,
        pltpu.SemaphoreType.DMA((2,)),
    ]
    return kernel_call(halves_kernel, [(depth, width // 2)] * 2, [mask, integrals], "halves", True, scratch)


def join_kernel(mine_ref, other_ref, out_ref):
    low = lax.axis_index("vir") % 2
    depth = mine_ref.shape[0]
    out_ref[pl.ds(pl.multiple_of(low * depth, depth), depth), :] = mine_ref[...]
    out_ref[pl.ds(pl.multiple_of((1 - low) * depth, depth), depth), :] = other_ref[...]


def fold_kernel(rows, stays, goes, held_ref, got_ref, *out_refs):
    for out_ref, places in zip(out_refs, (stays, goes)):
        for i, k in enumerate(places):
            take = pl.ds(k * rows, rows)
            out_ref[i * rows : (i + 1) * rows, :] = held_ref[take, :] + got_ref[take, :]


def fold(rows, stays, goes, held, got):
    outs = [(len(places) * rows, held.shape[1]) for places in (stays, goes) if places]
    return kernel_call(functools.partial(fold_kernel, rows, stays, goes), outs, [held, got], "fold")


def total_kernel(rows, *refs):
    total = refs[0][rows:, :]
    for ref in refs[1:-1]:
        total = total + ref[rows:, :]
    refs[-1][...] = total


def write_kernel(d, mine, other, *refs):
    out_ref, piece_ref, sems = refs[-3:]
    low = lax.axis_index("vir") % 2
    here = lax.axis_index("occ")
    rows, width = piece_ref.shape[1:]
    copies = []
    for i, (h, parts) in enumerate(((low, refs[:mine]), (1 - low, refs[mine : mine + other]))):
        total = parts[0][:rows, :]
        for ref in parts[1:]:
            total = total + ref[:rows, :]
        piece_ref[i] = total
        start = (2 * (here ^ d) + h) * (width // TILE_V)
        copies.append(pltpu.make_async_copy(piece_ref.at[i], out_ref.at[:, tiles(start, width // TILE_V)], sems.at[i]))
        copies[i].start()
    for copy in copies:
        copy.wait()


def write(out, shape, d, mine, other):
    given = [] if out is None else [out]
    parts = [pltpu.with_memory_space_constraint(x, pltpu.VMEM) for x in [*mine, *other]]
    return pl.pallas_call(
        functools.partial(write_kernel, d, len(mine), len(other)),
        out_shape=jax.ShapeDtypeStruct(shape, jnp.float32),
        in_specs=in_vmem(len(parts)) + in_hbm(len(given)),
        out_specs=pl.BlockSpec(memory_space=pltpu.HBM),
        scratch_shapes=[pltpu.VMEM((2, shape[0], other[0].shape[1]), jnp.float32), pltpu.SemaphoreType.DMA((2,))],
        input_output_aliases={len(parts): 0} if given else {},
        compiler_params=pltpu.CompilerParams(vmem_limit_bytes=VMEM_LIMIT),
        cost_estimate=pl.CostEstimate(flops=1, bytes_accessed=1, transcendentals=0),
        name="write",
    )(*parts, *given)


def split(x):
    high = x.astype(jnp.bfloat16)
    return high, (x - high.astype(jnp.float32)).astype(jnp.bfloat16)


def dot_kernel(count, outs, *refs):
    left, block_ref, out_refs = refs[: count * outs], refs[count * outs], refs[count * outs + 1 :]
    rows = left[0].shape[0]
    b_high, b_low = split(block_ref[...])
    for h in range(outs):
        for i in range(count):
            a_high, a_low = split(left[h * count + i][...])
            total = None
            for a, b in ((a_high, b_low), (a_low, b_high), (a_high, b_high)):
                term = jnp.dot(a, b, preferred_element_type=jnp.float32)
                total = term if total is None else total + term
            out_refs[h][i * rows : (i + 1) * rows, :] = total


def products(left, block):
    count = len(left[0])
    shape = (count * left[0][0].shape[0], block.shape[1])
    body = functools.partial(dot_kernel, count, len(left))
    return list(kernel_call(body, [shape] * len(left), [x for rows in left for x in rows] + [block], "products"))


def line_stages(own, nodes):
    def direct(x, d):
        return lax.ppermute(x, "occ", [(i, i ^ d) for i in range(nodes)])

    if nodes != 4:
        return [(d, own if d == 0 else direct(own, d)) for d in range(nodes)]
    centre = lax.ppermute(own, "occ", [(1, 2), (2, 1)])
    near = direct(own, 1)
    far = lax.ppermute(after(own, centre, near), "occ", [(0, 3), (3, 0)])
    here = lax.axis_index("occ")
    middle = (here == 1) | (here == 2)

    def last(*earlier):
        moving = jnp.where(middle, after(centre, *earlier), own)
        return 2, lax.ppermute(moving, "occ", [(1, 0), (2, 3), (0, 2), (3, 1)])

    return [(0, own), (1, near), (3, (middle, centre, far)), last]


def per_device(sizes, amplitudes, amp_mask, integrals, int_mask):
    n_occ, n_vir = sizes
    rows = amplitudes.shape[0]
    groups = n_vir // 2
    own_depth, width = integrals.shape
    depth, half = 2 * own_depth, width // 2

    def swap(x, bits):
        return lax.ppermute(x, "vir", [(i, i ^ bits) for i in range(n_vir)])

    mine, theirs = halves(int_mask, integrals)
    other = swap(theirs, 1)
    parts = cut(after(amp_mask, mine), amplitudes, groups, depth)
    (whole,) = kernel_call(join_kernel, [(depth, half)], [mine, after(other, *parts)], "join")
    stages = line_stages(whole, n_occ)

    rel = [[parts[0]] + [None] * (groups - 1), [None] * groups]
    for r in range(groups - 1, 0, -1):
        rel[0][r] = swap(parts[r], 2 * r)
    for r in range(groups - 1, -1, -1):
        rel[1][r] = swap(rel[0][r] if r else after(parts[0], rel[0][groups - 1]), 1)

    bits = []
    while (1 << len(bits)) < groups:
        bits.append(1 << len(bits))
    orders = [bits, bits[::-1]]
    away = [[r for r in range(groups) if r & o[0]] for o in orders]
    near = [[r for r in range(groups) if not r & o[0]] for o in orders]

    shape = (rows, n_occ * width)
    out = None
    token = []
    for n in range(len(stages)):
        d, block = stages[n]
        if isinstance(block, tuple):
            middle, centre, far = block
            centre, far = lax.optimization_barrier((centre, far, *held))[:2]
            block = jnp.where(middle, centre, far)
        if token:
            block = after(block, *token)
        if n + 1 < len(stages):
            order = list(range(groups - 1, 0, -1))
            sent = products([[rel[0][r], rel[1][r]] for r in order], block)
            moving = [swap(sent[i], 2 * r) for i, r in enumerate(order)]
            held = products([[rel[0][0], rel[1][0]]], after(block, *sent))
            (theirs,) = kernel_call(functools.partial(total_kernel, rows), [(rows, width // 2)], [*held, *moving], "total")
            token = held if out is None else [*held, out]
            out = write(out, shape, d, [*held, *moving], [swap(theirs, 1)])
            if n == 1 and callable(stages[-1]):
                stages[-1] = stages[-1](*held)
            continue
        sent = products([[rel[h][r] for r in away[h]] for h in range(2)], block)
        moving = [swap(sent[h], 2 * orders[h][0]) for h in range(2)]
        held = products([[rel[h][r] for r in near[h]] for h in range(2)], after(block, *sent))
        names = [near[0], near[1]]
        for level in range(1, len(bits)):
            for h in (1, 0):
                bit = orders[h][level]
                stays = [i for i, r in enumerate(names[h]) if not r & bit]
                goes = [i for i, r in enumerate(names[h]) if r & bit]
                held[h], moved = fold(rows, stays, goes, held[h], moving[h])
                moving[h] = swap(moved, 2 * bit + (h if level == len(bits) - 1 else 0))
                names[h] = [names[h][i] for i in stays]
        out = write(out, shape, d, [held[0], moving[0]], [swap(held[1], 1), moving[1]])
    return out


def solution(mesh):
    sizes = (mesh.shape["occ"], mesh.shape["vir"])

    def run(*args):
        return per_device(sizes, *args)

    in_specs = (P(("occ", "vir"), None), P(("occ", "vir"), None), P("vir", "occ"), P("vir", "occ"))
    out_specs = P(("occ", "vir"), None)
    return jax.shard_map(run, mesh=mesh, in_specs=in_specs, out_specs=out_specs, check_vma=False)
```

```python
import functools

import jax
import jax.numpy as jnp
from jax import lax
from jax.experimental import pallas as pl
from jax.experimental.pallas import tpu as pltpu
from jax.sharding import PartitionSpec as P

TILE_O = 32
TILE_V = 128
VMEM_LIMIT = 6 * 1024 * 1024


def after(value, *earlier):
    return lax.optimization_barrier((value,) + earlier)[0]


def in_vmem(count):
    return [pl.BlockSpec(memory_space=pltpu.VMEM)] * count


def in_hbm(count):
    return [pl.BlockSpec(memory_space=pltpu.HBM)] * count


def kernel_call(body, outs, operands, name, from_hbm=False, scratch=()):
    space = pltpu.HBM if from_hbm else pltpu.VMEM
    operands = [pltpu.with_memory_space_constraint(x, space) for x in operands]
    return pl.pallas_call(
        body,
        out_shape=[pltpu.VMEM(shape, jnp.float32) for shape in outs],
        in_specs=in_hbm(len(operands)) if from_hbm else in_vmem(len(operands)),
        out_specs=in_vmem(len(outs)),
        scratch_shapes=list(scratch),
        compiler_params=pltpu.CompilerParams(vmem_limit_bytes=VMEM_LIMIT),
        cost_estimate=pl.CostEstimate(flops=1, bytes_accessed=1, transcendentals=0),
        name=name,
    )(*operands)


def tiles(start, count):
    return pl.ds(pl.multiple_of(start * TILE_V, TILE_V), count * TILE_V)


def cut_kernel(groups, depth_tiles, mask_hbm, amp_hbm, *refs):
    out_refs, (mask_ref, amp_ref, mask_sem, amp_sems) = refs[:groups], refs[groups:]
    group = lax.axis_index("vir") // 2
    mask_copy = pltpu.make_async_copy(mask_hbm, mask_ref, mask_sem)
    mask_copy.start()
    starts = [(group ^ r) * depth_tiles for r in range(groups)]
    order = range(groups - 1, -1, -1)
    copies = {
        r: pltpu.make_async_copy(amp_hbm.at[:, tiles(starts[r], depth_tiles)], amp_ref.at[r], amp_sems.at[r]) for r in order
    }
    for r in order:
        copies[r].start()
    mask_copy.wait()
    for r in order:
        copies[r].wait()
        for t in range(depth_tiles):
            for o in range(amp_hbm.shape[0] // TILE_O):
                rows = pl.ds(o * TILE_O, TILE_O)
                scale = mask_ref[o, starts[r] + t].astype(jnp.float32)
                out_refs[r][rows, tiles(t, 1)] = amp_ref[r, rows, tiles(t, 1)] * scale


def cut(mask, amplitudes, groups, depth):
    rows = amplitudes.shape[0]
    scratch = [
        pltpu.SMEM(mask.shape, jnp.int32),
        pltpu.VMEM((groups, rows, depth), jnp.float32),
        pltpu.SemaphoreType.DMA,
        pltpu.SemaphoreType.DMA((groups,)),
    ]
    body = functools.partial(cut_kernel, groups, depth // TILE_V)
    return kernel_call(body, [(rows, depth)] * groups, [mask, amplitudes], "cut", True, scratch)


def halves_kernel(mask_hbm, int_hbm, mine_ref, theirs_ref, mask_ref, int_ref, mask_sem, int_sems):
    low = lax.axis_index("vir") % 2
    count = mine_ref.shape[1] // TILE_V
    mask_copy = pltpu.make_async_copy(mask_hbm, mask_ref, mask_sem)
    mask_copy.start()
    work = ((1 - low, theirs_ref), (low, mine_ref))
    copies = [
        pltpu.make_async_copy(int_hbm.at[:, tiles(half * count, count)], int_ref.at[i], int_sems.at[i])
        for i, (half, _) in enumerate(work)
    ]
    for copy in copies:
        copy.start()
    mask_copy.wait()
    for i, (half, out_ref) in enumerate(work):
        copies[i].wait()
        for t in range(count):
            for k in range(int_hbm.shape[0] // TILE_V):
                scale = mask_ref[k, half * count + t].astype(jnp.float32)
                out_ref[tiles(k, 1), tiles(t, 1)] = int_ref[i, tiles(k, 1), tiles(t, 1)] * scale


def halves(mask, integrals):
    depth, width = integrals.shape
    scratch = [
        pltpu.SMEM(mask.shape, jnp.int32),
        pltpu.VMEM((2, depth, width // 2), jnp.float32),
        pltpu.SemaphoreType.DMA,
        pltpu.SemaphoreType.DMA((2,)),
    ]
    return kernel_call(halves_kernel, [(depth, width // 2)] * 2, [mask, integrals], "halves", True, scratch)


def join_kernel(mine_ref, other_ref, out_ref):
    low = lax.axis_index("vir") % 2
    depth = mine_ref.shape[0]
    out_ref[pl.ds(pl.multiple_of(low * depth, depth), depth), :] = mine_ref[...]
    out_ref[pl.ds(pl.multiple_of((1 - low) * depth, depth), depth), :] = other_ref[...]


def fold_kernel(rows, stays, goes, held_ref, got_ref, *out_refs):
    for out_ref, places in zip(out_refs, (stays, goes)):
        for i, k in enumerate(places):
            take = pl.ds(k * rows, rows)
            out_ref[i * rows : (i + 1) * rows, :] = held_ref[take, :] + got_ref[take, :]


def fold(rows, stays, goes, held, got):
    outs = [(len(places) * rows, held.shape[1]) for places in (stays, goes) if places]
    return kernel_call(functools.partial(fold_kernel, rows, stays, goes), outs, [held, got], "fold")


def total_kernel(rows, *refs):
    total = refs[0][rows:, :]
    for ref in refs[1:-1]:
        total = total + ref[rows:, :]
    refs[-1][...] = total


def write_kernel(d, mine, other, *refs):
    out_ref, piece_ref, sems = refs[-3:]
    low = lax.axis_index("vir") % 2
    here = lax.axis_index("occ")
    rows, width = piece_ref.shape[1:]
    copies = []
    for i, (h, parts) in enumerate(((low, refs[:mine]), (1 - low, refs[mine : mine + other]))):
        total = parts[0][:rows, :]
        for ref in parts[1:]:
            total = total + ref[:rows, :]
        piece_ref[i] = total
        start = (2 * (here ^ d) + h) * (width // TILE_V)
        copies.append(pltpu.make_async_copy(piece_ref.at[i], out_ref.at[:, tiles(start, width // TILE_V)], sems.at[i]))
        copies[i].start()
    for copy in copies:
        copy.wait()


def write(out, shape, d, mine, other):
    given = [] if out is None else [out]
    parts = [pltpu.with_memory_space_constraint(x, pltpu.VMEM) for x in [*mine, *other]]
    return pl.pallas_call(
        functools.partial(write_kernel, d, len(mine), len(other)),
        out_shape=jax.ShapeDtypeStruct(shape, jnp.float32),
        in_specs=in_vmem(len(parts)) + in_hbm(len(given)),
        out_specs=pl.BlockSpec(memory_space=pltpu.HBM),
        scratch_shapes=[pltpu.VMEM((2, shape[0], other[0].shape[1]), jnp.float32), pltpu.SemaphoreType.DMA((2,))],
        input_output_aliases={len(parts): 0} if given else {},
        compiler_params=pltpu.CompilerParams(vmem_limit_bytes=VMEM_LIMIT),
        cost_estimate=pl.CostEstimate(flops=1, bytes_accessed=1, transcendentals=0),
        name="write",
    )(*parts, *given)


def split(x):
    high = x.astype(jnp.bfloat16)
    return high, (x - high.astype(jnp.float32)).astype(jnp.bfloat16)


def dot_kernel(count, outs, *refs):
    left, block_ref, out_refs = refs[: count * outs], refs[count * outs], refs[count * outs + 1 :]
    rows = left[0].shape[0]
    b_high, b_low = split(block_ref[...])
    for h in range(outs):
        for i in range(count):
            a_high, a_low = split(left[h * count + i][...])
            total = None
            for a, b in ((a_high, b_low), (a_low, b_high), (a_high, b_high)):
                term = jnp.dot(a, b, preferred_element_type=jnp.float32)
                total = term if total is None else total + term
            out_refs[h][i * rows : (i + 1) * rows, :] = total


def products(left, block):
    count = len(left[0])
    shape = (count * left[0][0].shape[0], block.shape[1])
    body = functools.partial(dot_kernel, count, len(left))
    return list(kernel_call(body, [shape] * len(left), [x for rows in left for x in rows] + [block], "products"))


def line_stages(own, nodes):
    def direct(x, d):
        return lax.ppermute(x, "occ", [(i, i ^ d) for i in range(nodes)])

    if nodes != 4:
        return [(d, own if d == 0 else direct(own, d)) for d in range(nodes)]
    centre = lax.ppermute(own, "occ", [(1, 2), (2, 1)])
    near = direct(own, 1)
    far = lax.ppermute(after(own, centre, near), "occ", [(0, 3), (3, 0)])
    here = lax.axis_index("occ")
    middle = (here == 1) | (here == 2)

    def last(*earlier):
        moving = jnp.where(middle, after(centre, *earlier), own)
        return 2, lax.ppermute(moving, "occ", [(1, 0), (2, 3), (0, 2), (3, 1)])

    return [(0, own), (1, near), (3, (middle, centre, far)), last]


def per_device(sizes, amplitudes, amp_mask, integrals, int_mask):
    n_occ, n_vir = sizes
    rows = amplitudes.shape[0]
    groups = n_vir // 2
    own_depth, width = integrals.shape
    depth, half = 2 * own_depth, width // 2

    def swap(x, bits):
        return lax.ppermute(x, "vir", [(i, i ^ bits) for i in range(n_vir)])

    mine, theirs = halves(int_mask, integrals)
    other = swap(theirs, 1)
    parts = cut(after(amp_mask, mine), amplitudes, groups, depth)
    (whole,) = kernel_call(join_kernel, [(depth, half)], [mine, after(other, *parts)], "join")
    stages = line_stages(whole, n_occ)

    rel = [[parts[0]] + [None] * (groups - 1), [None] * groups]
    for r in range(groups - 1, 0, -1):
        rel[0][r] = swap(parts[r], 2 * r)
    for r in range(groups - 1, -1, -1):
        rel[1][r] = swap(rel[0][r] if r else after(parts[0], rel[0][groups - 1]), 1)

    bits = []
    while (1 << len(bits)) < groups:
        bits.append(1 << len(bits))
    orders = [bits, bits[::-1]]
    away = [[r for r in range(groups) if r & o[0]] for o in orders]
    near = [[r for r in range(groups) if not r & o[0]] for o in orders]

    shape = (rows, n_occ * width)

    def finish(out, d, held, moving):
        (theirs,) = kernel_call(functools.partial(total_kernel, rows), [(rows, width // 2)], [*held, *moving], "total")
        return write(out, shape, d, [*held, *moving], [swap(theirs, 1)])

    out = None
    token = []
    waiting = None
    for n in range(len(stages)):
        d, block = stages[n]
        if isinstance(block, tuple):
            middle, centre, far = block
            centre, far = lax.optimization_barrier((centre, far, *held))[:2]
            block = jnp.where(middle, centre, far)
        if token:
            block = after(block, *token)
        if n + 2 < len(stages):
            order = list(range(groups - 1, 0, -1))
            sent = products([[rel[0][r], rel[1][r]] for r in order], block)
            moving = [swap(sent[i], 2 * r) for i, r in enumerate(order)]
            held = products([[rel[0][0], rel[1][0]]], after(block, *sent))
            token = held if out is None else [*held, out]
            if n + 3 < len(stages):
                out = finish(out, d, held, moving)
            else:
                waiting = d, held, moving
            if n == 1 and callable(stages[-1]):
                stages[-1] = stages[-1](*held)
            continue
        sent = products([[rel[h][r] for r in away[h]] for h in range(2)], block)
        if waiting is not None:
            d_before, held, moving = waiting
            out = finish(out, d_before, held, list(lax.optimization_barrier((*moving, *sent))[: len(moving)]))
            waiting = None
        moving = [swap(sent[h], 2 * orders[h][0]) for h in range(2)]
        held = products([[rel[h][r] for r in near[h]] for h in range(2)], after(block, *sent))
        names = [near[0], near[1]]
        for level in range(1, len(bits)):
            for h in (1, 0):
                bit = orders[h][level]
                stays = [i for i, r in enumerate(names[h]) if not r & bit]
                goes = [i for i, r in enumerate(names[h]) if r & bit]
                held[h], moved = fold(rows, stays, goes, held[h], moving[h])
                moving[h] = swap(moved, 2 * bit + (h if level == len(bits) - 1 else 0))
                names[h] = [names[h][i] for i in stays]
        other = [swap(held[1], 1), moving[1]]
        token = [held[0], moving[0], *other]
        out = write(out, shape, d, [held[0], moving[0]], other)
    return out


def solution(mesh):
    sizes = (mesh.shape["occ"], mesh.shape["vir"])

    def run(*args):
        return per_device(sizes, *args)

    in_specs = (P(("occ", "vir"), None), P(("occ", "vir"), None), P("vir", "occ"), P("vir", "occ"))
    out_specs = P(("occ", "vir"), None)
    return jax.shard_map(run, mesh=mesh, in_specs=in_specs, out_specs=out_specs, check_vma=False)
```

```python
import functools

import jax
import jax.numpy as jnp
from jax import lax
from jax.experimental import pallas as pl
from jax.experimental.pallas import tpu as pltpu
from jax.sharding import PartitionSpec as P

TILE_O = 32
TILE_V = 128
VMEM_LIMIT = 6 * 1024 * 1024


def after(value, *earlier):
    return lax.optimization_barrier((value,) + earlier)[0]


def in_vmem(count):
    return [pl.BlockSpec(memory_space=pltpu.VMEM)] * count


def in_hbm(count):
    return [pl.BlockSpec(memory_space=pltpu.HBM)] * count


def kernel_call(body, outs, operands, name, from_hbm=False, scratch=()):
    space = pltpu.HBM if from_hbm else pltpu.VMEM
    operands = [pltpu.with_memory_space_constraint(x, space) for x in operands]
    return pl.pallas_call(
        body,
        out_shape=[pltpu.VMEM(shape, jnp.float32) for shape in outs],
        in_specs=in_hbm(len(operands)) if from_hbm else in_vmem(len(operands)),
        out_specs=in_vmem(len(outs)),
        scratch_shapes=list(scratch),
        compiler_params=pltpu.CompilerParams(vmem_limit_bytes=VMEM_LIMIT),
        cost_estimate=pl.CostEstimate(flops=1, bytes_accessed=1, transcendentals=0),
        name=name,
    )(*operands)


def tiles(start, count):
    return pl.ds(pl.multiple_of(start * TILE_V, TILE_V), count * TILE_V)


def cut_kernel(groups, depth_tiles, mask_hbm, amp_hbm, *refs):
    out_refs, (mask_ref, amp_ref, mask_sem, amp_sems) = refs[:groups], refs[groups:]
    group = lax.axis_index("vir") // 2
    mask_copy = pltpu.make_async_copy(mask_hbm, mask_ref, mask_sem)
    mask_copy.start()
    starts = [(group ^ r) * depth_tiles for r in range(groups)]
    order = range(groups - 1, -1, -1)
    copies = {
        r: pltpu.make_async_copy(amp_hbm.at[:, tiles(starts[r], depth_tiles)], amp_ref.at[r], amp_sems.at[r]) for r in order
    }
    for r in order:
        copies[r].start()
    mask_copy.wait()
    for r in order:
        copies[r].wait()
        for t in range(depth_tiles):
            for o in range(amp_hbm.shape[0] // TILE_O):
                rows = pl.ds(o * TILE_O, TILE_O)
                scale = mask_ref[o, starts[r] + t].astype(jnp.float32)
                out_refs[r][rows, tiles(t, 1)] = amp_ref[r, rows, tiles(t, 1)] * scale


def cut(mask, amplitudes, groups, depth):
    rows = amplitudes.shape[0]
    scratch = [
        pltpu.SMEM(mask.shape, jnp.int32),
        pltpu.VMEM((groups, rows, depth), jnp.float32),
        pltpu.SemaphoreType.DMA,
        pltpu.SemaphoreType.DMA((groups,)),
    ]
    body = functools.partial(cut_kernel, groups, depth // TILE_V)
    return kernel_call(body, [(rows, depth)] * groups, [mask, amplitudes], "cut", True, scratch)


def halves_kernel(mask_hbm, int_hbm, mine_ref, theirs_ref, mask_ref, int_ref, mask_sem, int_sems):
    low = lax.axis_index("vir") % 2
    count = mine_ref.shape[1] // TILE_V
    mask_copy = pltpu.make_async_copy(mask_hbm, mask_ref, mask_sem)
    mask_copy.start()
    work = ((1 - low, theirs_ref), (low, mine_ref))
    copies = [
        pltpu.make_async_copy(int_hbm.at[:, tiles(half * count, count)], int_ref.at[i], int_sems.at[i])
        for i, (half, _) in enumerate(work)
    ]
    for copy in copies:
        copy.start()
    mask_copy.wait()
    for i, (half, out_ref) in enumerate(work):
        copies[i].wait()
        for t in range(count):
            for k in range(int_hbm.shape[0] // TILE_V):
                scale = mask_ref[k, half * count + t].astype(jnp.float32)
                out_ref[tiles(k, 1), tiles(t, 1)] = int_ref[i, tiles(k, 1), tiles(t, 1)] * scale


def halves(mask, integrals):
    depth, width = integrals.shape
    scratch = [
        pltpu.SMEM(mask.shape, jnp.int32),
        pltpu.VMEM((2, depth, width // 2), jnp.float32),
        pltpu.SemaphoreType.DMA,
        pltpu.SemaphoreType.DMA((2,)),
    ]
    return kernel_call(halves_kernel, [(depth, width // 2)] * 2, [mask, integrals], "halves", True, scratch)


def join_kernel(mine_ref, other_ref, out_ref):
    low = lax.axis_index("vir") % 2
    depth = mine_ref.shape[0]
    out_ref[pl.ds(pl.multiple_of(low * depth, depth), depth), :] = mine_ref[...]
    out_ref[pl.ds(pl.multiple_of((1 - low) * depth, depth), depth), :] = other_ref[...]


def fold_kernel(rows, stays, goes, held_ref, got_ref, *out_refs):
    for out_ref, places in zip(out_refs, (stays, goes)):
        for i, k in enumerate(places):
            take = pl.ds(k * rows, rows)
            out_ref[i * rows : (i + 1) * rows, :] = held_ref[take, :] + got_ref[take, :]


def fold(rows, stays, goes, held, got):
    outs = [(len(places) * rows, held.shape[1]) for places in (stays, goes) if places]
    return kernel_call(functools.partial(fold_kernel, rows, stays, goes), outs, [held, got], "fold")


def write_kernel(ds, half, mine_a, mine_b, other_a, other_b, *refs):
    out_ref, piece_ref, sems = refs[-3:]
    low = lax.axis_index("vir") % 2
    here = lax.axis_index("occ")
    piece_ref[0] = mine_a[...] + mine_b[...]
    piece_ref[1] = other_a[...] + other_b[...]
    copies = []
    for k, d in enumerate(ds):
        for i, h in enumerate((low, 1 - low)):
            start = (2 * (here ^ d) + h) * (half // TILE_V)
            source = piece_ref.at[i, :, pl.ds(k * half, half)]
            copies.append(pltpu.make_async_copy(source, out_ref.at[:, tiles(start, half // TILE_V)], sems.at[2 * k + i]))
    for copy in copies:
        copy.start()
    for copy in copies:
        copy.wait()


def write(out, shape, ds, half, pieces):
    given = [] if out is None else [out]
    pieces = [pltpu.with_memory_space_constraint(x, pltpu.VMEM) for x in pieces]
    return pl.pallas_call(
        functools.partial(write_kernel, ds, half),
        out_shape=jax.ShapeDtypeStruct(shape, jnp.float32),
        in_specs=in_vmem(4) + in_hbm(len(given)),
        out_specs=pl.BlockSpec(memory_space=pltpu.HBM),
        scratch_shapes=[pltpu.VMEM((2, *pieces[0].shape), jnp.float32), pltpu.SemaphoreType.DMA((2 * len(ds),))],
        input_output_aliases={4: 0} if given else {},
        compiler_params=pltpu.CompilerParams(vmem_limit_bytes=VMEM_LIMIT),
        cost_estimate=pl.CostEstimate(flops=1, bytes_accessed=1, transcendentals=0),
        name="write",
    )(*pieces, *given)


def split(x):
    high = x.astype(jnp.bfloat16)
    return high, (x - high.astype(jnp.float32)).astype(jnp.bfloat16)


def dot_kernel(count, blocks, *refs):
    left, right, outs = refs[: 2 * count], refs[2 * count : 2 * count + blocks], refs[2 * count + blocks :]
    rows, width = left[0].shape[0], right[0].shape[1]
    for k in range(blocks):
        b_high, b_low = split(right[k][...])
        for h in range(2):
            for i in range(count):
                a_high, a_low = split(left[h * count + i][...])
                total = None
                for a, b in ((a_high, b_low), (a_low, b_high), (a_high, b_high)):
                    term = jnp.dot(a, b, preferred_element_type=jnp.float32)
                    total = term if total is None else total + term
                outs[h][i * rows : (i + 1) * rows, k * width : (k + 1) * width] = total


def products(left, right):
    count = len(left[0])
    shape = (count * left[0][0].shape[0], len(right) * right[0].shape[1])
    return kernel_call(functools.partial(dot_kernel, count, len(right)), [shape] * 2, [*left[0], *left[1], *right], "products")


def line_stages(own, nodes):
    def direct(x, d):
        return lax.ppermute(x, "occ", [(i, i ^ d) for i in range(nodes)])

    if nodes != 4:
        return [[(d, own if d == 0 else direct(own, d))] for d in range(nodes)]
    centre = lax.ppermute(own, "occ", [(1, 2), (2, 1)])
    near = direct(own, 1)
    far = lax.ppermute(after(own, centre, near), "occ", [(0, 3), (3, 0)])
    here = lax.axis_index("occ")
    middle = (here == 1) | (here == 2)

    last = lax.ppermute(jnp.where(middle, centre, own), "occ", [(1, 0), (2, 3), (0, 2), (3, 1)])
    return [[(0, own)], [(1, near)], [(3, (middle, centre, far))], [(2, last)]]


def per_device(sizes, amplitudes, amp_mask, integrals, int_mask):
    n_occ, n_vir = sizes
    rows = amplitudes.shape[0]
    groups = n_vir // 2
    own_depth, width = integrals.shape
    depth, half = 2 * own_depth, width // 2

    def swap(x, bits):
        return lax.ppermute(x, "vir", [(i, i ^ bits) for i in range(n_vir)])

    mine, theirs = halves(int_mask, integrals)
    other = swap(theirs, 1)
    parts = cut(after(amp_mask, mine), amplitudes, groups, depth)
    (whole,) = kernel_call(join_kernel, [(depth, half)], [mine, after(other, *parts)], "join")
    stages = line_stages(whole, n_occ)

    rel = [[parts[0]] + [None] * (groups - 1), [None] * groups]
    for r in range(groups - 1, 0, -1):
        rel[0][r] = swap(parts[r], 2 * r)
    for r in range(groups - 1, -1, -1):
        rel[1][r] = swap(rel[0][r] if r else after(parts[0], rel[0][groups - 1]), 1)

    bits = []
    while (1 << len(bits)) < groups:
        bits.append(1 << len(bits))
    orders = [bits, bits[::-1]]
    away = [[r for r in range(groups) if r & o[0]] for o in orders]
    near = [[r for r in range(groups) if not r & o[0]] for o in orders]

    out = None
    token = settled = []
    for n in range(len(stages)):
        ds, right = [d for d, _ in stages[n]], [block for _, block in stages[n]]
        if isinstance(right[0], tuple):
            middle, centre, far = right[0]
            centre, far = lax.optimization_barrier((centre, far, *sent))[:2]
            right = [jnp.where(middle, centre, far)]
        right = list(lax.optimization_barrier((*right, *token))[: len(right)])
        sent = products([[rel[h][r] for r in away[h]] for h in range(2)], right)
        moving = [swap(sent[h], 2 * orders[h][0]) for h in range(2)]
        right[0] = after(right[0], *sent, *settled)
        held = list(products([[rel[h][r] for r in near[h]] for h in range(2)], right))
        names = [near[0], near[1]]
        for level in range(1, len(bits)):
            for h in (1, 0):
                bit = orders[h][level]
                stays = [i for i, r in enumerate(names[h]) if not r & bit]
                goes = [i for i, r in enumerate(names[h]) if r & bit]
                held[h], moved = fold(rows, stays, goes, held[h], moving[h])
                moving[h] = swap(moved, 2 * bit + (h if level == len(bits) - 1 else 0))
                names[h] = [names[h][i] for i in stays]
        pieces = [held[0], moving[0], swap(held[1], 1), moving[1]]
        token = [*held] if out is None else [*held, out]
        settled = moving if n + 2 < len(stages) else []
        out = write(out, (rows, n_occ * width), ds, half, pieces)
    return out


def solution(mesh):
    sizes = (mesh.shape["occ"], mesh.shape["vir"])

    def run(*args):
        return per_device(sizes, *args)

    in_specs = (P(("occ", "vir"), None), P(("occ", "vir"), None), P("vir", "occ"), P("vir", "occ"))
    out_specs = P(("occ", "vir"), None)
    return jax.shard_map(run, mesh=mesh, in_specs=in_specs, out_specs=out_specs, check_vma=False)
```

```python
import functools

import jax
import jax.numpy as jnp
from jax import lax
from jax.experimental import pallas as pl
from jax.experimental.pallas import tpu as pltpu
from jax.sharding import PartitionSpec as P

TILE_O = 32
TILE_V = 128
VMEM_LIMIT = 6 * 1024 * 1024


def after(value, *earlier):
    return lax.optimization_barrier((value,) + earlier)[0]


def in_vmem(count):
    return [pl.BlockSpec(memory_space=pltpu.VMEM)] * count


def in_hbm(count):
    return [pl.BlockSpec(memory_space=pltpu.HBM)] * count


def kernel_call(body, outs, operands, name, from_hbm=False, scratch=()):
    space = pltpu.HBM if from_hbm else pltpu.VMEM
    operands = [pltpu.with_memory_space_constraint(x, space) for x in operands]
    return pl.pallas_call(
        body,
        out_shape=[pltpu.VMEM(shape, jnp.float32) for shape in outs],
        in_specs=in_hbm(len(operands)) if from_hbm else in_vmem(len(operands)),
        out_specs=in_vmem(len(outs)),
        scratch_shapes=list(scratch),
        compiler_params=pltpu.CompilerParams(vmem_limit_bytes=VMEM_LIMIT),
        cost_estimate=pl.CostEstimate(flops=1, bytes_accessed=1, transcendentals=0),
        name=name,
    )(*operands)


def tiles(start, count):
    return pl.ds(pl.multiple_of(start * TILE_V, TILE_V), count * TILE_V)


def cut_kernel(groups, depth_tiles, mask_hbm, amp_hbm, *refs):
    out_refs, (mask_ref, amp_ref, mask_sem, amp_sems) = refs[:groups], refs[groups:]
    group = lax.axis_index("vir") // 2
    mask_copy = pltpu.make_async_copy(mask_hbm, mask_ref, mask_sem)
    mask_copy.start()
    starts = [(group ^ r) * depth_tiles for r in range(groups)]
    order = range(groups - 1, -1, -1)
    copies = {
        r: pltpu.make_async_copy(amp_hbm.at[:, tiles(starts[r], depth_tiles)], amp_ref.at[r], amp_sems.at[r]) for r in order
    }
    for r in order:
        copies[r].start()
    mask_copy.wait()
    for r in order:
        copies[r].wait()
        for t in range(depth_tiles):
            for o in range(amp_hbm.shape[0] // TILE_O):
                rows = pl.ds(o * TILE_O, TILE_O)
                scale = mask_ref[o, starts[r] + t].astype(jnp.float32)
                out_refs[r][rows, tiles(t, 1)] = amp_ref[r, rows, tiles(t, 1)] * scale


def cut(mask, amplitudes, groups, depth):
    rows = amplitudes.shape[0]
    scratch = [
        pltpu.SMEM(mask.shape, jnp.int32),
        pltpu.VMEM((groups, rows, depth), jnp.float32),
        pltpu.SemaphoreType.DMA,
        pltpu.SemaphoreType.DMA((groups,)),
    ]
    body = functools.partial(cut_kernel, groups, depth // TILE_V)
    return kernel_call(body, [(rows, depth)] * groups, [mask, amplitudes], "cut", True, scratch)


def halves_kernel(mask_hbm, int_hbm, mine_ref, theirs_ref, mask_ref, int_ref, mask_sem, int_sems):
    low = lax.axis_index("vir") % 2
    count = mine_ref.shape[1] // TILE_V
    mask_copy = pltpu.make_async_copy(mask_hbm, mask_ref, mask_sem)
    mask_copy.start()
    work = ((1 - low, theirs_ref), (low, mine_ref))
    copies = [
        pltpu.make_async_copy(int_hbm.at[:, tiles(half * count, count)], int_ref.at[i], int_sems.at[i])
        for i, (half, _) in enumerate(work)
    ]
    for copy in copies:
        copy.start()
    mask_copy.wait()
    for i, (half, out_ref) in enumerate(work):
        copies[i].wait()
        for t in range(count):
            for k in range(int_hbm.shape[0] // TILE_V):
                scale = mask_ref[k, half * count + t].astype(jnp.float32)
                out_ref[tiles(k, 1), tiles(t, 1)] = int_ref[i, tiles(k, 1), tiles(t, 1)] * scale


def halves(mask, integrals):
    depth, width = integrals.shape
    scratch = [
        pltpu.SMEM(mask.shape, jnp.int32),
        pltpu.VMEM((2, depth, width // 2), jnp.float32),
        pltpu.SemaphoreType.DMA,
        pltpu.SemaphoreType.DMA((2,)),
    ]
    return kernel_call(halves_kernel, [(depth, width // 2)] * 2, [mask, integrals], "halves", True, scratch)


def join_kernel(mine_ref, other_ref, out_ref):
    low = lax.axis_index("vir") % 2
    depth = mine_ref.shape[0]
    out_ref[pl.ds(pl.multiple_of(low * depth, depth), depth), :] = mine_ref[...]
    out_ref[pl.ds(pl.multiple_of((1 - low) * depth, depth), depth), :] = other_ref[...]


def fold_kernel(rows, stays, goes, held_ref, got_ref, *out_refs):
    for out_ref, places in zip(out_refs, (stays, goes)):
        for i, k in enumerate(places):
            take = pl.ds(k * rows, rows)
            out_ref[i * rows : (i + 1) * rows, :] = held_ref[take, :] + got_ref[take, :]


def fold(rows, stays, goes, held, got):
    outs = [(len(places) * rows, held.shape[1]) for places in (stays, goes) if places]
    return kernel_call(functools.partial(fold_kernel, rows, stays, goes), outs, [held, got], "fold")


def write_kernel(ds, half, mine_a, mine_b, other_a, other_b, *refs):
    out_ref, piece_ref, sems = refs[-3:]
    low = lax.axis_index("vir") % 2
    here = lax.axis_index("occ")
    piece_ref[0] = mine_a[...] + mine_b[...]
    piece_ref[1] = other_a[...] + other_b[...]
    copies = []
    for k, d in enumerate(ds):
        for i, h in enumerate((low, 1 - low)):
            start = (2 * (here ^ d) + h) * (half // TILE_V)
            source = piece_ref.at[i, :, pl.ds(k * half, half)]
            copies.append(pltpu.make_async_copy(source, out_ref.at[:, tiles(start, half // TILE_V)], sems.at[2 * k + i]))
    for copy in copies:
        copy.start()
    for copy in copies:
        copy.wait()


def write(out, shape, ds, half, pieces):
    given = [] if out is None else [out]
    pieces = [pltpu.with_memory_space_constraint(x, pltpu.VMEM) for x in pieces]
    return pl.pallas_call(
        functools.partial(write_kernel, ds, half),
        out_shape=jax.ShapeDtypeStruct(shape, jnp.float32),
        in_specs=in_vmem(4) + in_hbm(len(given)),
        out_specs=pl.BlockSpec(memory_space=pltpu.HBM),
        scratch_shapes=[pltpu.VMEM((2, *pieces[0].shape), jnp.float32), pltpu.SemaphoreType.DMA((2 * len(ds),))],
        input_output_aliases={4: 0} if given else {},
        compiler_params=pltpu.CompilerParams(vmem_limit_bytes=VMEM_LIMIT),
        cost_estimate=pl.CostEstimate(flops=1, bytes_accessed=1, transcendentals=0),
        name="write",
    )(*pieces, *given)


def split(x):
    high = x.astype(jnp.bfloat16)
    return high, (x - high.astype(jnp.float32)).astype(jnp.bfloat16)


def dot_kernel(count, blocks, *refs):
    left, right, outs = refs[: 2 * count], refs[2 * count : 2 * count + blocks], refs[2 * count + blocks :]
    rows, width = left[0].shape[0], right[0].shape[1]
    for k in range(blocks):
        b_high, b_low = split(right[k][...])
        for h in range(2):
            for i in range(count):
                a_high, a_low = split(left[h * count + i][...])
                total = None
                for a, b in ((a_high, b_low), (a_low, b_high), (a_high, b_high)):
                    term = jnp.dot(a, b, preferred_element_type=jnp.float32)
                    total = term if total is None else total + term
                outs[h][i * rows : (i + 1) * rows, k * width : (k + 1) * width] = total


def products(left, right):
    count = len(left[0])
    shape = (count * left[0][0].shape[0], len(right) * right[0].shape[1])
    return kernel_call(functools.partial(dot_kernel, count, len(right)), [shape] * 2, [*left[0], *left[1], *right], "products")


def line_stages(own, nodes):
    def direct(x, d):
        return lax.ppermute(x, "occ", [(i, i ^ d) for i in range(nodes)])

    if nodes != 4:
        return [[(d, own if d == 0 else direct(own, d))] for d in range(nodes)]
    centre = lax.ppermute(own, "occ", [(1, 2), (2, 1)])
    near = direct(own, 1)
    far = lax.ppermute(after(own, centre, near), "occ", [(0, 3), (3, 0)])
    here = lax.axis_index("occ")
    middle = (here == 1) | (here == 2)

    last = lax.ppermute(jnp.where(middle, centre, own), "occ", [(1, 0), (2, 3), (0, 2), (3, 1)])
    return [[(0, own)], [(1, near)], [(3, (middle, centre, far))], [(2, last)]]


def per_device(sizes, amplitudes, amp_mask, integrals, int_mask):
    n_occ, n_vir = sizes
    rows = amplitudes.shape[0]
    groups = n_vir // 2
    own_depth, width = integrals.shape
    depth, half = 2 * own_depth, width // 2

    def swap(x, bits):
        return lax.ppermute(x, "vir", [(i, i ^ bits) for i in range(n_vir)])

    mine, theirs = halves(int_mask, integrals)
    other = swap(theirs, 1)
    parts = cut(after(amp_mask, mine), amplitudes, groups, depth)
    (whole,) = kernel_call(join_kernel, [(depth, half)], [mine, after(other, *parts)], "join")
    stages = line_stages(whole, n_occ)

    rel = [[parts[0]] + [None] * (groups - 1), [None] * groups]
    for r in range(groups - 1, 0, -1):
        rel[0][r] = swap(parts[r], 2 * r)
    for r in range(groups - 1, -1, -1):
        rel[1][r] = swap(rel[0][r] if r else after(parts[0], rel[0][groups - 1]), 1)

    bits = []
    while (1 << len(bits)) < groups:
        bits.append(1 << len(bits))
    orders = [bits, bits[::-1]]
    away = [[r for r in range(groups) if r & o[0]] for o in orders]
    near = [[r for r in range(groups) if not r & o[0]] for o in orders]

    out = None
    token = []
    for n in range(len(stages)):
        ds, right = [d for d, _ in stages[n]], [block for _, block in stages[n]]
        if isinstance(right[0], tuple):
            middle, centre, far = right[0]
            centre, far = lax.optimization_barrier((centre, far, *sent))[:2]
            right = [jnp.where(middle, centre, far)]
        right = list(lax.optimization_barrier((*right, *token))[: len(right)])
        sent = products([[rel[h][r] for r in away[h]] for h in range(2)], right)
        moving = [swap(sent[h], 2 * orders[h][0]) for h in range(2)]
        right[0] = after(right[0], *sent)
        held = list(products([[rel[h][r] for r in near[h]] for h in range(2)], right))
        names = [near[0], near[1]]
        for level in range(1, len(bits)):
            for h in (1, 0):
                bit = orders[h][level]
                stays = [i for i, r in enumerate(names[h]) if not r & bit]
                goes = [i for i, r in enumerate(names[h]) if r & bit]
                held[h], moved = fold(rows, stays, goes, held[h], moving[h])
                moving[h] = swap(moved, 2 * bit + (h if level == len(bits) - 1 else 0))
                names[h] = [names[h][i] for i in stays]
        pieces = [held[0], moving[0], swap(held[1], 1), moving[1]]
        token = [*held] if out is None else [*held, out]
        out = write(out, (rows, n_occ * width), ds, half, pieces)
    return out


def solution(mesh):
    sizes = (mesh.shape["occ"], mesh.shape["vir"])

    def run(*args):
        return per_device(sizes, *args)

    in_specs = (P(("occ", "vir"), None), P(("occ", "vir"), None), P("vir", "occ"), P("vir", "occ"))
    out_specs = P(("occ", "vir"), None)
    return jax.shard_map(run, mesh=mesh, in_specs=in_specs, out_specs=out_specs, check_vma=False)
```

```python
import functools

import jax
import jax.numpy as jnp
from jax import lax
from jax.experimental import pallas as pl
from jax.experimental.pallas import tpu as pltpu
from jax.sharding import PartitionSpec as P

TILE_O = 32
TILE_V = 128
VMEM_LIMIT = 12 * 1024 * 1024


def after(value, *earlier):
    return lax.optimization_barrier((value,) + earlier)[0]


def in_vmem(count):
    return [pl.BlockSpec(memory_space=pltpu.VMEM)] * count


def in_hbm(count):
    return [pl.BlockSpec(memory_space=pltpu.HBM)] * count


def kernel_call(body, outs, operands, name, from_hbm=False, scratch=()):
    space = pltpu.HBM if from_hbm else pltpu.VMEM
    operands = [pltpu.with_memory_space_constraint(x, space) for x in operands]
    return pl.pallas_call(
        body,
        out_shape=[pltpu.VMEM(shape, jnp.float32) for shape in outs],
        in_specs=in_hbm(len(operands)) if from_hbm else in_vmem(len(operands)),
        out_specs=in_vmem(len(outs)),
        scratch_shapes=list(scratch),
        compiler_params=pltpu.CompilerParams(vmem_limit_bytes=VMEM_LIMIT),
        cost_estimate=pl.CostEstimate(flops=1, bytes_accessed=1, transcendentals=0),
        name=name,
    )(*operands)


def tiles(start, count):
    return pl.ds(pl.multiple_of(start * TILE_V, TILE_V), count * TILE_V)


def cut_kernel(groups, depth_tiles, mask_hbm, amp_hbm, *refs):
    out_refs, (mask_ref, amp_ref, mask_sem, amp_sems) = refs[:groups], refs[groups:]
    group = lax.axis_index("vir") // 2
    mask_copy = pltpu.make_async_copy(mask_hbm, mask_ref, mask_sem)
    mask_copy.start()
    starts = [(group ^ r) * depth_tiles for r in range(groups)]
    order = range(groups - 1, -1, -1)
    copies = {
        r: pltpu.make_async_copy(amp_hbm.at[:, tiles(starts[r], depth_tiles)], amp_ref.at[r], amp_sems.at[r]) for r in order
    }
    for r in order:
        copies[r].start()
    mask_copy.wait()
    for r in order:
        copies[r].wait()
        for t in range(depth_tiles):
            for o in range(amp_hbm.shape[0] // TILE_O):
                rows = pl.ds(o * TILE_O, TILE_O)
                scale = mask_ref[o, starts[r] + t].astype(jnp.float32)
                out_refs[r][rows, tiles(t, 1)] = amp_ref[r, rows, tiles(t, 1)] * scale


def cut(mask, amplitudes, groups, depth):
    rows = amplitudes.shape[0]
    scratch = [
        pltpu.SMEM(mask.shape, jnp.int32),
        pltpu.VMEM((groups, rows, depth), jnp.float32),
        pltpu.SemaphoreType.DMA,
        pltpu.SemaphoreType.DMA((groups,)),
    ]
    body = functools.partial(cut_kernel, groups, depth // TILE_V)
    return kernel_call(body, [(rows, depth)] * groups, [mask, amplitudes], "cut", True, scratch)


def halves_kernel(mask_hbm, int_hbm, mine_ref, theirs_ref, mask_ref, int_ref, mask_sem, int_sems):
    low = lax.axis_index("vir") % 2
    count = mine_ref.shape[1] // TILE_V
    mask_copy = pltpu.make_async_copy(mask_hbm, mask_ref, mask_sem)
    mask_copy.start()
    work = ((1 - low, theirs_ref), (low, mine_ref))
    copies = [
        pltpu.make_async_copy(int_hbm.at[:, tiles(half * count, count)], int_ref.at[i], int_sems.at[i])
        for i, (half, _) in enumerate(work)
    ]
    for copy in copies:
        copy.start()
    mask_copy.wait()
    for i, (half, out_ref) in enumerate(work):
        copies[i].wait()
        for t in range(count):
            for k in range(int_hbm.shape[0] // TILE_V):
                scale = mask_ref[k, half * count + t].astype(jnp.float32)
                out_ref[tiles(k, 1), tiles(t, 1)] = int_ref[i, tiles(k, 1), tiles(t, 1)] * scale


def halves(mask, integrals):
    depth, width = integrals.shape
    scratch = [
        pltpu.SMEM(mask.shape, jnp.int32),
        pltpu.VMEM((2, depth, width // 2), jnp.float32),
        pltpu.SemaphoreType.DMA,
        pltpu.SemaphoreType.DMA((2,)),
    ]
    return kernel_call(halves_kernel, [(depth, width // 2)] * 2, [mask, integrals], "halves", True, scratch)


def join_kernel(mine_ref, other_ref, out_ref):
    low = lax.axis_index("vir") % 2
    depth = mine_ref.shape[0]
    out_ref[pl.ds(pl.multiple_of(low * depth, depth), depth), :] = mine_ref[...]
    out_ref[pl.ds(pl.multiple_of((1 - low) * depth, depth), depth), :] = other_ref[...]


def fold_kernel(rows, stays, goes, held_ref, got_ref, *out_refs):
    for out_ref, places in zip(out_refs, (stays, goes)):
        for i, k in enumerate(places):
            take = pl.ds(k * rows, rows)
            out_ref[i * rows : (i + 1) * rows, :] = held_ref[take, :] + got_ref[take, :]


def fold(rows, stays, goes, held, got):
    outs = [(len(places) * rows, held.shape[1]) for places in (stays, goes) if places]
    return kernel_call(functools.partial(fold_kernel, rows, stays, goes), outs, [held, got], "fold")


def write_kernel(d, half, offset, held_ref, got_ref, other_ref, *refs):
    out_ref, piece_ref, sems = refs[-3:]
    low = lax.axis_index("vir") % 2
    place = lax.axis_index("occ") ^ d
    width = held_ref.shape[1] // TILE_V
    starts = [(2 * place + h) * (half // TILE_V) + offset // TILE_V for h in (low, 1 - low)]
    piece_ref[...] = held_ref[...] + got_ref[...]
    copies = [
        pltpu.make_async_copy(source, out_ref.at[:, tiles(start, width)], sems.at[i])
        for i, (source, start) in enumerate(zip((piece_ref, other_ref), starts))
    ]
    for copy in copies:
        copy.start()
    for copy in copies:
        copy.wait()


def write(out, shape, d, half, offset, held, got, other):
    given = [] if out is None else [out]
    return pl.pallas_call(
        functools.partial(write_kernel, d, half, offset),
        out_shape=jax.ShapeDtypeStruct(shape, jnp.float32),
        in_specs=in_vmem(3) + in_hbm(len(given)),
        out_specs=pl.BlockSpec(memory_space=pltpu.HBM),
        scratch_shapes=[pltpu.VMEM(held.shape, jnp.float32), pltpu.SemaphoreType.DMA((2,))],
        input_output_aliases={3: 0} if given else {},
        compiler_params=pltpu.CompilerParams(vmem_limit_bytes=VMEM_LIMIT),
        cost_estimate=pl.CostEstimate(flops=1, bytes_accessed=1, transcendentals=0),
        name="write",
    )(held, got, other, *given)


def split(x):
    high = x.astype(jnp.bfloat16)
    return high, (x - high.astype(jnp.float32)).astype(jnp.bfloat16)


def dot_kernel(count, *refs):
    left, block_ref, outs = refs[: 2 * count], refs[2 * count], refs[2 * count + 1 :]
    rows = left[0].shape[0]
    b_high, b_low = split(block_ref[...])
    for h in range(2):
        for i in range(count):
            a_high, a_low = split(left[h * count + i][...])
            total = None
            for a, b in ((a_high, b_low), (a_low, b_high), (a_high, b_high)):
                term = jnp.dot(a, b, preferred_element_type=jnp.float32)
                total = term if total is None else total + term
            outs[h][i * rows : (i + 1) * rows, :] = total


def products(left, block):
    count = len(left[0])
    shape = (count * left[0][0].shape[0], block.shape[1])
    return kernel_call(functools.partial(dot_kernel, count), [shape] * 2, [*left[0], *left[1], block], "products")


def line_blocks(own, nodes):
    here = lax.axis_index("occ")

    def direct(x, d):
        return lax.ppermute(x, "occ", [(i, i ^ d) for i in range(nodes)])

    if nodes != 4:
        return [(d, own if d == 0 else direct(own, d), 0) for d in range(nodes)]
    centre = lax.ppermute(own, "occ", [(1, 2), (2, 1)])
    near = direct(own, 1)
    far = lax.ppermute(after(own, centre, near), "occ", [(0, 3), (3, 0)])
    middle = (here == 1) | (here == 2)
    last = lax.ppermute(jnp.where(middle, centre, own), "occ", [(1, 0), (2, 3), (0, 2), (3, 1)])
    return [(0, own, 0), (1, near, 0), (3, (middle, centre, far), 0), (2, last, 0)]


def per_device(sizes, amplitudes, amp_mask, integrals, int_mask):
    n_occ, n_vir = sizes
    rows = amplitudes.shape[0]
    groups = n_vir // 2
    own_depth, width = integrals.shape
    depth, half = 2 * own_depth, width // 2

    def swap(x, bits):
        return lax.ppermute(x, "vir", [(i, i ^ bits) for i in range(n_vir)])

    mine, theirs = halves(int_mask, integrals)
    other = swap(theirs, 1)
    parts = cut(after(amp_mask, mine), amplitudes, groups, depth)
    (whole,) = kernel_call(join_kernel, [(depth, half)], [mine, after(other, *parts)], "join")
    blocks = line_blocks(whole, n_occ)

    rel = [[parts[0]] + [None] * (groups - 1), [None] * groups]
    for r in range(groups - 1, 0, -1):
        rel[0][r] = swap(parts[r], 2 * r)
    for r in range(groups - 1, -1, -1):
        rel[1][r] = swap(rel[0][r] if r else after(parts[0], rel[0][groups - 1]), 1)

    bits = []
    while (1 << len(bits)) < groups:
        bits.append(1 << len(bits))
    orders = [bits, bits[::-1]]
    away = [[r for r in range(groups) if r & o[0]] for o in orders]
    near = [[r for r in range(groups) if not r & o[0]] for o in orders]

    out = None
    token = None
    settled = []
    for n, (d, block, offset) in enumerate(blocks):
        if isinstance(block, tuple):
            middle, centre, far = block
            centre, far = lax.optimization_barrier((centre, far, *sent))[:2]
            block = jnp.where(middle, centre, far)
        if n > 0:
            block = after(block, *token)
        sent = products([[rel[h][r] for r in away[h]] for h in range(2)], block)
        moving = [swap(sent[h], 2 * orders[h][0]) for h in range(2)]
        held = list(products([[rel[h][r] for r in near[h]] for h in range(2)], after(block, *sent, *settled)))
        names = [near[0], near[1]]
        for level in range(1, len(bits)):
            for h in (1, 0):
                bit = orders[h][level]
                stays = [i for i, r in enumerate(names[h]) if not r & bit]
                goes = [i for i, r in enumerate(names[h]) if r & bit]
                held[h], moved = fold(rows, stays, goes, held[h], moving[h])
                moving[h] = swap(moved, 2 * bit)
                names[h] = [names[h][i] for i in stays]
        token = held if out is None else [*held, out]
        settled = moving if n == 0 else []
        (theirs,) = fold(rows, [0], [], held[1], moving[1])
        out = write(out, (rows, n_occ * width), d, half, offset, held[0], moving[0], swap(theirs, 1))
    return out


def solution(mesh):
    sizes = (mesh.shape["occ"], mesh.shape["vir"])

    def run(*args):
        return per_device(sizes, *args)

    in_specs = (P(("occ", "vir"), None), P(("occ", "vir"), None), P("vir", "occ"), P("vir", "occ"))
    out_specs = P(("occ", "vir"), None)
    return jax.shard_map(run, mesh=mesh, in_specs=in_specs, out_specs=out_specs, check_vma=False)
```

```python
import functools

import jax
import jax.numpy as jnp
from jax import lax
from jax.experimental import pallas as pl
from jax.experimental.pallas import tpu as pltpu
from jax.sharding import PartitionSpec as P

TILE_O = 32
TILE_V = 128
VMEM_LIMIT = 12 * 1024 * 1024


def after(value, *earlier):
    return lax.optimization_barrier((value,) + earlier)[0]


def in_vmem(count):
    return [pl.BlockSpec(memory_space=pltpu.VMEM)] * count


def in_hbm(count):
    return [pl.BlockSpec(memory_space=pltpu.HBM)] * count


def kernel_call(body, outs, operands, name, from_hbm=False, scratch=()):
    space = pltpu.HBM if from_hbm else pltpu.VMEM
    operands = [pltpu.with_memory_space_constraint(x, space) for x in operands]
    return pl.pallas_call(
        body,
        out_shape=[pltpu.VMEM(shape, jnp.float32) for shape in outs],
        in_specs=in_hbm(len(operands)) if from_hbm else in_vmem(len(operands)),
        out_specs=in_vmem(len(outs)),
        scratch_shapes=list(scratch),
        compiler_params=pltpu.CompilerParams(vmem_limit_bytes=VMEM_LIMIT),
        cost_estimate=pl.CostEstimate(flops=1, bytes_accessed=1, transcendentals=0),
        name=name,
    )(*operands)


def tiles(start, count):
    return pl.ds(pl.multiple_of(start * TILE_V, TILE_V), count * TILE_V)


def cut_kernel(groups, depth_tiles, mask_hbm, amp_hbm, *refs):
    out_refs, (mask_ref, amp_ref, mask_sem, amp_sems) = refs[:groups], refs[groups:]
    group = lax.axis_index("vir") // 2
    mask_copy = pltpu.make_async_copy(mask_hbm, mask_ref, mask_sem)
    mask_copy.start()
    starts = [(group ^ r) * depth_tiles for r in range(groups)]
    order = range(groups - 1, -1, -1)
    copies = {
        r: pltpu.make_async_copy(amp_hbm.at[:, tiles(starts[r], depth_tiles)], amp_ref.at[r], amp_sems.at[r]) for r in order
    }
    for r in order:
        copies[r].start()
    mask_copy.wait()
    for r in order:
        copies[r].wait()
        for t in range(depth_tiles):
            for o in range(amp_hbm.shape[0] // TILE_O):
                rows = pl.ds(o * TILE_O, TILE_O)
                scale = mask_ref[o, starts[r] + t].astype(jnp.float32)
                out_refs[r][rows, tiles(t, 1)] = amp_ref[r, rows, tiles(t, 1)] * scale


def cut(mask, amplitudes, groups, depth):
    rows = amplitudes.shape[0]
    scratch = [
        pltpu.SMEM(mask.shape, jnp.int32),
        pltpu.VMEM((groups, rows, depth), jnp.float32),
        pltpu.SemaphoreType.DMA,
        pltpu.SemaphoreType.DMA((groups,)),
    ]
    body = functools.partial(cut_kernel, groups, depth // TILE_V)
    return kernel_call(body, [(rows, depth)] * groups, [mask, amplitudes], "cut", True, scratch)


def halves_kernel(mask_hbm, int_hbm, mine_ref, theirs_ref, mask_ref, int_ref, mask_sem, int_sems):
    low = lax.axis_index("vir") % 2
    count = mine_ref.shape[1] // TILE_V
    mask_copy = pltpu.make_async_copy(mask_hbm, mask_ref, mask_sem)
    mask_copy.start()
    work = ((1 - low, theirs_ref), (low, mine_ref))
    copies = [
        pltpu.make_async_copy(int_hbm.at[:, tiles(half * count, count)], int_ref.at[i], int_sems.at[i])
        for i, (half, _) in enumerate(work)
    ]
    for copy in copies:
        copy.start()
    mask_copy.wait()
    for i, (half, out_ref) in enumerate(work):
        copies[i].wait()
        for t in range(count):
            for k in range(int_hbm.shape[0] // TILE_V):
                scale = mask_ref[k, half * count + t].astype(jnp.float32)
                out_ref[tiles(k, 1), tiles(t, 1)] = int_ref[i, tiles(k, 1), tiles(t, 1)] * scale


def halves(mask, integrals):
    depth, width = integrals.shape
    scratch = [
        pltpu.SMEM(mask.shape, jnp.int32),
        pltpu.VMEM((2, depth, width // 2), jnp.float32),
        pltpu.SemaphoreType.DMA,
        pltpu.SemaphoreType.DMA((2,)),
    ]
    return kernel_call(halves_kernel, [(depth, width // 2)] * 2, [mask, integrals], "halves", True, scratch)


def join_kernel(mine_ref, other_ref, out_ref):
    low = lax.axis_index("vir") % 2
    depth = mine_ref.shape[0]
    out_ref[pl.ds(pl.multiple_of(low * depth, depth), depth), :] = mine_ref[...]
    out_ref[pl.ds(pl.multiple_of((1 - low) * depth, depth), depth), :] = other_ref[...]


def fold_kernel(rows, stays, goes, held_ref, got_ref, *out_refs):
    for out_ref, places in zip(out_refs, (stays, goes)):
        for i, k in enumerate(places):
            take = pl.ds(k * rows, rows)
            out_ref[i * rows : (i + 1) * rows, :] = held_ref[take, :] + got_ref[take, :]


def fold(rows, stays, goes, held, got):
    outs = [(len(places) * rows, held.shape[1]) for places in (stays, goes) if places]
    return kernel_call(functools.partial(fold_kernel, rows, stays, goes), outs, [held, got], "fold")


def write_kernel(d, half, offset, held_ref, got_ref, other_ref, *refs):
    out_ref, piece_ref, sems = refs[-3:]
    low = lax.axis_index("vir") % 2
    place = lax.axis_index("occ") ^ d
    width = held_ref.shape[1] // TILE_V
    starts = [(2 * place + h) * (half // TILE_V) + offset // TILE_V for h in (low, 1 - low)]
    piece_ref[...] = held_ref[...] + got_ref[...]
    copies = [
        pltpu.make_async_copy(source, out_ref.at[:, tiles(start, width)], sems.at[i])
        for i, (source, start) in enumerate(zip((piece_ref, other_ref), starts))
    ]
    for copy in copies:
        copy.start()
    for copy in copies:
        copy.wait()


def write(out, shape, d, half, offset, held, got, other):
    given = [] if out is None else [out]
    return pl.pallas_call(
        functools.partial(write_kernel, d, half, offset),
        out_shape=jax.ShapeDtypeStruct(shape, jnp.float32),
        in_specs=in_vmem(3) + in_hbm(len(given)),
        out_specs=pl.BlockSpec(memory_space=pltpu.HBM),
        scratch_shapes=[pltpu.VMEM(held.shape, jnp.float32), pltpu.SemaphoreType.DMA((2,))],
        input_output_aliases={3: 0} if given else {},
        compiler_params=pltpu.CompilerParams(vmem_limit_bytes=VMEM_LIMIT),
        cost_estimate=pl.CostEstimate(flops=1, bytes_accessed=1, transcendentals=0),
        name="write",
    )(held, got, other, *given)


def split(x):
    high = x.astype(jnp.bfloat16)
    return high, (x - high.astype(jnp.float32)).astype(jnp.bfloat16)


def dot_kernel(count, *refs):
    left, block_ref, outs = refs[: 2 * count], refs[2 * count], refs[2 * count + 1 :]
    rows = left[0].shape[0]
    b_high, b_low = split(block_ref[...])
    for h in range(2):
        for i in range(count):
            a_high, a_low = split(left[h * count + i][...])
            total = None
            for a, b in ((a_high, b_low), (a_low, b_high), (a_high, b_high)):
                term = jnp.dot(a, b, preferred_element_type=jnp.float32)
                total = term if total is None else total + term
            outs[h][i * rows : (i + 1) * rows, :] = total


def products(left, block):
    count = len(left[0])
    shape = (count * left[0][0].shape[0], block.shape[1])
    return kernel_call(functools.partial(dot_kernel, count), [shape] * 2, [*left[0], *left[1], block], "products")


def line_blocks(own, nodes):
    here = lax.axis_index("occ")

    def direct(x, d):
        return lax.ppermute(x, "occ", [(i, i ^ d) for i in range(nodes)])

    if nodes != 4:
        return [(d, own if d == 0 else direct(own, d), 0) for d in range(nodes)]
    centre = lax.ppermute(own, "occ", [(1, 2), (2, 1)])
    near = direct(own, 1)
    far = lax.ppermute(after(own, centre, near), "occ", [(0, 3), (3, 0)])
    middle = (here == 1) | (here == 2)
    last = lax.ppermute(jnp.where(middle, centre, own), "occ", [(1, 0), (2, 3), (0, 2), (3, 1)])
    return [(0, own, 0), (1, near, 0), (3, (middle, centre, far), 0), (2, last, 0)]


def per_device(sizes, amplitudes, amp_mask, integrals, int_mask):
    n_occ, n_vir = sizes
    rows = amplitudes.shape[0]
    groups = n_vir // 2
    own_depth, width = integrals.shape
    depth, half = 2 * own_depth, width // 2

    def swap(x, bits):
        return lax.ppermute(x, "vir", [(i, i ^ bits) for i in range(n_vir)])

    mine, theirs = halves(int_mask, integrals)
    other = swap(theirs, 1)
    parts = cut(after(amp_mask, mine), amplitudes, groups, depth)
    (whole,) = kernel_call(join_kernel, [(depth, half)], [mine, after(other, *parts)], "join")
    blocks = line_blocks(whole, n_occ)

    rel = [[parts[0]] + [None] * (groups - 1), [None] * groups]
    for r in range(groups - 1, 0, -1):
        rel[0][r] = swap(parts[r], 2 * r)
    for r in range(groups - 1, -1, -1):
        rel[1][r] = swap(rel[0][r] if r else after(parts[0], rel[0][groups - 1]), 1)

    bits = []
    while (1 << len(bits)) < groups:
        bits.append(1 << len(bits))
    orders = [bits, bits[::-1]]
    away = [[r for r in range(groups) if r & o[0]] for o in orders]
    near = [[r for r in range(groups) if not r & o[0]] for o in orders]

    out = None
    token = None
    settled = []
    for n, (d, block, offset) in enumerate(blocks):
        if isinstance(block, tuple):
            middle, centre, far = block
            centre, far = lax.optimization_barrier((centre, far, *sent))[:2]
            block = jnp.where(middle, centre, far)
        if n > 0:
            block = after(block, *token)
        sent = products([[rel[h][r] for r in away[h]] for h in range(2)], block)
        moving = [swap(sent[h], 2 * orders[h][0]) for h in range(2)]
        held = list(products([[rel[h][r] for r in near[h]] for h in range(2)], after(block, *sent, *settled)))
        names = [near[0], near[1]]
        for level in range(1, len(bits)):
            for h in (1, 0):
                bit = orders[h][level]
                stays = [i for i, r in enumerate(names[h]) if not r & bit]
                goes = [i for i, r in enumerate(names[h]) if r & bit]
                held[h], moved = fold(rows, stays, goes, held[h], moving[h])
                across = n + 1 == n_occ and level + 1 == len(bits)
                moving[h] = swap(moved, 2 * bit + (h if across else 0))
                names[h] = [names[h][i] for i in stays]
        token = held if out is None else [*held, out]
        settled = moving if n == 0 else []
        if n + 1 == n_occ:
            (other,) = fold(rows, [0], [], swap(held[1], 1), moving[1])
        else:
            (theirs,) = fold(rows, [0], [], held[1], moving[1])
            other = swap(theirs, 1)
        out = write(out, (rows, n_occ * width), d, half, offset, held[0], moving[0], other)
    return out


def solution(mesh):
    sizes = (mesh.shape["occ"], mesh.shape["vir"])

    def run(*args):
        return per_device(sizes, *args)

    in_specs = (P(("occ", "vir"), None), P(("occ", "vir"), None), P("vir", "occ"), P("vir", "occ"))
    out_specs = P(("occ", "vir"), None)
    return jax.shard_map(run, mesh=mesh, in_specs=in_specs, out_specs=out_specs, check_vma=False)
```

```python
import functools

import jax
import jax.numpy as jnp
from jax import lax
from jax.experimental import pallas as pl
from jax.experimental.pallas import tpu as pltpu
from jax.sharding import PartitionSpec as P

TILE_O = 32
TILE_V = 128
VMEM_LIMIT = 12 * 1024 * 1024


def after(value, *earlier):
    return lax.optimization_barrier((value,) + earlier)[0]


def in_vmem(count):
    return [pl.BlockSpec(memory_space=pltpu.VMEM)] * count


def in_hbm(count):
    return [pl.BlockSpec(memory_space=pltpu.HBM)] * count


def kernel_call(body, outs, operands, name, from_hbm=False, scratch=()):
    space = pltpu.HBM if from_hbm else pltpu.VMEM
    operands = [pltpu.with_memory_space_constraint(x, space) for x in operands]
    return pl.pallas_call(
        body,
        out_shape=[pltpu.VMEM(shape, jnp.float32) for shape in outs],
        in_specs=in_hbm(len(operands)) if from_hbm else in_vmem(len(operands)),
        out_specs=in_vmem(len(outs)),
        scratch_shapes=list(scratch),
        compiler_params=pltpu.CompilerParams(vmem_limit_bytes=VMEM_LIMIT),
        cost_estimate=pl.CostEstimate(flops=1, bytes_accessed=1, transcendentals=0),
        name=name,
    )(*operands)


def tiles(start, count):
    return pl.ds(pl.multiple_of(start * TILE_V, TILE_V), count * TILE_V)


def cut_kernel(groups, depth_tiles, mask_hbm, amp_hbm, *refs):
    out_refs, (mask_ref, amp_ref, mask_sem, amp_sems) = refs[:groups], refs[groups:]
    group = lax.axis_index("vir") // 2
    mask_copy = pltpu.make_async_copy(mask_hbm, mask_ref, mask_sem)
    mask_copy.start()
    starts = [(group ^ r) * depth_tiles for r in range(groups)]
    order = range(groups - 1, -1, -1)
    copies = {
        r: pltpu.make_async_copy(amp_hbm.at[:, tiles(starts[r], depth_tiles)], amp_ref.at[r], amp_sems.at[r]) for r in order
    }
    for r in order:
        copies[r].start()
    mask_copy.wait()
    for r in order:
        copies[r].wait()
        for t in range(depth_tiles):
            for o in range(amp_hbm.shape[0] // TILE_O):
                rows = pl.ds(o * TILE_O, TILE_O)
                scale = mask_ref[o, starts[r] + t].astype(jnp.float32)
                out_refs[r][rows, tiles(t, 1)] = amp_ref[r, rows, tiles(t, 1)] * scale


def cut(mask, amplitudes, groups, depth):
    rows = amplitudes.shape[0]
    scratch = [
        pltpu.SMEM(mask.shape, jnp.int32),
        pltpu.VMEM((groups, rows, depth), jnp.float32),
        pltpu.SemaphoreType.DMA,
        pltpu.SemaphoreType.DMA((groups,)),
    ]
    body = functools.partial(cut_kernel, groups, depth // TILE_V)
    return kernel_call(body, [(rows, depth)] * groups, [mask, amplitudes], "cut", True, scratch)


def halves_kernel(mask_hbm, int_hbm, mine_ref, theirs_ref, mask_ref, int_ref, mask_sem, int_sems):
    low = lax.axis_index("vir") % 2
    count = mine_ref.shape[1] // TILE_V
    mask_copy = pltpu.make_async_copy(mask_hbm, mask_ref, mask_sem)
    mask_copy.start()
    work = ((1 - low, theirs_ref), (low, mine_ref))
    copies = [
        pltpu.make_async_copy(int_hbm.at[:, tiles(half * count, count)], int_ref.at[i], int_sems.at[i])
        for i, (half, _) in enumerate(work)
    ]
    for copy in copies:
        copy.start()
    mask_copy.wait()
    for i, (half, out_ref) in enumerate(work):
        copies[i].wait()
        for t in range(count):
            for k in range(int_hbm.shape[0] // TILE_V):
                scale = mask_ref[k, half * count + t].astype(jnp.float32)
                out_ref[tiles(k, 1), tiles(t, 1)] = int_ref[i, tiles(k, 1), tiles(t, 1)] * scale


def halves(mask, integrals):
    depth, width = integrals.shape
    scratch = [
        pltpu.SMEM(mask.shape, jnp.int32),
        pltpu.VMEM((2, depth, width // 2), jnp.float32),
        pltpu.SemaphoreType.DMA,
        pltpu.SemaphoreType.DMA((2,)),
    ]
    return kernel_call(halves_kernel, [(depth, width // 2)] * 2, [mask, integrals], "halves", True, scratch)


def join_kernel(mine_ref, other_ref, out_ref):
    low = lax.axis_index("vir") % 2
    depth = mine_ref.shape[0]
    out_ref[pl.ds(pl.multiple_of(low * depth, depth), depth), :] = mine_ref[...]
    out_ref[pl.ds(pl.multiple_of((1 - low) * depth, depth), depth), :] = other_ref[...]


def fold_kernel(rows, stays, goes, held_ref, got_ref, *out_refs):
    for out_ref, places in zip(out_refs, (stays, goes)):
        for i, k in enumerate(places):
            take = pl.ds(k * rows, rows)
            out_ref[i * rows : (i + 1) * rows, :] = held_ref[take, :] + got_ref[take, :]


def fold(rows, stays, goes, held, got):
    outs = [(len(places) * rows, held.shape[1]) for places in (stays, goes) if places]
    return kernel_call(functools.partial(fold_kernel, rows, stays, goes), outs, [held, got], "fold")


def write_kernel(d, half, offset, held_ref, got_ref, other_ref, *refs):
    out_ref, piece_ref, sems = refs[-3:]
    low = lax.axis_index("vir") % 2
    place = lax.axis_index("occ") ^ d
    width = held_ref.shape[1] // TILE_V
    starts = [(2 * place + h) * (half // TILE_V) + offset // TILE_V for h in (low, 1 - low)]
    piece_ref[...] = held_ref[...] + got_ref[...]
    copies = [
        pltpu.make_async_copy(source, out_ref.at[:, tiles(start, width)], sems.at[i])
        for i, (source, start) in enumerate(zip((piece_ref, other_ref), starts))
    ]
    for copy in copies:
        copy.start()
    for copy in copies:
        copy.wait()


def write(out, shape, d, half, offset, held, got, other):
    given = [] if out is None else [out]
    return pl.pallas_call(
        functools.partial(write_kernel, d, half, offset),
        out_shape=jax.ShapeDtypeStruct(shape, jnp.float32),
        in_specs=in_vmem(3) + in_hbm(len(given)),
        out_specs=pl.BlockSpec(memory_space=pltpu.HBM),
        scratch_shapes=[pltpu.VMEM(held.shape, jnp.float32), pltpu.SemaphoreType.DMA((2,))],
        input_output_aliases={3: 0} if given else {},
        compiler_params=pltpu.CompilerParams(vmem_limit_bytes=VMEM_LIMIT),
        cost_estimate=pl.CostEstimate(flops=1, bytes_accessed=1, transcendentals=0),
        name="write",
    )(held, got, other, *given)


def split(x):
    high = x.astype(jnp.bfloat16)
    return high, (x - high.astype(jnp.float32)).astype(jnp.bfloat16)


def dot_kernel(count, *refs):
    left, block_ref, outs = refs[: 2 * count], refs[2 * count], refs[2 * count + 1 :]
    rows = left[0].shape[0]
    b_high, b_low = split(block_ref[...])
    for h in range(2):
        for i in range(count):
            a_high, a_low = split(left[h * count + i][...])
            total = None
            for a, b in ((a_high, b_low), (a_low, b_high), (a_high, b_high)):
                term = jnp.dot(a, b, preferred_element_type=jnp.float32)
                total = term if total is None else total + term
            outs[h][i * rows : (i + 1) * rows, :] = total


def products(left, block):
    count = len(left[0])
    shape = (count * left[0][0].shape[0], block.shape[1])
    return kernel_call(functools.partial(dot_kernel, count), [shape] * 2, [*left[0], *left[1], block], "products")


def line_blocks(own, nodes):
    here = lax.axis_index("occ")

    def direct(x, d):
        return lax.ppermute(x, "occ", [(i, i ^ d) for i in range(nodes)])

    if nodes != 4:
        return [(d, own if d == 0 else direct(own, d), 0) for d in range(nodes)]
    centre = lax.ppermute(own, "occ", [(1, 2), (2, 1)])
    near = direct(own, 1)
    far = lax.ppermute(after(own, centre, near), "occ", [(0, 3), (3, 0)])
    middle = (here == 1) | (here == 2)
    last = lax.ppermute(jnp.where(middle, centre, own), "occ", [(1, 0), (2, 3), (0, 2), (3, 1)])
    return [(0, own, 0), (1, near, 0), (3, (middle, centre, far), 0), (2, last, 0)]


def per_device(sizes, amplitudes, amp_mask, integrals, int_mask):
    n_occ, n_vir = sizes
    rows = amplitudes.shape[0]
    groups = n_vir // 2
    own_depth, width = integrals.shape
    depth, half = 2 * own_depth, width // 2

    def swap(x, bits):
        return lax.ppermute(x, "vir", [(i, i ^ bits) for i in range(n_vir)])

    mine, theirs = halves(int_mask, integrals)
    other = swap(theirs, 1)
    parts = cut(after(amp_mask, mine), amplitudes, groups, depth)
    (whole,) = kernel_call(join_kernel, [(depth, half)], [mine, after(other, *parts)], "join")
    blocks = line_blocks(whole, n_occ)

    rel = [[parts[0]] + [None] * (groups - 1), [None] * groups]
    for r in range(groups - 1, 0, -1):
        rel[0][r] = swap(parts[r], 2 * r)
    for r in range(groups - 1, -1, -1):
        rel[1][r] = swap(rel[0][r] if r else after(parts[0], rel[0][groups - 1]), 1)

    bits = []
    while (1 << len(bits)) < groups:
        bits.append(1 << len(bits))
    orders = [bits, bits[::-1]]
    away = [[r for r in range(groups) if r & o[0]] for o in orders]
    near = [[r for r in range(groups) if not r & o[0]] for o in orders]

    out = None
    token = None
    settled = []
    late = []
    for n, (d, block, offset) in enumerate(blocks):
        if isinstance(block, tuple):
            middle, centre, far = block
            centre, far = lax.optimization_barrier((centre, far, *sent))[:2]
            block = jnp.where(middle, centre, far)
        if n > 0:
            block = after(block, *token)
        sent = products([[rel[h][r] for r in away[h]] for h in range(2)], block)
        moving = [swap(sent[h], 2 * orders[h][0]) for h in range(2)]
        held = list(products([[rel[h][r] for r in near[h]] for h in range(2)], after(block, *sent, *settled)))
        names = [near[0], near[1]]
        for level in range(1, len(bits)):
            for h in (1, 0):
                bit = orders[h][level]
                stays = [i for i, r in enumerate(names[h]) if not r & bit]
                goes = [i for i, r in enumerate(names[h]) if r & bit]
                held[h], moved = fold(rows, stays, goes, held[h], moving[h])
                across = n + 2 >= n_occ and level + 1 == len(bits)
                moving[h] = swap(moved, 2 * bit + (h if across else 0))
                names[h] = [names[h][i] for i in stays]
        token = held if out is None else [*held, out]
        settled = moving if n == 0 else []
        if n + 2 >= n_occ:
            late.append((d, held[0], moving, swap(held[1], 1), token))
            continue
        (theirs,) = fold(rows, [0], [], held[1], moving[1])
        out = write(out, (rows, n_occ * width), d, half, offset, held[0], moving[0], swap(theirs, 1))
    for i, (d, held_mine, moving, theirs, _) in enumerate(late):
        got = lax.optimization_barrier((*moving, theirs, *(late[1][4] if i == 0 else [])))[:3]
        (other,) = fold(rows, [0], [], got[2], got[1])
        out = write(out, (rows, n_occ * width), d, half, 0, held_mine, got[0], other)
    return out


def solution(mesh):
    sizes = (mesh.shape["occ"], mesh.shape["vir"])

    def run(*args):
        return per_device(sizes, *args)

    in_specs = (P(("occ", "vir"), None), P(("occ", "vir"), None), P("vir", "occ"), P("vir", "occ"))
    out_specs = P(("occ", "vir"), None)
    return jax.shard_map(run, mesh=mesh, in_specs=in_specs, out_specs=out_specs, check_vma=False)
```

```python
import functools

import jax
import jax.numpy as jnp
from jax import lax
from jax.experimental import pallas as pl
from jax.experimental.pallas import tpu as pltpu
from jax.sharding import PartitionSpec as P

TILE_O = 32
TILE_V = 128
VMEM_LIMIT = 12 * 1024 * 1024


def after(value, *earlier):
    return lax.optimization_barrier((value,) + earlier)[0]


def in_vmem(count):
    return [pl.BlockSpec(memory_space=pltpu.VMEM)] * count


def in_hbm(count):
    return [pl.BlockSpec(memory_space=pltpu.HBM)] * count


def kernel_call(body, outs, operands, name, from_hbm=False, scratch=()):
    space = pltpu.HBM if from_hbm else pltpu.VMEM
    operands = [pltpu.with_memory_space_constraint(x, space) for x in operands]
    return pl.pallas_call(
        body,
        out_shape=[pltpu.VMEM(shape, jnp.float32) for shape in outs],
        in_specs=in_hbm(len(operands)) if from_hbm else in_vmem(len(operands)),
        out_specs=in_vmem(len(outs)),
        scratch_shapes=list(scratch),
        compiler_params=pltpu.CompilerParams(vmem_limit_bytes=VMEM_LIMIT),
        cost_estimate=pl.CostEstimate(flops=1, bytes_accessed=1, transcendentals=0),
        name=name,
    )(*operands)


def tiles(start, count):
    return pl.ds(pl.multiple_of(start * TILE_V, TILE_V), count * TILE_V)


def cut_kernel(groups, depth_tiles, mask_hbm, amp_hbm, *refs):
    out_refs, (mask_ref, amp_ref, mask_sem, amp_sems) = refs[:groups], refs[groups:]
    group = lax.axis_index("vir") // 2
    mask_copy = pltpu.make_async_copy(mask_hbm, mask_ref, mask_sem)
    mask_copy.start()
    starts = [(group ^ r) * depth_tiles for r in range(groups)]
    order = range(groups - 1, -1, -1)
    copies = {
        r: pltpu.make_async_copy(amp_hbm.at[:, tiles(starts[r], depth_tiles)], amp_ref.at[r], amp_sems.at[r]) for r in order
    }
    for r in order:
        copies[r].start()
    mask_copy.wait()
    for r in order:
        copies[r].wait()
        for t in range(depth_tiles):
            for o in range(amp_hbm.shape[0] // TILE_O):
                rows = pl.ds(o * TILE_O, TILE_O)
                scale = mask_ref[o, starts[r] + t].astype(jnp.float32)
                out_refs[r][rows, tiles(t, 1)] = amp_ref[r, rows, tiles(t, 1)] * scale


def cut(mask, amplitudes, groups, depth):
    rows = amplitudes.shape[0]
    scratch = [
        pltpu.SMEM(mask.shape, jnp.int32),
        pltpu.VMEM((groups, rows, depth), jnp.float32),
        pltpu.SemaphoreType.DMA,
        pltpu.SemaphoreType.DMA((groups,)),
    ]
    body = functools.partial(cut_kernel, groups, depth // TILE_V)
    return kernel_call(body, [(rows, depth)] * groups, [mask, amplitudes], "cut", True, scratch)


def halves_kernel(mask_hbm, int_hbm, mine_ref, theirs_ref, mask_ref, int_ref, mask_sem, int_sems):
    low = lax.axis_index("vir") % 2
    count = mine_ref.shape[1] // TILE_V
    mask_copy = pltpu.make_async_copy(mask_hbm, mask_ref, mask_sem)
    mask_copy.start()
    work = ((1 - low, theirs_ref), (low, mine_ref))
    copies = [
        pltpu.make_async_copy(int_hbm.at[:, tiles(half * count, count)], int_ref.at[i], int_sems.at[i])
        for i, (half, _) in enumerate(work)
    ]
    for copy in copies:
        copy.start()
    mask_copy.wait()
    for i, (half, out_ref) in enumerate(work):
        copies[i].wait()
        for t in range(count):
            for k in range(int_hbm.shape[0] // TILE_V):
                scale = mask_ref[k, half * count + t].astype(jnp.float32)
                out_ref[tiles(k, 1), tiles(t, 1)] = int_ref[i, tiles(k, 1), tiles(t, 1)] * scale


def halves(mask, integrals):
    depth, width = integrals.shape
    scratch = [
        pltpu.SMEM(mask.shape, jnp.int32),
        pltpu.VMEM((2, depth, width // 2), jnp.float32),
        pltpu.SemaphoreType.DMA,
        pltpu.SemaphoreType.DMA((2,)),
    ]
    return kernel_call(halves_kernel, [(depth, width // 2)] * 2, [mask, integrals], "halves", True, scratch)


def join_kernel(mine_ref, other_ref, out_ref):
    low = lax.axis_index("vir") % 2
    depth = mine_ref.shape[0]
    out_ref[pl.ds(pl.multiple_of(low * depth, depth), depth), :] = mine_ref[...]
    out_ref[pl.ds(pl.multiple_of((1 - low) * depth, depth), depth), :] = other_ref[...]


def fold_kernel(rows, stays, goes, held_ref, got_ref, *out_refs):
    for out_ref, places in zip(out_refs, (stays, goes)):
        for i, k in enumerate(places):
            take = pl.ds(k * rows, rows)
            out_ref[i * rows : (i + 1) * rows, :] = held_ref[take, :] + got_ref[take, :]


def fold(rows, stays, goes, held, got):
    outs = [(len(places) * rows, held.shape[1]) for places in (stays, goes) if places]
    return kernel_call(functools.partial(fold_kernel, rows, stays, goes), outs, [held, got], "fold")


def write_kernel(d, half, offset, held_ref, got_ref, other_ref, *refs):
    out_ref, piece_ref, sems = refs[-3:]
    low = lax.axis_index("vir") % 2
    place = lax.axis_index("occ") ^ d
    width = held_ref.shape[1] // TILE_V
    starts = [(2 * place + h) * (half // TILE_V) + offset // TILE_V for h in (low, 1 - low)]
    piece_ref[...] = held_ref[...] + got_ref[...]
    copies = [
        pltpu.make_async_copy(source, out_ref.at[:, tiles(start, width)], sems.at[i])
        for i, (source, start) in enumerate(zip((piece_ref, other_ref), starts))
    ]
    for copy in copies:
        copy.start()
    for copy in copies:
        copy.wait()


def write(out, shape, d, half, offset, held, got, other):
    given = [] if out is None else [out]
    return pl.pallas_call(
        functools.partial(write_kernel, d, half, offset),
        out_shape=jax.ShapeDtypeStruct(shape, jnp.float32),
        in_specs=in_vmem(3) + in_hbm(len(given)),
        out_specs=pl.BlockSpec(memory_space=pltpu.HBM),
        scratch_shapes=[pltpu.VMEM(held.shape, jnp.float32), pltpu.SemaphoreType.DMA((2,))],
        input_output_aliases={3: 0} if given else {},
        compiler_params=pltpu.CompilerParams(vmem_limit_bytes=VMEM_LIMIT),
        cost_estimate=pl.CostEstimate(flops=1, bytes_accessed=1, transcendentals=0),
        name="write",
    )(held, got, other, *given)


def split(x):
    high = x.astype(jnp.bfloat16)
    return high, (x - high.astype(jnp.float32)).astype(jnp.bfloat16)


def dot_kernel(count, *refs):
    left, block_ref, outs = refs[: 2 * count], refs[2 * count], refs[2 * count + 1 :]
    rows = left[0].shape[0]
    b_high, b_low = split(block_ref[...])
    for h in range(2):
        for i in range(count):
            a_high, a_low = split(left[h * count + i][...])
            total = None
            for a, b in ((a_high, b_low), (a_low, b_high), (a_high, b_high)):
                term = jnp.dot(a, b, preferred_element_type=jnp.float32)
                total = term if total is None else total + term
            outs[h][i * rows : (i + 1) * rows, :] = total


def products(left, block):
    count = len(left[0])
    shape = (count * left[0][0].shape[0], block.shape[1])
    return kernel_call(functools.partial(dot_kernel, count), [shape] * 2, [*left[0], *left[1], block], "products")


def line_blocks(own, nodes):
    here = lax.axis_index("occ")

    def direct(x, d):
        return lax.ppermute(x, "occ", [(i, i ^ d) for i in range(nodes)])

    if nodes != 4:
        return [(d, own if d == 0 else direct(own, d), 0) for d in range(nodes)]
    centre = lax.ppermute(own, "occ", [(1, 2), (2, 1)])
    near = direct(own, 1)
    far = lax.ppermute(after(own, centre, near), "occ", [(0, 3), (3, 0)])
    middle = (here == 1) | (here == 2)
    last = lax.ppermute(jnp.where(middle, centre, own), "occ", [(1, 0), (2, 3), (0, 2), (3, 1)])
    return [(0, own, 0), (1, near, 0), (3, (middle, centre, far), 0), (2, last, 0)]


def per_device(sizes, amplitudes, amp_mask, integrals, int_mask):
    n_occ, n_vir = sizes
    rows = amplitudes.shape[0]
    groups = n_vir // 2
    own_depth, width = integrals.shape
    depth, half = 2 * own_depth, width // 2

    def swap(x, bits):
        return lax.ppermute(x, "vir", [(i, i ^ bits) for i in range(n_vir)])

    mine, theirs = halves(int_mask, integrals)
    other = swap(theirs, 1)
    parts = cut(after(amp_mask, mine), amplitudes, groups, depth)
    (whole,) = kernel_call(join_kernel, [(depth, half)], [mine, after(other, *parts)], "join")
    blocks = line_blocks(whole, n_occ)

    rel = [[parts[0]] + [None] * (groups - 1), [None] * groups]
    for r in range(groups - 1, 0, -1):
        rel[0][r] = swap(parts[r], 2 * r)
    for r in range(groups - 1, -1, -1):
        rel[1][r] = swap(rel[0][r] if r else after(parts[0], rel[0][groups - 1]), 1)

    bits = []
    while (1 << len(bits)) < groups:
        bits.append(1 << len(bits))
    orders = [bits, bits[::-1]]
    away = [[r for r in range(groups) if r & o[0]] for o in orders]
    near = [[r for r in range(groups) if not r & o[0]] for o in orders]

    out = None
    token = None
    settled = []
    late = []
    for n, (d, block, offset) in enumerate(blocks):
        if isinstance(block, tuple):
            middle, centre, far = block
            centre, far = lax.optimization_barrier((centre, far, *sent))[:2]
            block = jnp.where(middle, centre, far)
        if n > 0:
            block = after(block, *token)
        sent = products([[rel[h][r] for r in away[h]] for h in range(2)], block)
        moving = [swap(sent[h], 2 * orders[h][0]) for h in range(2)]
        held = list(products([[rel[h][r] for r in near[h]] for h in range(2)], after(block, *sent, *settled)))
        names = [near[0], near[1]]
        for level in range(1, len(bits)):
            for h in (1, 0):
                bit = orders[h][level]
                stays = [i for i, r in enumerate(names[h]) if not r & bit]
                goes = [i for i, r in enumerate(names[h]) if r & bit]
                held[h], moved = fold(rows, stays, goes, held[h], moving[h])
                across = n + 2 >= n_occ and level + 1 == len(bits)
                moving[h] = swap(moved, 2 * bit + (h if across else 0))
                names[h] = [names[h][i] for i in stays]
        token = [*held, out] if n == 1 else [*held]
        settled = moving if n == 0 else []
        if n + 2 >= n_occ:
            late.append((d, held[0], moving, swap(held[1], 1), token))
            continue
        (theirs,) = fold(rows, [0], [], held[1], moving[1])
        out = write(out, (rows, n_occ * width), d, half, offset, held[0], moving[0], swap(theirs, 1))
    for i, (d, held_mine, moving, theirs, _) in enumerate(late):
        got = lax.optimization_barrier((*moving, theirs, *(late[1][4] if i == 0 else [])))[:3]
        (other,) = fold(rows, [0], [], got[2], got[1])
        out = write(out, (rows, n_occ * width), d, half, 0, held_mine, got[0], other)
    return out


def solution(mesh):
    sizes = (mesh.shape["occ"], mesh.shape["vir"])

    def run(*args):
        return per_device(sizes, *args)

    in_specs = (P(("occ", "vir"), None), P(("occ", "vir"), None), P("vir", "occ"), P("vir", "occ"))
    out_specs = P(("occ", "vir"), None)
    return jax.shard_map(run, mesh=mesh, in_specs=in_specs, out_specs=out_specs, check_vma=False)
```
